32 devices in a mesh: seq: 4 (over z), dp: 2 (over core), mp: 4 (over y, x).
Axes of the slice: x: 2, y: 2, z: 4, core: 2. Of those that a mesh axis runs over, the one named last changes fastest.
Arguments:
- stream: float32 [2, 1088, 1024], P('dp', 'seq'), may hold values from -6 to 6
- text_len: int32 [2], P('dp'), may hold values from 1 to 64, as said below
- norm_gain: float32 [2, 4, 1024], replicated, may hold values from 0.1 to 1.9
- norm_shift: float32 [2, 4, 1024], replicated, may hold values from -3 to 3
- w_qkv: bfloat16 [2, 1024, 3, 1024], P(None, None, None, 'mp'), may hold values from -0.1875 to 0.1875
- bias_qv: float32 [2, 2, 1024], P(None, None, 'mp'), may hold values from -4 to 4
- w_out: bfloat16 [2, 1024, 1024], P(None, 'mp'), may hold values from -0.1875 to 0.1875
- bias_out: float32 [2, 1024], replicated, may hold values from -4 to 4
- w_up: bfloat16 [2, 1024, 4096], P(None, None, 'mp'), may hold values from -0.1875 to 0.1875
- bias_up: float32 [2, 4096], P(None, 'mp'), may hold values from -4 to 4
- w_down: bfloat16 [2, 4096, 1024], P(None, 'mp'), may hold values from -0.09375 to 0.09375
- bias_down: float32 [2, 1024], replicated, may hold values from -4 to 4
- cotangent: float32 [2, 1088, 1024], P('dp', 'seq'), may hold values from -6 to 6
Outputs:
- result: float32 [2, 1088, 1024], P('dp', 'seq')
- grad_stream: float32 [2, 1088, 1024], P('dp', 'seq')
- grad_norm_gain: float32 [2, 4, 1024], P(None, None, ('seq', 'dp'))
- grad_norm_shift: float32 [2, 4, 1024], P(None, None, ('seq', 'dp'))
- grad_w_qkv: float32 [2, 1024, 3, 1024], P(None, ('seq', 'dp'), None, 'mp')
- grad_bias_qv: float32 [2, 2, 1024], P(None, None, ('mp', 'seq', 'dp'))
- grad_w_out: float32 [2, 1024, 1024], P(None, 'mp', ('seq', 'dp'))
- grad_bias_out: float32 [2, 1024], P(None, ('seq', 'dp'))
- grad_w_up: float32 [2, 1024, 4096], P(None, ('seq', 'dp'), 'mp')
- grad_bias_up: float32 [2, 4096], P(None, ('mp', 'seq', 'dp'))
- grad_w_down: float32 [2, 4096, 1024], P(None, 'mp', ('seq', 'dp'))
- grad_bias_down: float32 [2, 1024], P(None, ('seq', 'dp'))
The draws below stay inside these ranges and needn't reach their ends.
Inputs may be any that keep to these rules, and one draw needn't show every extreme that they name: Text positions at and after text_len (below 64) are padding; one sequence of the batch has all 64 text positions valid, every other one fewer.
All inputs are finite; a program needn't handle non-finite values.
Results may differ from the reference program's by a relative error of at most 0.02.
Values may be sent and summed in bfloat16 or wider, within the bound.
A program may use at most 128 MiB of HBM per device.

```python
import math
import jax
import jax.numpy as jnp
from jax import lax

D = 1024
HEADS = 16
FF = 4096
LAYERS = 2
TEXT = 64
LEN = 1088
SEQS = 2


def draw_text_len(key, part):
    key = jax.random.fold_in(key, 7)
    pick_key, rest_key = jax.random.split(key)
    chosen = jax.random.randint(pick_key, (), 0, SEQS, dtype=jnp.int32)
    shorter = jax.random.randint(rest_key, (SEQS,), 1, TEXT, dtype=jnp.int32)
    places = jnp.arange(SEQS, dtype=jnp.int32)
    return jnp.where(places == chosen, jnp.int32(TEXT), shorter).astype(jnp.int32)


def block_scale(own_key, shape, pieces, low, high):
    factor_of = 1.0
    for position, shards_of in pieces:
        steps = jax.random.uniform(jax.random.fold_in(jax.random.fold_in(own_key, 6), position), (shards_of,), jnp.float32, low / len(pieces), high / len(pieces))
        factor_of = factor_of * jnp.repeat(jnp.exp(steps), shape[position] // shards_of).reshape((-1,) + (1,) * (len(shape) - 1 - position))
    return factor_of


def scatter_about(rng, shape, deviation, reach, cuts=(), kind=jnp.bfloat16):
    values = jax.random.normal(rng, shape, jnp.float32) * deviation
    if len(cuts) > 0:
        values = block_scale(rng, shape, cuts, -0.22, 0.18) * values
    return jnp.clip(values, min=-reach, max=reach).astype(kind)


def setup_inputs(seed: int = 0) -> dict:
    splits = jax.random.split(jax.random.key(seed), 14)
    return {
        "stream": scatter_about(splits[0], (SEQS, LEN, D), 1.0, 6.0, ((0, 2), (1, 4)), jnp.float32),
        "text_len": draw_text_len(jax.random.fold_in(splits[13], 71), 0),
        "norm_gain": jnp.clip(1.0 + 0.18 * jax.random.normal(splits[2], (LAYERS, 4, D), jnp.float32), 0.1, 1.9),
        "norm_shift": scatter_about(splits[3], (LAYERS, 4, D), 0.3, 3.0, (), jnp.float32),
        "w_qkv": scatter_about(splits[4], (LAYERS, D, 3, D), D ** -0.5, 0.1875, ((3, 4),)),
        "bias_qv": scatter_about(splits[5], (LAYERS, 2, D), 0.5, 4.0, ((2, 4),), jnp.float32),
        "w_out": scatter_about(splits[6], (LAYERS, D, D), D ** -0.5, 0.1875, ((1, 4),)),
        "bias_out": scatter_about(splits[7], (LAYERS, D), 0.5, 4.0, (), jnp.float32),
        "w_up": scatter_about(splits[8], (LAYERS, D, FF), D ** -0.5, 0.1875, ((2, 4),)),
        "bias_up": scatter_about(splits[9], (LAYERS, FF), 0.5, 4.0, ((1, 4),), jnp.float32),
        "w_down": scatter_about(splits[10], (LAYERS, FF, D), FF ** -0.5, 0.09375, ((1, 4),)),
        "bias_down": scatter_about(splits[11], (LAYERS, D), 0.5, 4.0, (), jnp.float32),
        "cotangent": scatter_about(splits[12], (SEQS, LEN, D), 1.0, 6.0, ((0, 2), (1, 4)), jnp.float32),
    }


relax_alpha = 32.0
norm_eps = 1e-05

@jax.custom_vjp
def low(v):
    return lax.optimization_barrier(v.astype(jnp.bfloat16)).astype(jnp.float32)

@jax.custom_vjp
def low_back(v):
    return v

def low_keep(v):
    return (low(v), None)

def low_pass(kept, grad):
    return (grad,)

def back_keep(v):
    return (v, None)

def back_low(kept, grad):
    return (low(grad),)
low.defvjp(low_keep, low_pass)
low_back.defvjp(back_keep, back_low)

def layer_norm(row_values, gain_row, shift_row):
    row_mean = lax.optimization_barrier(jnp.mean(row_values, axis=-1, keepdims=True))
    centred = row_values - row_mean
    variance = lax.optimization_barrier(jnp.mean(centred * centred, axis=-1, keepdims=True))
    return centred * lax.rsqrt(variance + norm_eps) * gain_row + shift_row

def matmul(left, right):
    return jnp.dot(left, right, precision=lax.Precision.HIGHEST)

def forward_sequence(seq_rows, length, params):
    norm_gain, norm_shift, w_qkv, bias_qv, w_out, bias_out, w_up, bias_up, w_down, bias_down = params
    head_dim = D // HEADS
    score_scale = 1.0 / math.sqrt(head_dim)
    positions = jnp.arange(LEN, dtype=jnp.int32)
    causal = positions[None, :] <= positions[:, None]
    visible = (positions >= TEXT) | (positions < length)
    allowed = causal & visible[None, :]
    current = seq_rows
    for layer_at in range(LAYERS):
        gain_rows = norm_gain[layer_at]
        shift_rows = norm_shift[layer_at]
        normed = low(layer_norm(current, gain_rows[0], shift_rows[0]))
        projected = jnp.einsum('td,dcf->tcf', normed, w_qkv[layer_at], precision=lax.Precision.HIGHEST)
        queries = low_back(low(projected[:, 0] + bias_qv[layer_at, 0]))
        key_rows = low_back(low(projected[:, 1]))
        value_rows = low_back(low(projected[:, 2] + bias_qv[layer_at, 1]))
        query_heads = queries.reshape(LEN, HEADS, head_dim)
        key_heads = key_rows.reshape(LEN, HEADS, head_dim)
        value_heads = value_rows.reshape(LEN, HEADS, head_dim)
        raw_scores = low_back(jnp.einsum('qhe,khe->hqk', query_heads, key_heads, precision=lax.Precision.HIGHEST) * score_scale)
        tempered = jnp.where(allowed[None], raw_scores / relax_alpha, -1e+30)
        highest = lax.optimization_barrier(jnp.max(tempered, axis=-1, keepdims=True))
        exponent = jnp.exp(relax_alpha * (tempered - highest))
        probabilities = low(exponent / lax.optimization_barrier(jnp.sum(exponent, axis=-1, keepdims=True)))
        attended = jnp.einsum('hqk,khe->qhe', probabilities, value_heads, precision=lax.Precision.HIGHEST)
        attended = low_back(low(attended.reshape(LEN, D)))
        branch = low_back(matmul(attended, w_out[layer_at]) + bias_out[layer_at])
        settled = current + layer_norm(branch, gain_rows[1], shift_rows[1])
        hidden_in = low(layer_norm(settled, gain_rows[2], shift_rows[2]))
        lifted = low_back(matmul(hidden_in, w_up[layer_at]) + bias_up[layer_at])
        activated = low(jax.nn.gelu(lifted, approximate=True))
        output_branch = low_back(matmul(activated, w_down[layer_at]) + bias_down[layer_at])
        current = settled + layer_norm(output_branch, gain_rows[3], shift_rows[3])
    return current

def reference(stream, text_len, norm_gain, norm_shift, w_qkv, bias_qv, w_out, bias_out, w_up, bias_up, w_down, bias_down, cotangent):
    params = tuple((item.astype(jnp.float32) for item in (norm_gain, norm_shift, w_qkv, bias_qv, w_out, bias_out, w_up, bias_up, w_down, bias_down)))

    def run_layers(stream_in, param_set):

        def one_sequence(seq_item):
            return jax.checkpoint(forward_sequence)(seq_item[0], seq_item[1], param_set)
        return lax.map(one_sequence, (stream_in, text_len))
    result, pull_back = jax.vjp(run_layers, stream.astype(jnp.float32), params)
    grad_stream, grad_params = pull_back(cotangent.astype(jnp.float32))
    return (result, grad_stream, grad_params[0], grad_params[1], grad_params[2], grad_params[3], grad_params[4], grad_params[5], grad_params[6], grad_params[7], grad_params[8], grad_params[9])
```

```python
from functools import partial
import math

import jax
import jax.numpy as jnp
from jax import lax
from jax.experimental import pallas as pl
from jax.experimental.pallas import tpu as pltpu
from jax.sharding import PartitionSpec as P

D = 1024
HEADS = 16
TEXT = 64


relax_alpha = 32.0
norm_eps = 1e-05


def layer_norm(row_values, gain_row, shift_row):
    row_mean = jnp.mean(row_values, axis=-1, keepdims=True)
    centred = row_values - row_mean
    variance = jnp.mean(centred * centred, axis=-1, keepdims=True)
    return centred * lax.rsqrt(variance + norm_eps) * gain_row + shift_row


def norm_back(row_values, gain_row, shift_row, grad_rows):
    result_value, pull_back = jax.vjp(layer_norm, row_values, gain_row, shift_row)
    return pull_back(grad_rows)


def reduce_rows(partial_sum):
    return lax.psum_scatter(
        partial_sum.astype(jnp.bfloat16), "mp", scatter_dimension=0, tiled=True
    ).astype(jnp.float32)


def widen_rows(row_values):
    return lax.all_gather(row_values, "mp", axis=0, tiled=True)


def reduce_grads(partial_sum):
    return lax.psum_scatter(
        partial_sum.astype(jnp.bfloat16), "mp", scatter_dimension=0, tiled=True
    ).astype(jnp.float32)


def widen_grads(row_values):
    return lax.all_gather(row_values, "mp", axis=0, tiled=True)


def relaxed_scores(query_heads, key_heads, allowed, score_scale):
    raw_scores = (
        jnp.einsum("sqhe,skhe->shqk", query_heads, key_heads, preferred_element_type=jnp.float32)
        * score_scale
    )
    return jnp.where(allowed, raw_scores / relax_alpha, -1e30)


def shards(
    stream,
    text_len,
    norm_gain,
    norm_shift,
    w_qkv,
    bias_qv,
    w_out,
    bias_out,
    w_up,
    bias_up,
    w_down,
    bias_down,
    cotangent,
):
    seq_count, block_len, model_width = stream.shape
    rows_all = seq_count * block_len
    layers = w_qkv.shape[0]
    local_cols = w_qkv.shape[3]
    head_dim = D // HEADS
    heads_here = local_cols // head_dim
    score_scale = 1.0 / math.sqrt(head_dim)
    share_rows = rows_all // lax.axis_size("mp")
    first_row = lax.axis_index("mp") * share_rows
    block_start = lax.axis_index("seq") * block_len
    seq_span = block_len * lax.axis_size("seq")
    query_pos = block_start + jnp.arange(block_len, dtype=jnp.int32)
    key_pos = jnp.arange(seq_span, dtype=jnp.int32)
    causal = key_pos[None, :] <= query_pos[:, None]
    visible = (key_pos[None, :] >= TEXT) | (key_pos[None, :] < text_len[:, None])
    allowed = causal[None, None] & visible[:, None, None, :]
    flat_rows = stream.reshape(rows_all, model_width)
    grad_rows = cotangent.reshape(rows_all, model_width)
    current = lax.dynamic_slice_in_dim(flat_rows, first_row, share_rows, 0)
    grad_rows = lax.dynamic_slice_in_dim(grad_rows, first_row, share_rows, 0)
    gelu_tanh = partial(jax.nn.gelu, approximate=True)
    kept_state = []
    for layer_at in range(layers):
        gain_rows = norm_gain[layer_at]
        shift_rows = norm_shift[layer_at]
        normed = widen_rows(layer_norm(current, gain_rows[0], shift_rows[0]).astype(jnp.bfloat16))
        projected = jnp.einsum(
            "td,dcf->tcf", normed, w_qkv[layer_at], preferred_element_type=jnp.float32
        )
        queries = (projected[:, 0] + bias_qv[layer_at, 0]).astype(jnp.bfloat16)
        key_rows = projected[:, 1].astype(jnp.bfloat16)
        value_rows = (projected[:, 2] + bias_qv[layer_at, 1]).astype(jnp.bfloat16)
        keys_all, values_all = (
            lax.all_gather(
                key_rows.reshape(seq_count, block_len, local_cols), "seq", axis=1, tiled=True
            ),
            lax.all_gather(
                value_rows.reshape(seq_count, block_len, local_cols), "seq", axis=1, tiled=True
            ),
        )
        query_heads = queries.reshape(seq_count, block_len, heads_here, head_dim)
        key_heads = keys_all.reshape(seq_count, seq_span, heads_here, head_dim)
        value_heads = values_all.reshape(seq_count, seq_span, heads_here, head_dim)
        tempered = relaxed_scores(query_heads, key_heads, allowed, score_scale)
        highest = jnp.max(tempered, axis=-1, keepdims=True)
        exponent = jnp.exp(relax_alpha * (tempered - highest))
        totals = jnp.sum(exponent, axis=-1, keepdims=True)
        log_total = relax_alpha * highest + jnp.log(totals)
        weights = (exponent / totals).astype(jnp.bfloat16)
        attended = jnp.einsum(
            "shqk,skhe->sqhe", weights, value_heads, preferred_element_type=jnp.float32
        )
        attended = attended.astype(jnp.bfloat16).reshape(rows_all, local_cols)
        branch = (
            reduce_rows(jnp.dot(attended, w_out[layer_at], preferred_element_type=jnp.float32))
            + bias_out[layer_at]
        )
        settled = current + layer_norm(branch, gain_rows[1], shift_rows[1])
        hidden_in = widen_rows(
            layer_norm(settled, gain_rows[2], shift_rows[2]).astype(jnp.bfloat16)
        )
        lifted = (
            jnp.dot(hidden_in, w_up[layer_at], preferred_element_type=jnp.float32)
            + bias_up[layer_at]
        )
        activated = gelu_tanh(lifted).astype(jnp.bfloat16)
        output_branch = (
            reduce_rows(jnp.dot(activated, w_down[layer_at], preferred_element_type=jnp.float32))
            + bias_down[layer_at]
        )
        kept_state.append(
            (
                current,
                normed,
                query_heads,
                key_heads,
                value_heads,
                log_total,
                attended,
                branch,
                settled,
                hidden_in,
                lifted,
                activated,
                output_branch,
            )
        )
        current = settled + layer_norm(output_branch, gain_rows[3], shift_rows[3])
    collected = []
    for layer_at in reversed(range(layers)):
        (
            layer_in,
            normed,
            query_heads,
            key_heads,
            value_heads,
            log_total,
            attended,
            branch,
            settled,
            hidden_in,
            lifted,
            activated,
            output_branch,
        ) = kept_state[layer_at]
        gain_rows = norm_gain[layer_at]
        shift_rows = norm_shift[layer_at]
        d_out_branch, gain_three, shift_three = norm_back(
            output_branch, gain_rows[3], shift_rows[3], grad_rows
        )
        d_out_branch = d_out_branch.astype(jnp.bfloat16)
        d_bias_down = jnp.sum(d_out_branch.astype(jnp.float32), axis=0)
        d_down_full = widen_grads(d_out_branch)
        d_w_down = jnp.einsum(
            "tf,td->fd", activated, d_down_full, preferred_element_type=jnp.float32
        )
        d_activated = jnp.einsum(
            "td,fd->tf", d_down_full, w_down[layer_at], preferred_element_type=jnp.float32
        )
        gelu_value, gelu_pull = jax.vjp(gelu_tanh, lifted)
        d_lifted = gelu_pull(d_activated)[0].astype(jnp.bfloat16)
        d_bias_up = jnp.sum(d_lifted.astype(jnp.float32), axis=0)
        d_w_up = jnp.einsum("td,tf->df", hidden_in, d_lifted, preferred_element_type=jnp.float32)
        d_hidden = reduce_grads(
            jnp.einsum("tf,df->td", d_lifted, w_up[layer_at], preferred_element_type=jnp.float32)
        )
        d_norm_two, gain_two, shift_two = norm_back(settled, gain_rows[2], shift_rows[2], d_hidden)
        d_settled = grad_rows + d_norm_two
        d_branch, gain_one, shift_one = norm_back(branch, gain_rows[1], shift_rows[1], d_settled)
        d_branch = d_branch.astype(jnp.bfloat16)
        d_bias_out = jnp.sum(d_branch.astype(jnp.float32), axis=0)
        d_branch_full = widen_grads(d_branch)
        d_w_out = jnp.einsum(
            "tf,td->fd", attended, d_branch_full, preferred_element_type=jnp.float32
        )
        d_attended = jnp.einsum(
            "td,fd->tf", d_branch_full, w_out[layer_at], preferred_element_type=jnp.float32
        )
        d_attended = d_attended.astype(jnp.bfloat16).reshape(
            seq_count, block_len, heads_here, head_dim
        )
        tempered = relaxed_scores(query_heads, key_heads, allowed, score_scale)
        probabilities = jnp.exp(relax_alpha * tempered - log_total)
        d_probs = jnp.einsum(
            "sqhe,skhe->shqk", d_attended, value_heads, preferred_element_type=jnp.float32
        )
        d_values = jnp.einsum(
            "shqk,sqhe->skhe",
            probabilities.astype(jnp.bfloat16),
            d_attended,
            preferred_element_type=jnp.float32,
        )
        mean_term = jnp.sum(probabilities * d_probs, axis=-1, keepdims=True)
        d_raw = (probabilities * (d_probs - mean_term)).astype(jnp.bfloat16)
        d_queries = (
            jnp.einsum("shqk,skhe->sqhe", d_raw, key_heads, preferred_element_type=jnp.float32)
            * score_scale
        )
        d_keys = (
            jnp.einsum("shqk,sqhe->skhe", d_raw, query_heads, preferred_element_type=jnp.float32)
            * score_scale
        )
        d_keys_own, d_values_own = (
            lax.psum_scatter(
                d_keys.reshape(seq_count, seq_span, local_cols).astype(jnp.bfloat16),
                "seq",
                scatter_dimension=1,
                tiled=True,
            ).astype(jnp.float32),
            lax.psum_scatter(
                d_values.reshape(seq_count, seq_span, local_cols).astype(jnp.bfloat16),
                "seq",
                scatter_dimension=1,
                tiled=True,
            ).astype(jnp.float32),
        )
        d_queries = d_queries.reshape(rows_all, local_cols).astype(jnp.bfloat16)
        d_keys_own = d_keys_own.reshape(rows_all, local_cols).astype(jnp.bfloat16)
        d_values_own = d_values_own.reshape(rows_all, local_cols).astype(jnp.bfloat16)
        d_bias_qv = jnp.stack(
            [
                jnp.sum(d_queries.astype(jnp.float32), axis=0),
                jnp.sum(d_values_own.astype(jnp.float32), axis=0),
            ]
        )
        d_projected = jnp.stack([d_queries, d_keys_own, d_values_own], axis=1)
        d_w_qkv = jnp.einsum("td,tcf->dcf", normed, d_projected, preferred_element_type=jnp.float32)
        d_normed = reduce_grads(
            jnp.einsum(
                "tcf,dcf->td", d_projected, w_qkv[layer_at], preferred_element_type=jnp.float32
            )
        )
        d_layer_in, gain_zero, shift_zero = norm_back(
            layer_in, gain_rows[0], shift_rows[0], d_normed
        )
        grad_rows = d_settled + d_layer_in
        collected.append(
            (
                jnp.stack([gain_zero, gain_one, gain_two, gain_three]),
                jnp.stack([shift_zero, shift_one, shift_two, shift_three]),
                d_w_qkv,
                d_bias_qv,
                d_w_out,
                d_bias_out,
                d_w_up,
                d_bias_up,
                d_w_down,
                d_bias_down,
            )
        )
    collected = collected[::-1]
    stacked = tuple((jnp.stack([entry[index_at] for entry in collected]) for index_at in range(10)))
    (
        gain_grads,
        shift_grads,
        grad_qkv,
        grad_qv,
        grad_out_w,
        grad_out_b,
        grad_up_w,
        grad_up_b,
        grad_down_w,
        grad_down_b,
    ) = stacked
    gain_grads, shift_grads, grad_out_b, grad_down_b = (
        lax.psum(gain_grads.astype(jnp.bfloat16), "mp").astype(jnp.float32),
        lax.psum(shift_grads.astype(jnp.bfloat16), "mp").astype(jnp.float32),
        lax.psum(grad_out_b.astype(jnp.bfloat16), "mp").astype(jnp.float32),
        lax.psum(grad_down_b.astype(jnp.bfloat16), "mp").astype(jnp.float32),
    )
    current, grad_rows = (
        lax.all_gather(current.astype(jnp.bfloat16), "mp", axis=0, tiled=True).astype(
            current.dtype
        ),
        lax.all_gather(grad_rows.astype(jnp.bfloat16), "mp", axis=0, tiled=True).astype(
            grad_rows.dtype
        ),
    )
    summed = (
        lax.psum_scatter(
            gain_grads.astype(jnp.bfloat16), ("seq", "dp"), scatter_dimension=2, tiled=True
        ).astype(jnp.float32),
        lax.psum_scatter(
            shift_grads.astype(jnp.bfloat16), ("seq", "dp"), scatter_dimension=2, tiled=True
        ).astype(jnp.float32),
        lax.psum_scatter(
            grad_qkv.astype(jnp.bfloat16), ("seq", "dp"), scatter_dimension=1, tiled=True
        ).astype(jnp.float32),
        lax.psum_scatter(
            grad_qv.astype(jnp.bfloat16), ("seq", "dp"), scatter_dimension=2, tiled=True
        ).astype(jnp.float32),
        lax.psum_scatter(
            grad_out_w.astype(jnp.bfloat16), ("seq", "dp"), scatter_dimension=2, tiled=True
        ).astype(jnp.float32),
        lax.psum_scatter(
            grad_out_b.astype(jnp.bfloat16), ("seq", "dp"), scatter_dimension=1, tiled=True
        ).astype(jnp.float32),
        lax.psum_scatter(
            grad_up_w.astype(jnp.bfloat16), ("seq", "dp"), scatter_dimension=1, tiled=True
        ).astype(jnp.float32),
        lax.psum_scatter(
            grad_up_b.astype(jnp.bfloat16), ("seq", "dp"), scatter_dimension=1, tiled=True
        ).astype(jnp.float32),
        lax.psum_scatter(
            grad_down_w.astype(jnp.bfloat16), ("seq", "dp"), scatter_dimension=2, tiled=True
        ).astype(jnp.float32),
        lax.psum_scatter(
            grad_down_b.astype(jnp.bfloat16), ("seq", "dp"), scatter_dimension=1, tiled=True
        ).astype(jnp.float32),
    )
    result = current.reshape(seq_count, block_len, model_width)
    grad_stream = grad_rows.reshape(seq_count, block_len, model_width)
    return (
        result,
        grad_stream,
        summed[0],
        summed[1],
        summed[2],
        summed[3],
        summed[4],
        summed[5],
        summed[6],
        summed[7],
        summed[8],
        summed[9],
    )


MESH = pl.DeviceIdType.MESH
BF = jnp.bfloat16
F32 = jnp.float32

SEQ_N, DP_N, MP_N = 4, 2, 4
ROWS = 272
SHARE = 64
TAIL = 16
OWN = SHARE + TAIL
HD = 64
COLS = 256
FFL = 1024
PACK = 32
BLK = SHARE + PACK
QKV_ROWS = MP_N * BLK + 2 * TAIL
VP_ROWS = MP_N * PACK + TAIL
SEG = {"d": (0, 1024), "u": (1024, 1024), "o": (2048, 256), "q": (2304, 768)}
SEG_AT = {"d": 0, "u": 1, "o": 2, "q": 3}
GROWS = 3072
SMALL = 16
SQRT_2_PI = math.sqrt(2.0 / math.pi)
SCORE_SCALE = 0.125


def dot(a, b, ca=1, cb=0):
    return lax.dot_general(a, b, (((ca,), (cb,)), ((), ())), preferred_element_type=F32)


def fits(mesh):
    return dict(mesh.shape) == {"seq": SEQ_N, "dp": DP_N, "mp": MP_N}


VMEM_SCRATCH = {
    "wq": ((2, 3, D, COLS), BF),
    "wo": ((2, COLS, D), BF),
    "wu": ((2, D, FFL), BF),
    "wd": ((2, FFL, D), BF),
    "cur": ((OWN, D), F32),
    "grd": ((OWN, D), F32),
    "stl": ((OWN, D), F32),
    "own": ((OWN, D), F32),
    "xh": ((2, 4, OWN, D), F32),
    "rstd": ((2, 4, OWN, 128), F32),
    "nrm": ((2, ROWS, D), BF),
    "hin": ((2, ROWS, D), BF),
    "act": ((2, ROWS, FFL), BF),
    "gpr": ((2, ROWS, FFL), F32),
    "dob": ((ROWS, D), BF),
    "dbr": ((ROWS, D), BF),
    "dlf": ((ROWS, FFL), BF),
    "att": ((2, ROWS, COLS), BF),
    "dpr": ((ROWS, 3 * COLS), BF),
    "qkvA": ((2, SEQ_N, QKV_ROWS, 128), BF),
    "q_s": ((2, SEQ_N * ROWS, HD), BF),
    "k_s": ((2, SEQ_N * ROWS, HD), BF),
    "v_s": ((2, SEQ_N * ROWS, HD), BF),
    "do_s": ((SEQ_N * ROWS, HD), BF),
    "dk_s": ((SEQ_N * ROWS, HD), F32),
    "dv_s": ((SEQ_N * ROWS, HD), F32),
    "pt0": ((2, ROWS, ROWS), BF),
    "pt1": ((2, 2 * ROWS, ROWS), BF),
    "pt2": ((2, 3 * ROWS, ROWS), BF),
    "pt3": ((2, 4 * ROWS, ROWS), BF),
    "oA": ((2, SEQ_N, VP_ROWS, 128), BF),
    "dA": ((2, SEQ_N, VP_ROWS, 128), BF),
    "eA": ((2, SEQ_N, QKV_ROWS, 128), BF),
    "qs": ((SEQ_N, QKV_ROWS, 128), BF),
    "os_": ((SEQ_N, VP_ROWS, 128), BF),
    "ds_": ((SEQ_N, VP_ROWS, 128), BF),
    "es": ((SEQ_N, QKV_ROWS, 128), BF),
    "rsS": ((ROWS, D), BF),
    "rsR": ((3, SHARE, D), BF),
    "rtR": ((2, 3, TAIL, D), BF),
    "gb": ((2, 2, 2, GROWS, 128), BF),
    "rA": ((2, 2, GROWS, 128), BF),
    "rB": ((2, GROWS, 128), BF),
    "rC": ((GROWS, 128), BF),
    "oq": ((3, 128, COLS), F32),
    "ou": ((128, FFL), F32),
    "od": ((FFL, 128), F32),
    "oo": ((COLS, 128), F32),
    "sg": ((2, SMALL, D), F32),
    "smR": ((7, 2, SMALL, 128), F32),
    "smS": ((2, SMALL, 128), F32),
    "smM": ((3, 2, SMALL, 128), F32),
    "resb": ((OWN, D), BF),
    "gstb": ((OWN, D), BF),
}
DMA_SEMS = {
    "ld": (16,),
    "ag_s": (3,), "ag_r": (3,),
    "rs_s": (3,), "rs_r": (3,),
    "rt_s": (2, 3), "rt_r": (2, 3),
    "qk_s": (3, 5), "qk_r": (3, 5),
    "do_ss": (3, 5), "do_r": (3, 5),
    "o_s": (3,), "o_r": (3,),
    "e_s": (3,), "e_r": (3,),
    "g_s": (3, 4), "g_r": (3, 4),
    "out": (4,),
    "fr_s": (2, 3), "fr_r": (2, 3), "fr_t": (2, 3), "fr_u": (2, 3),
    "fl": (2, 2),
    "sm_s": (7,), "sm_r": (7,), "sn_s": (3,), "sn_r": (3,),
}
IN_NAMES = ("tl", "stream", "cot", "gain", "shift", "bqv", "bo", "bu", "bd", "wq_h", "wo_h", "wu_h", "wd_h")
OUT_NAMES = ("res_o", "gst_o", "oq_o", "oo_o", "ou_o", "od_o", "sm_o")


class Refs:
    pass


def fused_kernel(*all_refs):
    n = Refs()
    names = IN_NAMES + OUT_NAMES + tuple(VMEM_SCRATCH) + tuple(DMA_SEMS)
    for name, ref in zip(names, all_refs):
        setattr(n, name, ref)
    pts = (n.pt0, n.pt1, n.pt2, n.pt3)

    s = lax.axis_index("seq")
    c = lax.axis_index("dp")
    m = lax.axis_index("mp")
    mx, my = lax.rem(m, 2), lax.div(m, 2)
    peers = (my * 2 + (1 - mx), (1 - my) * 2 + mx, (1 - my) * 2 + (1 - mx))
    z0, z1 = lax.rem(s, 2), lax.div(s, 2)
    zs = (z1 * 2 + (1 - z0), (1 - z1) * 2 + z0, (1 - z1) * 2 + (1 - z0))

    def mp_dev(r):
        return (s, c, peers[r])

    def z_dev(k):
        return (zs[k], c, m)

    core_dev = (s, 1 - c, m)
    group = [core_dev] + [z_dev(k) for k in range(3)] + [(zs[k], 1 - c, m) for k in range(3)]

    barrier = pltpu.get_barrier_semaphore()
    everyone = group + [mp_dev(r) for r in range(3)]
    for dev in everyone:
        pl.semaphore_signal(barrier, inc=1, device_id=dev, device_id_type=MESH)

    loads = [
        pltpu.make_async_copy(n.stream.at[pl.ds(pl.multiple_of(m * SHARE, SHARE), SHARE)], n.cur.at[pl.ds(0, SHARE)], n.ld.at[0]),
        pltpu.make_async_copy(n.stream.at[pl.ds(MP_N * SHARE, TAIL)], n.cur.at[pl.ds(SHARE, TAIL)], n.ld.at[1]),
        pltpu.make_async_copy(n.wq_h, n.wq, n.ld.at[2]),
        pltpu.make_async_copy(n.wo_h, n.wo, n.ld.at[3]),
        pltpu.make_async_copy(n.wu_h, n.wu, n.ld.at[4]),
        pltpu.make_async_copy(n.wd_h, n.wd, n.ld.at[5]),
        pltpu.make_async_copy(n.cot.at[pl.ds(pl.multiple_of(m * SHARE, SHARE), SHARE)], n.grd.at[pl.ds(0, SHARE)], n.ld.at[6]),
        pltpu.make_async_copy(n.cot.at[pl.ds(MP_N * SHARE, TAIL)], n.grd.at[pl.ds(SHARE, TAIL)], n.ld.at[7]),
    ]
    for cp in loads:
        cp.start()
    pl.semaphore_wait(barrier, len(everyone))
    loads[0].wait()
    loads[1].wait()

    def rcopy(src, dst, ss, rs, dev):
        return pltpu.make_async_remote_copy(
            src_ref=src, dst_ref=dst, send_sem=ss, recv_sem=rs, device_id=dev, device_id_type=MESH
        )

    def share(j):
        return pl.ds(pl.multiple_of(j * SHARE, SHARE), SHARE)

    tail = pl.ds(MP_N * SHARE, TAIL)

    def ln(v, l, j):
        ce = v - jnp.mean(v, axis=-1, keepdims=True)
        r = lax.rsqrt(jnp.mean(ce * ce, axis=-1, keepdims=True) + norm_eps)
        h = ce * r
        n.xh[l, j] = h
        n.rstd[l, j] = jnp.broadcast_to(r, (OWN, 128))
        return h * n.gain[l, pl.ds(j, 1), :] + n.shift[l, pl.ds(j, 1), :]

    def ln_back(l, j, dy):
        h = n.xh[l, j]
        r = n.rstd[l, j][:, :1]
        t = dy * n.gain[l, pl.ds(j, 1), :]
        m1 = jnp.mean(t, axis=-1, keepdims=True)
        m2 = jnp.mean(t * h, axis=-1, keepdims=True)
        return r * (t - m1 - h * m2)

    row_ids = lax.broadcasted_iota(jnp.int32, (OWN, 1), 0)
    counted = jnp.where((row_ids < SHARE) | (m == 0), 1.0, 0.0).astype(F32)

    def ln_params(l, j, dy):
        dw = dy * counted
        n.sg[l, pl.ds(j, 1), :] = jnp.sum(dw * n.xh[l, j], axis=0, keepdims=True)
        n.sg[l, pl.ds(4 + j, 1), :] = jnp.sum(dw, axis=0, keepdims=True)

    def gather_rows(buf, own_rows):
        buf[share(m), :] = own_rows[:SHARE]
        buf[tail, :] = own_rows[SHARE:]
        copies = []
        for r in range(3):
            cp = rcopy(buf.at[share(m)], buf.at[share(m)], n.ag_s.at[r], n.ag_r.at[r], mp_dev(r))
            cp.start()
            copies.append(cp)
        return copies

    def scatter_copy(r):
        return rcopy(n.rsS.at[share(peers[r])], n.rsR.at[r], n.rs_s.at[r], n.rs_r.at[r], mp_dev(r))

    def tail_copy(turn, r):
        return rcopy(n.rsS.at[tail], n.rtR.at[turn, r], n.rt_s.at[turn, r], n.rt_r.at[turn, r], mp_dev(r))

    def send_part(r, part):
        n.rsS[share(peers[r]), :] = part.astype(BF)
        scatter_copy(r).start()

    def send_tail(turn, part):
        n.rsS[tail, :] = part.astype(BF)
        for r in range(3):
            tail_copy(turn, r).start()

    def keep_own(part):
        n.own[...] = part

    def reduced(turn):
        for r in range(3):
            tail_copy(turn, r).wait_recv()
        for r in range(3):
            scatter_copy(r).wait_recv()
        total = n.own[:SHARE, :]
        rest = n.own[SHARE:, :].astype(BF).astype(F32)
        for r in range(3):
            total = total + n.rsR[r].astype(F32)
            rest = rest + n.rtR[turn, r].astype(F32)
        for r in range(3):
            scatter_copy(r).wait_send()
            tail_copy(turn, r).wait_send()
        return jnp.concatenate([total, rest], axis=0)

    def pack_rows(v):
        return jnp.concatenate([v[:PACK], v[PACK:]], axis=1)

    def pad_lanes(v):
        return jnp.concatenate([v, jnp.zeros_like(v)], axis=1)

    def chunk_rows(j, size):
        return pl.ds(pl.multiple_of(j * size, size), size)

    def chunk_send(stage, dest, l, j, pos, size, ss, rs):
        dest[l, s, chunk_rows(j, size), :] = stage[s, chunk_rows(j, size), :]
        for k in range(3):
            rcopy(
                stage.at[zs[k], chunk_rows(j, size)], dest.at[l, s, chunk_rows(j, size)],
                ss.at[k, pos], rs.at[k, pos], z_dev(k),
            ).start()

    def tail_send(stage, dest, l, start, size, ss, rs):
        dest[l, s, pl.ds(start, size), :] = stage[s, pl.ds(start, size), :]
        for k in range(3):
            rcopy(
                stage.at[zs[k], pl.ds(start, size)], dest.at[l, s, pl.ds(start, size)],
                ss.at[k, 4], rs.at[k, 4], z_dev(k),
            ).start()

    def chunk_wait(stage, dest, l, size, start, tail_size, ss, rs):
        order = (m,) + peers
        for k in range(3):
            for pos in range(4):
                cp = rcopy(
                    stage.at[zs[k], chunk_rows(order[pos], size)], dest.at[l, s, chunk_rows(order[pos], size)],
                    ss.at[k, pos], rs.at[k, pos], z_dev(k),
                )
                cp.wait()
            rcopy(
                stage.at[zs[k], pl.ds(start, tail_size)], dest.at[l, s, pl.ds(start, tail_size)],
                ss.at[k, 4], rs.at[k, 4], z_dev(k),
            ).wait()

    def whole_copies(stage, dest, l, ss, rs):
        return [rcopy(stage.at[zs[k]], dest.at[l, s], ss.at[k], rs.at[k], z_dev(k)) for k in range(3)]

    def seg_rows(seg):
        return pl.ds(SEG[seg][0], SEG[seg][1])

    def g_copy(phase, seg):
        at, rows = SEG_AT[seg], seg_rows(seg)
        if phase == 0:
            src, dst, dev = n.gb.at[1 - c, :, :, rows], n.rA.at[:, :, rows], core_dev
        elif phase == 1:
            src, dst, dev = n.gb.at[c, 1 - z0, :, rows], n.rB.at[:, rows], z_dev(0)
        else:
            src, dst, dev = n.gb.at[c, z0, 1 - z1, rows], n.rC.at[rows], z_dev(1)
        return rcopy(src, dst, n.g_s.at[phase, at], n.g_r.at[phase, at], dev)

    def g_first(seg):
        g_copy(0, seg).start()

    def g_second(seg):
        g_copy(0, seg).wait()
        rows = seg_rows(seg)
        for a in range(2):
            for b in range(2):
                n.gb[c, a, b, rows, :] = (n.gb[c, a, b, rows, :].astype(F32) + n.rA[a, b, rows, :].astype(F32)).astype(BF)
        g_copy(1, seg).start()

    def g_third(seg):
        g_copy(1, seg).wait()
        rows = seg_rows(seg)
        for b in range(2):
            n.gb[c, z0, b, rows, :] = (n.gb[c, z0, b, rows, :].astype(F32) + n.rB[b, rows, :].astype(F32)).astype(BF)
        g_copy(2, seg).start()

    def g_out(l, seg):
        src, dst = {"d": (n.od, n.od_o), "u": (n.ou, n.ou_o), "o": (n.oo, n.oo_o), "q": (n.oq, n.oq_o)}[seg]
        return pltpu.make_async_copy(src, dst.at[l], n.out.at[SEG_AT[seg]])

    def g_last(l, seg, again):
        g_copy(2, seg).wait()
        if again:
            g_out(1, seg).wait()
        start, count = SEG[seg]
        if seg in ("d", "o"):
            rows = seg_rows(seg)
            value = n.gb[c, z0, z1, rows, :].astype(F32) + n.rC[rows, :].astype(F32)
            if seg == "d":
                n.od[...] = value
            else:
                n.oo[...] = value
        else:
            for t in range(count // 128):
                rows = pl.ds(start + 128 * t, 128)
                value = n.gb[c, z0, z1, rows, :].astype(F32) + n.rC[rows, :].astype(F32)
                if seg == "u":
                    n.ou[:, pl.ds(128 * t, 128)] = value
                else:
                    n.oq[t // 2, :, pl.ds(128 * (t % 2), 128)] = value
        g_out(l, seg).start()

    text_count = n.tl[0]

    def gelu_pair(u):
        uu = u * u
        t = jnp.tanh(SQRT_2_PI * (u + 0.044715 * u * uu))
        half = 0.5 * (1.0 + t)
        slope = half + 0.5 * u * (1.0 - t * t) * (SQRT_2_PI * (1.0 + 3 * 0.044715 * uu))
        return u * half, slope

    order_rows = lambda own_value, pos, buf: own_value if pos == 0 else buf[share(peers[pos - 1]), :]

    def forward(l, first):
        own_rows = ln(n.cur[...], l, 0).astype(BF)
        copies = gather_rows(n.nrm.at[l], own_rows)
        if first:
            loads[2].wait()
        for pos in range(4):
            if pos > 0:
                copies[pos - 1].wait_recv()
            rows = order_rows(own_rows, pos, n.nrm.at[l])
            q = dot(rows, n.wq[l, 0]) + n.bqv[l, pl.ds(0, 1), :]
            k = dot(rows, n.wq[l, 1])
            v = dot(rows, n.wq[l, 2]) + n.bqv[l, pl.ds(1, 1), :]
            j = m if pos == 0 else peers[pos - 1]
            at = pl.multiple_of(j * BLK, BLK)
            for h in range(SEQ_N):
                cut = slice(HD * h, HD * h + HD)
                n.qs[h, pl.ds(at, SHARE), :] = jnp.concatenate([q[:SHARE, cut], k[:SHARE, cut]], axis=1).astype(BF)
                n.qs[h, pl.ds(at + SHARE, PACK), :] = pack_rows(v[:SHARE, cut]).astype(BF)
                if pos == 0:
                    n.qs[h, pl.ds(MP_N * BLK, TAIL), :] = jnp.concatenate([q[SHARE:, cut], k[SHARE:, cut]], axis=1).astype(BF)
                    n.qs[h, pl.ds(MP_N * BLK + TAIL, TAIL), :] = pad_lanes(v[SHARE:, cut]).astype(BF)
            chunk_send(n.qs, n.qkvA, l, j, pos, BLK, n.qk_s, n.qk_r)
            if pos == 0:
                tail_send(n.qs, n.qkvA, l, MP_N * BLK, 2 * TAIL, n.qk_s, n.qk_r)
        for cp in copies:
            cp.wait_send()
        chunk_wait(n.qs, n.qkvA, l, BLK, MP_N * BLK, 2 * TAIL, n.qk_s, n.qk_r)
        for zb in range(SEQ_N):
            for j in range(MP_N):
                both = n.qkvA[l, zb, pl.ds(BLK * j, SHARE), :]
                vals = n.qkvA[l, zb, pl.ds(BLK * j + SHARE, PACK), :]
                at = ROWS * zb + SHARE * j
                n.q_s[l, pl.ds(at, SHARE), :] = both[:, :HD]
                n.k_s[l, pl.ds(at, SHARE), :] = both[:, HD:]
                n.v_s[l, pl.ds(at, PACK), :] = vals[:, :HD]
                n.v_s[l, pl.ds(at + PACK, PACK), :] = vals[:, HD:]
            both = n.qkvA[l, zb, pl.ds(BLK * MP_N, TAIL), :]
            vals = n.qkvA[l, zb, pl.ds(BLK * MP_N + TAIL, TAIL), :]
            at = ROWS * zb + SHARE * MP_N
            n.q_s[l, pl.ds(at, TAIL), :] = both[:, :HD]
            n.k_s[l, pl.ds(at, TAIL), :] = both[:, HD:]
            n.v_s[l, pl.ds(at, TAIL), :] = vals[:, :HD]
        for i in range(SEQ_N):
            width = ROWS * (i + 1)
            st = dot(n.k_s[l, pl.ds(0, width), :], n.q_s[l, pl.ds(ROWS * i, ROWS), :], 1, 1) * SCORE_SCALE
            key_at = lax.broadcasted_iota(jnp.int32, (ROWS, ROWS), 0)
            query_at = lax.broadcasted_iota(jnp.int32, (ROWS, ROWS), 1)
            causal = key_at <= query_at
            if i == 0:
                st = jnp.where(causal & ((key_at >= TEXT) | (key_at < text_count)), st, -1e30)
            else:
                text_at = lax.broadcasted_iota(jnp.int32, (TEXT, ROWS), 0)
                st = jnp.concatenate([
                    jnp.where(text_at < text_count, st[:TEXT], -1e30),
                    st[TEXT:ROWS * i],
                    jnp.where(causal, st[ROWS * i:], -1e30),
                ], axis=0)
            e = jnp.exp(st - jnp.max(st, axis=0, keepdims=True))
            p = (e * (1.0 / jnp.sum(e, axis=0, keepdims=True))).astype(BF)
            pts[i][l] = p
            o = dot(n.v_s[l, pl.ds(0, width), :], p, 0, 0).T
            for j in range(MP_N):
                n.os_[i, pl.ds(PACK * j, PACK), :] = pack_rows(o[SHARE * j:SHARE * j + SHARE]).astype(BF)
            n.os_[i, pl.ds(PACK * MP_N, TAIL), :] = pad_lanes(o[SHARE * MP_N:]).astype(BF)
        copies = whole_copies(n.os_, n.oA, l, n.o_s, n.o_r)
        for cp in copies:
            cp.start()
        n.oA[l, s] = n.os_[s]
        if first:
            loads[3].wait()
        for cp in copies:
            cp.wait()
        for j in range(MP_N):
            got = [n.oA[l, h, pl.ds(PACK * j, PACK), :] for h in range(SEQ_N)]
            n.att[l, pl.ds(SHARE * j, PACK), :] = jnp.concatenate([g[:, :HD] for g in got], axis=1)
            n.att[l, pl.ds(SHARE * j + PACK, PACK), :] = jnp.concatenate([g[:, HD:] for g in got], axis=1)
        got = [n.oA[l, h, pl.ds(PACK * MP_N, TAIL), :] for h in range(SEQ_N)]
        n.att[l, tail, :] = jnp.concatenate([g[:, :HD] for g in got], axis=1)
        for r in (2, 0, 1):
            send_part(r, dot(n.att[l, share(peers[r]), :], n.wo[l]))
        part = dot(jnp.concatenate([n.att[l, share(m), :], n.att[l, tail, :]], axis=0), n.wo[l])
        send_tail(0, part[SHARE:])
        keep_own(part)
        branch = reduced(0) + n.bo[l]
        settled = n.cur[...] + ln(branch, l, 1)
        n.stl[...] = settled
        own_rows = ln(settled, l, 2).astype(BF)
        copies = gather_rows(n.hin.at[l], own_rows)
        if first:
            loads[4].wait()
            loads[5].wait()
        for pos in range(4):
            if pos > 0:
                copies[pos - 1].wait_recv()
            rows = order_rows(own_rows, pos, n.hin.at[l])
            value, slope = gelu_pair(dot(rows, n.wu[l]) + n.bu[l])
            value = value.astype(BF)
            j = m if pos == 0 else peers[pos - 1]
            n.act[l, share(j), :] = value[:SHARE]
            n.gpr[l, share(j), :] = slope[:SHARE]
            part = dot(value, n.wd[l])
            if pos == 0:
                n.act[l, tail, :] = value[SHARE:]
                n.gpr[l, tail, :] = slope[SHARE:]
                send_tail(1, part[SHARE:])
                keep_own(part)
            else:
                send_part(pos - 1, part)
        for cp in copies:
            cp.wait_send()
        out_branch = reduced(1) + n.bd[l]
        n.cur[...] = n.stl[...] + ln(out_branch, l, 3)

    def final_rows(which, stage, out, value):
        stage[...] = value.astype(BF)
        copies = []
        for r in range(3):
            copies.append(rcopy(stage.at[pl.ds(0, SHARE)], out.at[share(m)], n.fr_s.at[which, r], n.fr_r.at[which, r], mp_dev(r)))
        copies.append(pltpu.make_async_copy(stage.at[pl.ds(0, SHARE)], out.at[share(m)], n.fl.at[which, 0]))
        copies.append(pltpu.make_async_copy(stage.at[pl.ds(SHARE, TAIL)], out.at[tail], n.fl.at[which, 1]))
        for cp in copies:
            cp.start()
        return copies

    def backward(l, again):
        grad_rows = n.grd[...]
        d_ob = ln_back(l, 3, grad_rows).astype(BF)
        copies = gather_rows(n.dob, d_ob)
        ln_params(l, 3, grad_rows)
        n.sg[l, pl.ds(9, 1), :] = jnp.sum(d_ob.astype(F32) * counted, axis=0, keepdims=True)
        for pos in range(4):
            if pos > 0:
                copies[pos - 1].wait_recv()
            rows = order_rows(d_ob, pos, n.dob)
            j = m if pos == 0 else peers[pos - 1]
            slope = n.gpr[l, share(j), :]
            if pos == 0:
                slope = jnp.concatenate([slope, n.gpr[l, tail, :]], axis=0)
            d_l = (dot(rows, n.wd[l], 1, 1) * slope).astype(BF)
            n.dlf[share(j), :] = d_l[:SHARE]
            part = dot(d_l, n.wu[l], 1, 1)
            if pos == 0:
                n.dlf[tail, :] = d_l[SHARE:]
                send_tail(0, part[SHARE:])
                keep_own(part)
            else:
                send_part(pos - 1, part)
        for cp in copies:
            cp.wait_send()
        if again:
            g_third("o")
            g_third("q")
            g_last(1, "d", False)
            g_last(1, "u", False)
        grad = dot(n.act[l], n.dob[...], 0, 0).astype(BF)
        for k in range(8):
            n.gb[k % 2, (k // 2) % 2, k // 4, seg_rows("d"), :] = grad[:, 128 * k:128 * k + 128]
        g_first("d")
        grad = dot(n.hin[l], n.dlf[...], 0, 0).astype(BF)
        for k in range(8):
            for t in range(8):
                n.gb[k % 2, (k // 2) % 2, k // 4, pl.ds(1024 + 128 * t, 128), :] = grad[128 * k:128 * k + 128, 128 * t:128 * t + 128]
        g_first("u")
        n.sg[l, pl.ds(10, 1), :] = jnp.sum(n.dlf[...].astype(F32), axis=0, keepdims=True)
        d_hidden = reduced(0)
        d_settled = grad_rows + ln_back(l, 2, d_hidden)
        d_br = ln_back(l, 1, d_settled).astype(BF)
        copies = gather_rows(n.dbr, d_br)
        n.stl[...] = d_settled
        ln_params(l, 2, d_hidden)
        ln_params(l, 1, d_settled)
        n.sg[l, pl.ds(8, 1), :] = jnp.sum(d_br.astype(F32) * counted, axis=0, keepdims=True)
        for pos in range(4):
            if pos > 0:
                copies[pos - 1].wait_recv()
            rows = order_rows(d_br, pos, n.dbr)
            j = m if pos == 0 else peers[pos - 1]
            d_at = dot(rows, n.wo[l], 1, 1)
            for h in range(SEQ_N):
                cut = slice(HD * h, HD * h + HD)
                n.ds_[h, chunk_rows(j, PACK), :] = pack_rows(d_at[:SHARE, cut]).astype(BF)
                if pos == 0:
                    n.ds_[h, pl.ds(MP_N * PACK, TAIL), :] = pad_lanes(d_at[SHARE:, cut]).astype(BF)
            chunk_send(n.ds_, n.dA, l, j, pos, PACK, n.do_ss, n.do_r)
            if pos == 0:
                tail_send(n.ds_, n.dA, l, MP_N * PACK, TAIL, n.do_ss, n.do_r)
        for cp in copies:
            cp.wait_send()
        g_second("d")
        g_second("u")
        grad = dot(n.att[l], n.dbr[...], 0, 0).astype(BF)
        if again:
            g_last(1, "o", False)
        for k in range(8):
            n.gb[k % 2, (k // 2) % 2, k // 4, seg_rows("o"), :] = grad[:, 128 * k:128 * k + 128]
        g_first("o")
        chunk_wait(n.ds_, n.dA, l, PACK, MP_N * PACK, TAIL, n.do_ss, n.do_r)
        for zb in range(SEQ_N):
            for j in range(MP_N):
                vals = n.dA[l, zb, pl.ds(PACK * j, PACK), :]
                at = ROWS * zb + SHARE * j
                n.do_s[pl.ds(at, PACK), :] = vals[:, :HD]
                n.do_s[pl.ds(at + PACK, PACK), :] = vals[:, HD:]
            n.do_s[pl.ds(ROWS * zb + SHARE * MP_N, TAIL), :] = n.dA[l, zb, pl.ds(PACK * MP_N, TAIL), :][:, :HD]
        for i in reversed(range(SEQ_N)):
            width = ROWS * (i + 1)
            here = pl.ds(ROWS * i, ROWS)
            p = pts[i][l]
            dpt = dot(n.v_s[l, pl.ds(0, width), :], n.do_s[here, :], 1, 1)
            pf = p.astype(F32)
            mean_term = jnp.sum(pf * dpt, axis=0, keepdims=True)
            dst = (pf * (dpt - mean_term)).astype(BF)
            dv = dot(p, n.do_s[here, :])
            dk = dot(dst, n.q_s[l, here, :])
            if i < SEQ_N - 1:
                dv = dv + n.dv_s[pl.ds(0, width), :]
                dk = dk + n.dk_s[pl.ds(0, width), :]
            if i > 0:
                n.dv_s[pl.ds(0, ROWS * i), :] = dv[:ROWS * i]
                n.dk_s[pl.ds(0, ROWS * i), :] = dk[:ROWS * i]
            dq = dot(n.k_s[l, pl.ds(0, width), :], dst, 0, 0).T * SCORE_SCALE
            dk = dk[ROWS * i:] * SCORE_SCALE
            dv = dv[ROWS * i:]
            for j in range(MP_N):
                cut = slice(SHARE * j, SHARE * j + SHARE)
                n.es[i, pl.ds(BLK * j, SHARE), :] = jnp.concatenate([dq[cut], dk[cut]], axis=1).astype(BF)
                n.es[i, pl.ds(BLK * j + SHARE, PACK), :] = pack_rows(dv[cut]).astype(BF)
            cut = slice(SHARE * MP_N, ROWS)
            n.es[i, pl.ds(BLK * MP_N, TAIL), :] = jnp.concatenate([dq[cut], dk[cut]], axis=1).astype(BF)
            n.es[i, pl.ds(BLK * MP_N + TAIL, TAIL), :] = pad_lanes(dv[cut]).astype(BF)
        copies = whole_copies(n.es, n.eA, l, n.e_s, n.e_r)
        for cp in copies:
            cp.start()
        n.eA[l, s] = n.es[s]
        g_second("o")
        g_third("d")
        if again:
            g_last(1, "q", False)
        for cp in copies:
            cp.wait()
        for j in range(MP_N + 1):
            count = SHARE if j < MP_N else TAIL
            both = [n.eA[l, h, pl.ds(BLK * j, count), :] for h in range(SEQ_N)]
            vals = [n.eA[l, h, pl.ds(BLK * j + count, PACK if j < MP_N else TAIL), :] for h in range(SEQ_N)]
            n.dpr[pl.ds(SHARE * j, count), pl.ds(0, COLS)] = jnp.concatenate([g[:, :HD] for g in both], axis=1)
            n.dpr[pl.ds(SHARE * j, count), pl.ds(COLS, COLS)] = jnp.concatenate([g[:, HD:] for g in both], axis=1)
            if j < MP_N:
                n.dpr[pl.ds(SHARE * j, PACK), pl.ds(2 * COLS, COLS)] = jnp.concatenate([g[:, :HD] for g in vals], axis=1)
                n.dpr[pl.ds(SHARE * j + PACK, PACK), pl.ds(2 * COLS, COLS)] = jnp.concatenate([g[:, HD:] for g in vals], axis=1)
            else:
                n.dpr[tail, pl.ds(2 * COLS, COLS)] = jnp.concatenate([g[:, :HD] for g in vals], axis=1)

        def d_norm_part(rows):
            total = dot(rows[:, :COLS], n.wq[l, 0], 1, 1)
            total = total + dot(rows[:, COLS:2 * COLS], n.wq[l, 1], 1, 1)
            return total + dot(rows[:, 2 * COLS:], n.wq[l, 2], 1, 1)

        for r in (2, 0, 1):
            send_part(r, d_norm_part(n.dpr[share(peers[r]), :]))
        part = d_norm_part(jnp.concatenate([n.dpr[share(m), :], n.dpr[tail, :]], axis=0))
        send_tail(1, part[SHARE:])
        keep_own(part)
        grad = dot(n.nrm[l], n.dpr[...], 0, 0).astype(BF)
        for k in range(8):
            for t in range(6):
                n.gb[k % 2, (k // 2) % 2, k // 4, pl.ds(2304 + 128 * t, 128), :] = grad[128 * k:128 * k + 128, 128 * t:128 * t + 128]
        g_first("q")
        sums = jnp.sum(n.dpr[...].astype(F32), axis=0, keepdims=True)
        for at, lane in ((11, 0), (12, 128), (13, 512), (14, 640)):
            n.sg[l, pl.ds(at, 1), :] = jnp.concatenate([sums[:, lane:lane + 128]] * 8, axis=1)
        n.sg[l, pl.ds(15, 1), :] = jnp.zeros((1, D), F32)
        g_third("u")
        d_norm = reduced(1)
        n.grd[...] = n.stl[...] + ln_back(l, 0, d_norm)
        ln_params(l, 0, d_norm)
        g_second("q")

    forward(0, True)
    forward(1, False)
    result_copies = final_rows(0, n.resb, n.res_o, n.cur[...])
    loads[6].wait()
    loads[7].wait()
    backward(1, False)
    backward(0, True)
    grad_copies = final_rows(1, n.gstb, n.gst_o, n.grd[...])

    small = []
    for t, dev in enumerate(group):
        lanes = pl.ds(pl.multiple_of((dev[0] * 2 + dev[1]) * 128, 128), 128)
        cp = rcopy(n.sg.at[:, :, lanes], n.smR.at[t], n.sm_s.at[t], n.sm_r.at[t], dev)
        cp.start()
        small.append(cp)
    g_third("o")
    for cp in small:
        cp.wait()
    total = n.sg[:, :, pl.ds(pl.multiple_of((s * 2 + c) * 128, 128), 128)]
    for t in range(7):
        total = total + n.smR[t]
    n.smS[...] = total
    small = []
    for r in range(3):
        cp = rcopy(n.smS, n.smM.at[r], n.sn_s.at[r], n.sn_r.at[r], mp_dev(r))
        cp.start()
        small.append(cp)
    g_third("q")
    g_last(0, "d", True)
    g_last(0, "u", True)
    g_last(0, "o", True)
    for cp in small:
        cp.wait()
    shared = lax.broadcasted_iota(jnp.int32, (2, SMALL, 128), 1) < 10
    n.sm_o[...] = total + jnp.where(shared, n.smM[0] + n.smM[1] + n.smM[2], 0.0)
    g_last(0, "q", True)
    for seg in SEG:
        g_out(0, seg).wait()
    for cp in result_copies + grad_copies:
        cp.wait()


def fused_shards(
    stream, text_len, norm_gain, norm_shift, w_qkv, bias_qv, w_out, bias_out, w_up, bias_up, w_down, bias_down, cotangent
):
    rows = (ROWS, D)
    any_space = pl.BlockSpec(memory_space=pl.ANY)
    vmem = pl.BlockSpec(memory_space=pltpu.VMEM)
    smem = pl.BlockSpec(memory_space=pltpu.SMEM)
    outs = pl.pallas_call(
        fused_kernel,
        out_shape=(
            jax.ShapeDtypeStruct(rows, BF),
            jax.ShapeDtypeStruct(rows, BF),
            jax.ShapeDtypeStruct((2, 3, 128, COLS), F32),
            jax.ShapeDtypeStruct((2, COLS, 128), F32),
            jax.ShapeDtypeStruct((2, 128, FFL), F32),
            jax.ShapeDtypeStruct((2, FFL, 128), F32),
            jax.ShapeDtypeStruct((2, SMALL, 128), F32),
        ),
        in_specs=[smem, any_space, any_space, vmem, vmem, vmem, vmem, vmem, vmem] + [any_space] * 4,
        out_specs=[any_space] * 6 + [vmem],
        scratch_shapes=[pltpu.VMEM(shape, dtype) for shape, dtype in VMEM_SCRATCH.values()]
        + [pltpu.SemaphoreType.DMA(shape) for shape in DMA_SEMS.values()],
        compiler_params=pltpu.CompilerParams(
            collective_id=0, has_side_effects=True, vmem_limit_bytes=63 * 2**20
        ),
    )(
        text_len,
        stream.reshape(rows),
        cotangent.reshape(rows),
        norm_gain,
        norm_shift,
        bias_qv,
        bias_out.reshape(2, 1, D),
        bias_up.reshape(2, 1, FFL),
        bias_down.reshape(2, 1, D),
        w_qkv.transpose(0, 2, 1, 3),
        w_out,
        w_up,
        w_down,
    )
    result, grad_stream, grad_q, grad_o, grad_u, grad_d, small = outs
    mine = (lax.axis_index("seq") * DP_N + lax.axis_index("dp")) * 32
    qv = small[:, 11:15].reshape(2, 2, COLS)
    return (
        result.astype(F32).reshape(1, ROWS, D),
        grad_stream.astype(F32).reshape(1, ROWS, D),
        small[:, 0:4],
        small[:, 4:8],
        grad_q.transpose(0, 2, 1, 3),
        lax.dynamic_slice_in_dim(qv, mine, 32, 2),
        grad_o,
        small[:, 8],
        grad_u,
        small[:, 10],
        grad_d,
        small[:, 9],
    )


def solution(mesh):
    return jax.shard_map(
        fused_shards if fits(mesh) else shards,
        mesh=mesh,
        in_specs=(
            P("dp", "seq", None),
            P("dp"),
            P(),
            P(),
            P(None, None, None, "mp"),
            P(None, None, "mp"),
            P(None, "mp", None),
            P(),
            P(None, None, "mp"),
            P(None, "mp"),
            P(None, "mp", None),
            P(),
            P("dp", "seq", None),
        ),
        out_specs=(
            P("dp", "seq", None),
            P("dp", "seq", None),
            P(None, None, ("seq", "dp")),
            P(None, None, ("seq", "dp")),
            P(None, ("seq", "dp"), None, "mp"),
            P(None, None, ("mp", "seq", "dp")),
            P(None, "mp", ("seq", "dp")),
            P(None, ("seq", "dp")),
            P(None, ("seq", "dp"), "mp"),
            P(None, ("mp", "seq", "dp")),
            P(None, "mp", ("seq", "dp")),
            P(None, ("seq", "dp")),
        ),
        check_vma=False,
    )
```

```python
from functools import partial
import math

import jax
import jax.numpy as jnp
from jax import lax
from jax.experimental import pallas as pl
from jax.experimental.pallas import tpu as pltpu
from jax.sharding import PartitionSpec as P

D = 1024
HEADS = 16
TEXT = 64


relax_alpha = 32.0
norm_eps = 1e-05


def layer_norm(row_values, gain_row, shift_row):
    row_mean = jnp.mean(row_values, axis=-1, keepdims=True)
    centred = row_values - row_mean
    variance = jnp.mean(centred * centred, axis=-1, keepdims=True)
    return centred * lax.rsqrt(variance + norm_eps) * gain_row + shift_row


def norm_back(row_values, gain_row, shift_row, grad_rows):
    result_value, pull_back = jax.vjp(layer_norm, row_values, gain_row, shift_row)
    return pull_back(grad_rows)


def reduce_rows(partial_sum):
    return lax.psum_scatter(
        partial_sum.astype(jnp.bfloat16), "mp", scatter_dimension=0, tiled=True
    ).astype(jnp.float32)


def widen_rows(row_values):
    return lax.all_gather(row_values, "mp", axis=0, tiled=True)


def reduce_grads(partial_sum):
    return lax.psum_scatter(
        partial_sum.astype(jnp.bfloat16), "mp", scatter_dimension=0, tiled=True
    ).astype(jnp.float32)


def widen_grads(row_values):
    return lax.all_gather(row_values, "mp", axis=0, tiled=True)


def relaxed_scores(query_heads, key_heads, allowed, score_scale):
    raw_scores = (
        jnp.einsum("sqhe,skhe->shqk", query_heads, key_heads, preferred_element_type=jnp.float32)
        * score_scale
    )
    return jnp.where(allowed, raw_scores / relax_alpha, -1e30)


def shards(
    stream,
    text_len,
    norm_gain,
    norm_shift,
    w_qkv,
    bias_qv,
    w_out,
    bias_out,
    w_up,
    bias_up,
    w_down,
    bias_down,
    cotangent,
):
    seq_count, block_len, model_width = stream.shape
    rows_all = seq_count * block_len
    layers = w_qkv.shape[0]
    local_cols = w_qkv.shape[3]
    head_dim = D // HEADS
    heads_here = local_cols // head_dim
    score_scale = 1.0 / math.sqrt(head_dim)
    share_rows = rows_all // lax.axis_size("mp")
    first_row = lax.axis_index("mp") * share_rows
    block_start = lax.axis_index("seq") * block_len
    seq_span = block_len * lax.axis_size("seq")
    query_pos = block_start + jnp.arange(block_len, dtype=jnp.int32)
    key_pos = jnp.arange(seq_span, dtype=jnp.int32)
    causal = key_pos[None, :] <= query_pos[:, None]
    visible = (key_pos[None, :] >= TEXT) | (key_pos[None, :] < text_len[:, None])
    allowed = causal[None, None] & visible[:, None, None, :]
    flat_rows = stream.reshape(rows_all, model_width)
    grad_rows = cotangent.reshape(rows_all, model_width)
    current = lax.dynamic_slice_in_dim(flat_rows, first_row, share_rows, 0)
    grad_rows = lax.dynamic_slice_in_dim(grad_rows, first_row, share_rows, 0)
    gelu_tanh = partial(jax.nn.gelu, approximate=True)
    kept_state = []
    for layer_at in range(layers):
        gain_rows = norm_gain[layer_at]
        shift_rows = norm_shift[layer_at]
        normed = widen_rows(layer_norm(current, gain_rows[0], shift_rows[0]).astype(jnp.bfloat16))
        projected = jnp.einsum(
            "td,dcf->tcf", normed, w_qkv[layer_at], preferred_element_type=jnp.float32
        )
        queries = (projected[:, 0] + bias_qv[layer_at, 0]).astype(jnp.bfloat16)
        key_rows = projected[:, 1].astype(jnp.bfloat16)
        value_rows = (projected[:, 2] + bias_qv[layer_at, 1]).astype(jnp.bfloat16)
        keys_all, values_all = (
            lax.all_gather(
                key_rows.reshape(seq_count, block_len, local_cols), "seq", axis=1, tiled=True
            ),
            lax.all_gather(
                value_rows.reshape(seq_count, block_len, local_cols), "seq", axis=1, tiled=True
            ),
        )
        query_heads = queries.reshape(seq_count, block_len, heads_here, head_dim)
        key_heads = keys_all.reshape(seq_count, seq_span, heads_here, head_dim)
        value_heads = values_all.reshape(seq_count, seq_span, heads_here, head_dim)
        tempered = relaxed_scores(query_heads, key_heads, allowed, score_scale)
        highest = jnp.max(tempered, axis=-1, keepdims=True)
        exponent = jnp.exp(relax_alpha * (tempered - highest))
        totals = jnp.sum(exponent, axis=-1, keepdims=True)
        log_total = relax_alpha * highest + jnp.log(totals)
        weights = (exponent / totals).astype(jnp.bfloat16)
        attended = jnp.einsum(
            "shqk,skhe->sqhe", weights, value_heads, preferred_element_type=jnp.float32
        )
        attended = attended.astype(jnp.bfloat16).reshape(rows_all, local_cols)
        branch = (
            reduce_rows(jnp.dot(attended, w_out[layer_at], preferred_element_type=jnp.float32))
            + bias_out[layer_at]
        )
        settled = current + layer_norm(branch, gain_rows[1], shift_rows[1])
        hidden_in = widen_rows(
            layer_norm(settled, gain_rows[2], shift_rows[2]).astype(jnp.bfloat16)
        )
        lifted = (
            jnp.dot(hidden_in, w_up[layer_at], preferred_element_type=jnp.float32)
            + bias_up[layer_at]
        )
        activated = gelu_tanh(lifted).astype(jnp.bfloat16)
        output_branch = (
            reduce_rows(jnp.dot(activated, w_down[layer_at], preferred_element_type=jnp.float32))
            + bias_down[layer_at]
        )
        kept_state.append(
            (
                current,
                normed,
                query_heads,
                key_heads,
                value_heads,
                log_total,
                attended,
                branch,
                settled,
                hidden_in,
                lifted,
                activated,
                output_branch,
            )
        )
        current = settled + layer_norm(output_branch, gain_rows[3], shift_rows[3])
    collected = []
    for layer_at in reversed(range(layers)):
        (
            layer_in,
            normed,
            query_heads,
            key_heads,
            value_heads,
            log_total,
            attended,
            branch,
            settled,
            hidden_in,
            lifted,
            activated,
            output_branch,
        ) = kept_state[layer_at]
        gain_rows = norm_gain[layer_at]
        shift_rows = norm_shift[layer_at]
        d_out_branch, gain_three, shift_three = norm_back(
            output_branch, gain_rows[3], shift_rows[3], grad_rows
        )
        d_out_branch = d_out_branch.astype(jnp.bfloat16)
        d_bias_down = jnp.sum(d_out_branch.astype(jnp.float32), axis=0)
        d_down_full = widen_grads(d_out_branch)
        d_w_down = jnp.einsum(
            "tf,td->fd", activated, d_down_full, preferred_element_type=jnp.float32
        )
        d_activated = jnp.einsum(
            "td,fd->tf", d_down_full, w_down[layer_at], preferred_element_type=jnp.float32
        )
        gelu_value, gelu_pull = jax.vjp(gelu_tanh, lifted)
        d_lifted = gelu_pull(d_activated)[0].astype(jnp.bfloat16)
        d_bias_up = jnp.sum(d_lifted.astype(jnp.float32), axis=0)
        d_w_up = jnp.einsum("td,tf->df", hidden_in, d_lifted, preferred_element_type=jnp.float32)
        d_hidden = reduce_grads(
            jnp.einsum("tf,df->td", d_lifted, w_up[layer_at], preferred_element_type=jnp.float32)
        )
        d_norm_two, gain_two, shift_two = norm_back(settled, gain_rows[2], shift_rows[2], d_hidden)
        d_settled = grad_rows + d_norm_two
        d_branch, gain_one, shift_one = norm_back(branch, gain_rows[1], shift_rows[1], d_settled)
        d_branch = d_branch.astype(jnp.bfloat16)
        d_bias_out = jnp.sum(d_branch.astype(jnp.float32), axis=0)
        d_branch_full = widen_grads(d_branch)
        d_w_out = jnp.einsum(
            "tf,td->fd", attended, d_branch_full, preferred_element_type=jnp.float32
        )
        d_attended = jnp.einsum(
            "td,fd->tf", d_branch_full, w_out[layer_at], preferred_element_type=jnp.float32
        )
        d_attended = d_attended.astype(jnp.bfloat16).reshape(
            seq_count, block_len, heads_here, head_dim
        )
        tempered = relaxed_scores(query_heads, key_heads, allowed, score_scale)
        probabilities = jnp.exp(relax_alpha * tempered - log_total)
        d_probs = jnp.einsum(
            "sqhe,skhe->shqk", d_attended, value_heads, preferred_element_type=jnp.float32
        )
        d_values = jnp.einsum(
            "shqk,sqhe->skhe",
            probabilities.astype(jnp.bfloat16),
            d_attended,
            preferred_element_type=jnp.float32,
        )
        mean_term = jnp.sum(probabilities * d_probs, axis=-1, keepdims=True)
        d_raw = (probabilities * (d_probs - mean_term)).astype(jnp.bfloat16)
        d_queries = (
            jnp.einsum("shqk,skhe->sqhe", d_raw, key_heads, preferred_element_type=jnp.float32)
            * score_scale
        )
        d_keys = (
            jnp.einsum("shqk,sqhe->skhe", d_raw, query_heads, preferred_element_type=jnp.float32)
            * score_scale
        )
        d_keys_own, d_values_own = (
            lax.psum_scatter(
                d_keys.reshape(seq_count, seq_span, local_cols).astype(jnp.bfloat16),
                "seq",
                scatter_dimension=1,
                tiled=True,
            ).astype(jnp.float32),
            lax.psum_scatter(
                d_values.reshape(seq_count, seq_span, local_cols).astype(jnp.bfloat16),
                "seq",
                scatter_dimension=1,
                tiled=True,
            ).astype(jnp.float32),
        )
        d_queries = d_queries.reshape(rows_all, local_cols).astype(jnp.bfloat16)
        d_keys_own = d_keys_own.reshape(rows_all, local_cols).astype(jnp.bfloat16)
        d_values_own = d_values_own.reshape(rows_all, local_cols).astype(jnp.bfloat16)
        d_bias_qv = jnp.stack(
            [
                jnp.sum(d_queries.astype(jnp.float32), axis=0),
                jnp.sum(d_values_own.astype(jnp.float32), axis=0),
            ]
        )
        d_projected = jnp.stack([d_queries, d_keys_own, d_values_own], axis=1)
        d_w_qkv = jnp.einsum("td,tcf->dcf", normed, d_projected, preferred_element_type=jnp.float32)
        d_normed = reduce_grads(
            jnp.einsum(
                "tcf,dcf->td", d_projected, w_qkv[layer_at], preferred_element_type=jnp.float32
            )
        )
        d_layer_in, gain_zero, shift_zero = norm_back(
            layer_in, gain_rows[0], shift_rows[0], d_normed
        )
        grad_rows = d_settled + d_layer_in
        collected.append(
            (
                jnp.stack([gain_zero, gain_one, gain_two, gain_three]),
                jnp.stack([shift_zero, shift_one, shift_two, shift_three]),
                d_w_qkv,
                d_bias_qv,
                d_w_out,
                d_bias_out,
                d_w_up,
                d_bias_up,
                d_w_down,
                d_bias_down,
            )
        )
    collected = collected[::-1]
    stacked = tuple((jnp.stack([entry[index_at] for entry in collected]) for index_at in range(10)))
    (
        gain_grads,
        shift_grads,
        grad_qkv,
        grad_qv,
        grad_out_w,
        grad_out_b,
        grad_up_w,
        grad_up_b,
        grad_down_w,
        grad_down_b,
    ) = stacked
    gain_grads, shift_grads, grad_out_b, grad_down_b = (
        lax.psum(gain_grads.astype(jnp.bfloat16), "mp").astype(jnp.float32),
        lax.psum(shift_grads.astype(jnp.bfloat16), "mp").astype(jnp.float32),
        lax.psum(grad_out_b.astype(jnp.bfloat16), "mp").astype(jnp.float32),
        lax.psum(grad_down_b.astype(jnp.bfloat16), "mp").astype(jnp.float32),
    )
    current, grad_rows = (
        lax.all_gather(current.astype(jnp.bfloat16), "mp", axis=0, tiled=True).astype(
            current.dtype
        ),
        lax.all_gather(grad_rows.astype(jnp.bfloat16), "mp", axis=0, tiled=True).astype(
            grad_rows.dtype
        ),
    )
    summed = (
        lax.psum_scatter(
            gain_grads.astype(jnp.bfloat16), ("seq", "dp"), scatter_dimension=2, tiled=True
        ).astype(jnp.float32),
        lax.psum_scatter(
            shift_grads.astype(jnp.bfloat16), ("seq", "dp"), scatter_dimension=2, tiled=True
        ).astype(jnp.float32),
        lax.psum_scatter(
            grad_qkv.astype(jnp.bfloat16), ("seq", "dp"), scatter_dimension=1, tiled=True
        ).astype(jnp.float32),
        lax.psum_scatter(
            grad_qv.astype(jnp.bfloat16), ("seq", "dp"), scatter_dimension=2, tiled=True
        ).astype(jnp.float32),
        lax.psum_scatter(
            grad_out_w.astype(jnp.bfloat16), ("seq", "dp"), scatter_dimension=2, tiled=True
        ).astype(jnp.float32),
        lax.psum_scatter(
            grad_out_b.astype(jnp.bfloat16), ("seq", "dp"), scatter_dimension=1, tiled=True
        ).astype(jnp.float32),
        lax.psum_scatter(
            grad_up_w.astype(jnp.bfloat16), ("seq", "dp"), scatter_dimension=1, tiled=True
        ).astype(jnp.float32),
        lax.psum_scatter(
            grad_up_b.astype(jnp.bfloat16), ("seq", "dp"), scatter_dimension=1, tiled=True
        ).astype(jnp.float32),
        lax.psum_scatter(
            grad_down_w.astype(jnp.bfloat16), ("seq", "dp"), scatter_dimension=2, tiled=True
        ).astype(jnp.float32),
        lax.psum_scatter(
            grad_down_b.astype(jnp.bfloat16), ("seq", "dp"), scatter_dimension=1, tiled=True
        ).astype(jnp.float32),
    )
    result = current.reshape(seq_count, block_len, model_width)
    grad_stream = grad_rows.reshape(seq_count, block_len, model_width)
    return (
        result,
        grad_stream,
        summed[0],
        summed[1],
        summed[2],
        summed[3],
        summed[4],
        summed[5],
        summed[6],
        summed[7],
        summed[8],
        summed[9],
    )


MESH = pl.DeviceIdType.MESH
BF = jnp.bfloat16
F32 = jnp.float32

SEQ_N, DP_N, MP_N = 4, 2, 4
ROWS = 272
SHARE = 64
TAIL = 16
OWN = SHARE + TAIL
HD = 64
COLS = 256
FFL = 1024
PACK = 32
BLK = SHARE + PACK
QKV_ROWS = MP_N * BLK + 2 * TAIL
VP_ROWS = MP_N * PACK + TAIL
SEG = {"d": (0, 1024), "u": (1024, 1024), "o": (2048, 256), "q": (2304, 768)}
SEG_AT = {"d": 0, "u": 1, "o": 2, "q": 3}
GROWS = 3072
GPIECE = GROWS // 8
OUT_GRADS = 2 * ROWS
OUT_SMALL = OUT_GRADS + 2 * GPIECE
OUT_ROWS = OUT_SMALL + 16
SMALL = 16
SQRT_2_PI = math.sqrt(2.0 / math.pi)
SCORE_SCALE = 0.125


def dot(a, b, ca=1, cb=0):
    return lax.dot_general(a, b, (((ca,), (cb,)), ((), ())), preferred_element_type=F32)


def fits(mesh):
    return dict(mesh.shape) == {"seq": SEQ_N, "dp": DP_N, "mp": MP_N}


VMEM_SCRATCH = {
    "wq": ((2, 3, D, COLS), BF),
    "wo": ((2, COLS, D), BF),
    "wu": ((2, D, FFL), BF),
    "wd": ((2, FFL, D), BF),
    "cur": ((OWN, D), F32),
    "grd": ((OWN, D), F32),
    "stl": ((OWN, D), F32),
    "own": ((OWN, D), F32),
    "xh": ((2, 4, OWN, D), F32),
    "rstd": ((2, 4, OWN, 128), F32),
    "nrm": ((2, ROWS, D), BF),
    "hin0": ((4 * ROWS, D), BF),
    "hin1": ((2 * ROWS, D), BF),
    "act0": ((4 * ROWS, FFL), BF),
    "act1": ((2 * ROWS, FFL), BF),
    "gpr": ((2, ROWS, FFL), F32),
    "gprP": ((3 * ROWS, FFL), F32),
    "dob0": ((4 * ROWS, D), BF),
    "dob1": ((2 * ROWS, D), BF),
    "dbr": ((ROWS, D), BF),
    "dlf": ((4 * ROWS, FFL), BF),
    "att": ((2, ROWS, COLS), BF),
    "dpr": ((ROWS, 3 * COLS), BF),
    "qkvA": ((2, SEQ_N, QKV_ROWS, 128), BF),
    "q_s": ((2, SEQ_N * ROWS, HD), BF),
    "k_s": ((2, SEQ_N * ROWS, HD), BF),
    "v_s": ((2, SEQ_N * ROWS, HD), BF),
    "do_s": ((SEQ_N * ROWS, HD), BF),
    "dk_s": ((SEQ_N * ROWS, HD), F32),
    "dv_s": ((SEQ_N * ROWS, HD), F32),
    "pt0": ((2, ROWS, ROWS), BF),
    "pt1": ((2, 2 * ROWS, ROWS), BF),
    "pt2": ((2, 3 * ROWS, ROWS), BF),
    "pt3": ((2, 4 * ROWS, ROWS), BF),
    "oA": ((2, SEQ_N, VP_ROWS, 128), BF),
    "dA": ((2, SEQ_N, VP_ROWS, 128), BF),
    "eA": ((2, SEQ_N, QKV_ROWS, 128), BF),
    "qs": ((SEQ_N, QKV_ROWS, 128), BF),
    "os_": ((SEQ_N, VP_ROWS, 128), BF),
    "ds_": ((SEQ_N, VP_ROWS, 128), BF),
    "es": ((SEQ_N, QKV_ROWS, 128), BF),
    "rsS": ((ROWS, D), BF),
    "rsR": ((3, SHARE, D), BF),
    "rtR": ((2, 3, TAIL, D), BF),
    "gb0": ((2, 2048, 128), BF),
    "gb1": ((2, 2, 2048, 128), BF),
    "rA0": ((2048, 128), BF),
    "gb2": ((2, 2, 2, 2, 1024, 128), BF),
    "rA1": ((2, 2048, 128), BF),
    "rA2": ((2, 2, 2, 1024, 128), BF),
    "rB": ((2, 2, 1024, 128), BF),
    "rC": ((2, GROWS, 128), BF),
    "ob": ((2, GROWS, 128), BF),
    "sb": ((16, D), BF),
    "sg": ((2, SMALL, D), F32),
    "smR": ((7, 2, SMALL, 128), F32),
    "smS": ((2, SMALL, 128), F32),
    "smM": ((3, 2, SMALL, 128), F32),
    "resb": ((OWN, D), BF),
    "gstb": ((OWN, D), BF),
}
DMA_SEMS = {
    "ld": (16,),
    "ag_s": (3,), "ag_r": (3,),
    "rs_s": (3,), "rs_r": (3,),
    "rt_s": (2, 3), "rt_r": (2, 3),
    "qk_s": (3, 5), "qk_r": (3, 5),
    "do_ss": (3, 5), "do_r": (3, 5),
    "o_s": (3,), "o_r": (3,),
    "e_s": (3,), "e_r": (3,),
    "g_s": (2, 5, 4), "g_r": (2, 5, 4),
    "hp_s": (5,), "hp_r": (5,), "dp_s": (5,), "dp_r": (5,),
    "hz_s": (3, 2), "hz_r": (3, 2), "dz_s": (3, 2), "dz_r": (3, 2),
    "hf_s": (3, 3), "hf_r": (3, 3), "df_s": (3, 3), "df_r": (3, 3),
    "out": (2, 8), "so": (1,),
    "fr_s": (2, 3), "fr_r": (2, 3), "fr_t": (2, 3), "fr_u": (2, 3),
    "fl": (2, 2),
    "sm_s": (7,), "sm_r": (7,), "sn_s": (3,), "sn_r": (3,),
}
SCHEDULE = {
    (1, 7): ("a01d", "a01u",),
    (1, 70): ("f31d", "f41d",),
    (1, 8): ("a01o", "f11o", "f21o", "f31u", "f41u",),
    (1, 9): ("a01q", "f11q", "f21q",),
    (0, 2): ("a11o", "f31o", "a11q", "f31q", "a21o", "a21q",),
    (0, 7): ("a31d", "a31u", "a00o", "f10o", "f20o",),
    (0, 8): ("a00q", "f10q", "f20q", "a10o", "f30o", "a20o",),
    (0, 9): ("a31o", "a31q", "a00d", "a00u",),
    (2, 0): ("a10q", "f30q", "a20q",),
    (2, 1): ("a30o",),
    (2, 2): ("a30q",),
}
IN_NAMES = ("tl", "stream", "cot", "gain", "shift", "bqv", "bo", "bu", "bd", "wq_h", "wo_h", "wu_h", "wd_h")
OUT_NAMES = ("out_o",)


class Refs:
    pass


def fused_kernel(*all_refs):
    n = Refs()
    names = IN_NAMES + OUT_NAMES + tuple(VMEM_SCRATCH) + tuple(DMA_SEMS)
    for name, ref in zip(names, all_refs):
        setattr(n, name, ref)
    pts = (n.pt0, n.pt1, n.pt2, n.pt3)
    hin, act, dob = (n.hin0, n.hin1), (n.act0, n.act1), (n.dob0, n.dob1)

    s = lax.axis_index("seq")
    c = lax.axis_index("dp")
    m = lax.axis_index("mp")
    mx, my = lax.rem(m, 2), lax.div(m, 2)
    peers = (my * 2 + (1 - mx), (1 - my) * 2 + mx, (1 - my) * 2 + (1 - mx))
    z0, z1 = lax.rem(s, 2), lax.div(s, 2)
    zs = (z1 * 2 + (1 - z0), (1 - z1) * 2 + z0, (1 - z1) * 2 + (1 - z0))

    def mp_dev(r):
        return (s, c, peers[r])

    def z_dev(k):
        return (zs[k], c, m)

    core_dev = (s, 1 - c, m)
    group = [core_dev] + [z_dev(k) for k in range(3)] + [(zs[k], 1 - c, m) for k in range(3)]

    barrier = pltpu.get_barrier_semaphore()
    everyone = group + [mp_dev(r) for r in range(3)]
    for dev in everyone:
        pl.semaphore_signal(barrier, inc=1, device_id=dev, device_id_type=MESH)

    loads = [
        pltpu.make_async_copy(n.stream.at[pl.ds(pl.multiple_of(m * SHARE, SHARE), SHARE)], n.cur.at[pl.ds(0, SHARE)], n.ld.at[0]),
        pltpu.make_async_copy(n.stream.at[pl.ds(MP_N * SHARE, TAIL)], n.cur.at[pl.ds(SHARE, TAIL)], n.ld.at[1]),
        pltpu.make_async_copy(n.wq_h, n.wq, n.ld.at[2]),
        pltpu.make_async_copy(n.wo_h, n.wo, n.ld.at[3]),
        pltpu.make_async_copy(n.wu_h, n.wu, n.ld.at[4]),
        pltpu.make_async_copy(n.wd_h, n.wd, n.ld.at[5]),
        pltpu.make_async_copy(n.cot.at[pl.ds(pl.multiple_of(m * SHARE, SHARE), SHARE)], n.grd.at[pl.ds(0, SHARE)], n.ld.at[6]),
        pltpu.make_async_copy(n.cot.at[pl.ds(MP_N * SHARE, TAIL)], n.grd.at[pl.ds(SHARE, TAIL)], n.ld.at[7]),
    ]
    for cp in loads:
        cp.start()
    pl.semaphore_wait(barrier, len(everyone))
    loads[0].wait()
    loads[1].wait()

    def rcopy(src, dst, ss, rs, dev):
        return pltpu.make_async_remote_copy(
            src_ref=src, dst_ref=dst, send_sem=ss, recv_sem=rs, device_id=dev, device_id_type=MESH
        )

    def share(j):
        return pl.ds(pl.multiple_of(j * SHARE, SHARE), SHARE)

    tail = pl.ds(MP_N * SHARE, TAIL)

    def ln(v, l, j):
        ce = v - jnp.mean(v, axis=-1, keepdims=True)
        r = lax.rsqrt(jnp.mean(ce * ce, axis=-1, keepdims=True) + norm_eps)
        h = ce * r
        n.xh[l, j] = h
        n.rstd[l, j] = jnp.broadcast_to(r, (OWN, 128))
        return h * n.gain[l, pl.ds(j, 1), :] + n.shift[l, pl.ds(j, 1), :]

    def ln_back(l, j, dy):
        h = n.xh[l, j]
        r = n.rstd[l, j][:, :1]
        t = dy * n.gain[l, pl.ds(j, 1), :]
        m1 = jnp.mean(t, axis=-1, keepdims=True)
        m2 = jnp.mean(t * h, axis=-1, keepdims=True)
        return r * (t - m1 - h * m2)

    row_ids = lax.broadcasted_iota(jnp.int32, (OWN, 1), 0)
    counted = jnp.where((row_ids < SHARE) | (m == 0), 1.0, 0.0).astype(F32)

    def ln_params(l, j, dy):
        dw = dy * counted
        n.sg[l, pl.ds(j, 1), :] = jnp.sum(dw * n.xh[l, j], axis=0, keepdims=True)
        n.sg[l, pl.ds(4 + j, 1), :] = jnp.sum(dw, axis=0, keepdims=True)

    def gather_rows(buf, own_rows):
        buf[share(m), :] = own_rows[:SHARE]
        buf[tail, :] = own_rows[SHARE:]
        copies = []
        for r in range(3):
            cp = rcopy(buf.at[share(m)], buf.at[share(m)], n.ag_s.at[r], n.ag_r.at[r], mp_dev(r))
            cp.start()
            copies.append(cp)
        return copies

    def scatter_copy(r):
        return rcopy(n.rsS.at[share(peers[r])], n.rsR.at[r], n.rs_s.at[r], n.rs_r.at[r], mp_dev(r))

    def tail_copy(turn, r):
        return rcopy(n.rsS.at[tail], n.rtR.at[turn, r], n.rt_s.at[turn, r], n.rt_r.at[turn, r], mp_dev(r))

    def send_part(r, part):
        n.rsS[share(peers[r]), :] = part.astype(BF)
        scatter_copy(r).start()

    def send_tail(turn, part):
        n.rsS[tail, :] = part.astype(BF)
        for r in range(3):
            tail_copy(turn, r).start()

    def keep_own(part):
        n.own[...] = part

    def reduced(turn):
        for r in range(3):
            tail_copy(turn, r).wait_recv()
        for r in range(3):
            scatter_copy(r).wait_recv()
        total = n.own[:SHARE, :]
        rest = n.own[SHARE:, :].astype(BF).astype(F32)
        for r in range(3):
            total = total + n.rsR[r].astype(F32)
            rest = rest + n.rtR[turn, r].astype(F32)
        for r in range(3):
            scatter_copy(r).wait_send()
            tail_copy(turn, r).wait_send()
        return jnp.concatenate([total, rest], axis=0)

    def pack_rows(v):
        return jnp.concatenate([v[:PACK], v[PACK:]], axis=1)

    def pad_lanes(v):
        return jnp.concatenate([v, jnp.zeros_like(v)], axis=1)

    def chunk_rows(j, size):
        return pl.ds(pl.multiple_of(j * size, size), size)

    def chunk_send(stage, dest, l, j, pos, size, ss, rs):
        dest[l, s, chunk_rows(j, size), :] = stage[s, chunk_rows(j, size), :]
        for k in range(3):
            rcopy(
                stage.at[zs[k], chunk_rows(j, size)], dest.at[l, s, chunk_rows(j, size)],
                ss.at[k, pos], rs.at[k, pos], z_dev(k),
            ).start()

    def tail_send(stage, dest, l, start, size, ss, rs):
        dest[l, s, pl.ds(start, size), :] = stage[s, pl.ds(start, size), :]
        for k in range(3):
            rcopy(
                stage.at[zs[k], pl.ds(start, size)], dest.at[l, s, pl.ds(start, size)],
                ss.at[k, 4], rs.at[k, 4], z_dev(k),
            ).start()

    def chunk_wait(stage, dest, l, size, start, tail_size, ss, rs):
        order = (m,) + peers
        for k in range(3):
            for pos in range(4):
                cp = rcopy(
                    stage.at[zs[k], chunk_rows(order[pos], size)], dest.at[l, s, chunk_rows(order[pos], size)],
                    ss.at[k, pos], rs.at[k, pos], z_dev(k),
                )
                cp.wait()
            rcopy(
                stage.at[zs[k], pl.ds(start, tail_size)], dest.at[l, s, pl.ds(start, tail_size)],
                ss.at[k, 4], rs.at[k, 4], z_dev(k),
            ).wait()

    def whole_copies(stage, dest, l, ss, rs):
        return [rcopy(stage.at[zs[k]], dest.at[l, s], ss.at[k], rs.at[k], z_dev(k)) for k in range(3)]

    def g_copy(phase, l, seg):
        at = SEG_AT[seg]
        start, count = SEG[seg]
        rows = pl.ds(start, count)
        low = pl.ds(start - 2048, count)
        if phase == 0:
            dev = core_dev
            if seg in "du" and l == 0:
                src, dst = n.gb0.at[1 - c, rows], n.rA0.at[rows]
            elif seg in "du":
                src, dst = n.gb1.at[1 - c, :, rows], n.rA1.at[:, rows]
            else:
                src, dst = n.gb2.at[l, 1 - c, :, :, low], n.rA2.at[l, :, :, low]
        elif phase <= 2:
            b = 1 - z1 if phase == 1 else z1
            src, dst, dev = n.gb2.at[l, c, 1 - z0, b, low], n.rB.at[l, b, low], z_dev(0)
        else:
            dev = z_dev(1)
            if seg in "du":
                rows = pl.ds(start + 512 * (phase - 3), 512)
                src = n.gb1.at[c, 1 - z1, rows]
            else:
                src = n.gb2.at[l, c, z0, 1 - z1, low]
            dst = n.rC.at[l, rows]
        return rcopy(src, dst, n.g_s.at[l, phase, at], n.g_r.at[l, phase, at], dev)

    def f(phase, l, seg):
        g_copy(phase, l, seg).start()

    def add_to(ref, got):
        ref[...] = (ref[...].astype(F32) + got[...].astype(F32)).astype(BF)

    def a(phase, l, seg):
        g_copy(phase, l, seg).wait()
        start, count = SEG[seg]
        rows = pl.ds(start, count)
        low = pl.ds(start - 2048, count)
        if phase == 0 and seg in "du" and l == 0:
            n.ob[l, rows, :] = (n.gb0[c, rows, :].astype(F32) + n.rA0[rows, :].astype(F32)).astype(BF)
        elif phase == 0:
            for b in range(2):
                if seg in "du":
                    add_to(n.gb1.at[c, b, rows], n.rA1.at[b, rows])
                else:
                    for i in range(2):
                        add_to(n.gb2.at[l, c, i, b, low], n.rA2.at[l, i, b, low])
        elif phase <= 2:
            b = 1 - z1 if phase == 1 else z1
            add_to(n.gb2.at[l, c, z0, b, low], n.rB.at[l, b, low])
        else:
            if seg in "du":
                g_copy(4, l, seg).wait()
                mine = n.gb1[c, z1, rows, :]
            else:
                mine = n.gb2[l, c, z0, z1, low, :]
            n.ob[l, rows, :] = (mine.astype(F32) + n.rC[l, rows, :].astype(F32)).astype(BF)

    def partner_copy(buf, pos, ss, rs):
        if pos == 4:
            src, dst = tail, pl.ds(ROWS + MP_N * SHARE, TAIL)
        else:
            j = m if pos == 0 else peers[pos - 1]
            src, dst = share(j), pl.ds(pl.multiple_of(ROWS + j * SHARE, TAIL), SHARE)
        return rcopy(buf.at[src], buf.at[dst], ss.at[pos], rs.at[pos], z_dev(0))

    def block_copies(buf, k, ss, rs):
        at = ROWS * (k + 1)
        return (
            rcopy(buf.at[share(m)], buf.at[pl.ds(pl.multiple_of(at + m * SHARE, TAIL), SHARE)], ss.at[k, 0], rs.at[k, 0], z_dev(k)),
            rcopy(buf.at[tail], buf.at[pl.ds(at + MP_N * SHARE, TAIL)], ss.at[k, 1], rs.at[k, 1], z_dev(k)),
        )

    def pass_copy(buf, k, r, ss, rs):
        rows = pl.ds(pl.multiple_of(ROWS * (k + 1) + m * SHARE, TAIL), SHARE)
        return rcopy(buf.at[rows], buf.at[rows], ss.at[k, r], rs.at[k, r], mp_dev(r))

    def block_send(buf, ss, rs):
        for k in range(3):
            for cp in block_copies(buf, k, ss, rs):
                cp.start()

    def block_pass(buf, zss, zrs, ss, rs):
        for k in range(3):
            for cp in block_copies(buf, k, zss, zrs):
                cp.wait()
            for r in range(3):
                pass_copy(buf, k, r, ss, rs).start()

    def block_wait(buf, ss, rs):
        for k in range(3):
            for r in range(3):
                pass_copy(buf, k, r, ss, rs).wait()

    def others_forward(l):
        if l == 1:
            for pos in range(5):
                partner_copy(hin[1], pos, n.hp_s, n.hp_r).wait()
        else:
            block_wait(hin[0], n.hf_s, n.hf_r)
        for k in range(3 if l == 0 else 1):
            rows = pl.ds(ROWS * (k + 1), ROWS)
            value, slope = gelu_pair(dot(hin[l][rows, :], n.wu[l]) + n.bu[pl.ds(l, 1), :])
            act[l][rows, :] = value.astype(BF)
            n.gprP[pl.ds(ROWS * k, ROWS), :] = slope

    def others_backward(l):
        if l == 1:
            for pos in range(5):
                partner_copy(dob[1], pos, n.dp_s, n.dp_r).wait()
        else:
            block_wait(dob[0], n.df_s, n.df_r)
        for k in range(3 if l == 0 else 1):
            rows = pl.ds(ROWS * (k + 1), ROWS)
            n.dlf[rows, :] = (dot(dob[l][rows, :], n.wd[l], 1, 1) * n.gprP[pl.ds(ROWS * k, ROWS), :]).astype(BF)

    def half_columns(ref):
        return jnp.concatenate([ref[:, pl.ds(pl.multiple_of(z0 * 256 + 512 * b, 256), 256)] for b in range(2)], axis=1)

    def own_columns(ref):
        return ref[:, pl.ds(pl.multiple_of(s * 256, 256), 256)]

    def grad_down(l):
        if l == 1:
            grad = dot(act[1][...], half_columns(dob[1]), 0, 0).astype(BF)
            for k in range(4):
                n.gb1[k % 2, k // 2, pl.ds(0, 1024), :] = grad[:, 128 * k:128 * k + 128]
        else:
            grad = dot(own_columns(dob[0]), act[0][...], 0, 0).T.astype(BF)
            for k in range(2):
                n.gb0[k, pl.ds(0, 1024), :] = grad[:, 128 * k:128 * k + 128]
        f(0, l, "d")

    def grad_up(l):
        if l == 1:
            grad = dot(half_columns(hin[1]), n.dlf[:2 * ROWS, :], 0, 0).astype(BF)
        else:
            grad = dot(own_columns(hin[0]), n.dlf[...], 0, 0).astype(BF)
        for k in range(4 if l == 1 else 2):
            for t in range(8):
                piece = grad[128 * k:128 * k + 128, 128 * t:128 * t + 128]
                if l == 1:
                    n.gb1[k % 2, k // 2, pl.ds(1024 + 128 * t, 128), :] = piece
                else:
                    n.gb0[k, pl.ds(1024 + 128 * t, 128), :] = piece
        f(0, l, "u")

    def hook(l, at):
        for step in SCHEDULE.get((l, at), ()):
            (f if step[0] == "f" else a)(int(step[1]), int(step[2]), step[3])

    def g_out(l):
        return [
            pltpu.make_async_copy(
                n.ob.at[l, pl.ds(GPIECE * t, GPIECE)],
                n.out_o.at[pl.ds(OUT_GRADS + GPIECE * l, GPIECE), pl.ds(128 * t, 128)],
                n.out.at[l, t],
            )
            for t in range(8)
        ]

    text_count = n.tl[0]

    def gelu_pair(u):
        uu = u * u
        t = jnp.tanh(SQRT_2_PI * (u + 0.044715 * u * uu))
        half = 0.5 * (1.0 + t)
        slope = half + 0.5 * u * (1.0 - t * t) * (SQRT_2_PI * (1.0 + 3 * 0.044715 * uu))
        return u * half, slope

    order_rows = lambda own_value, pos, buf: own_value if pos == 0 else buf[share(peers[pos - 1]), :]

    def forward(l, first):
        own_rows = ln(n.cur[...], l, 0).astype(BF)
        copies = gather_rows(n.nrm.at[l], own_rows)
        if first:
            loads[2].wait()
        for pos in range(4):
            if pos > 0:
                copies[pos - 1].wait_recv()
            rows = order_rows(own_rows, pos, n.nrm.at[l])
            q = dot(rows, n.wq[l, 0]) + n.bqv[l, pl.ds(0, 1), :]
            k = dot(rows, n.wq[l, 1])
            v = dot(rows, n.wq[l, 2]) + n.bqv[l, pl.ds(1, 1), :]
            j = m if pos == 0 else peers[pos - 1]
            at = pl.multiple_of(j * BLK, BLK)
            for h in range(SEQ_N):
                cut = slice(HD * h, HD * h + HD)
                n.qs[h, pl.ds(at, SHARE), :] = jnp.concatenate([q[:SHARE, cut], k[:SHARE, cut]], axis=1).astype(BF)
                n.qs[h, pl.ds(at + SHARE, PACK), :] = pack_rows(v[:SHARE, cut]).astype(BF)
                if pos == 0:
                    n.qs[h, pl.ds(MP_N * BLK, TAIL), :] = jnp.concatenate([q[SHARE:, cut], k[SHARE:, cut]], axis=1).astype(BF)
                    n.qs[h, pl.ds(MP_N * BLK + TAIL, TAIL), :] = pad_lanes(v[SHARE:, cut]).astype(BF)
            chunk_send(n.qs, n.qkvA, l, j, pos, BLK, n.qk_s, n.qk_r)
            if pos == 0:
                tail_send(n.qs, n.qkvA, l, MP_N * BLK, 2 * TAIL, n.qk_s, n.qk_r)
        for cp in copies:
            cp.wait_send()
        if not first:
            block_pass(hin[0], n.hz_s, n.hz_r, n.hf_s, n.hf_r)
        chunk_wait(n.qs, n.qkvA, l, BLK, MP_N * BLK, 2 * TAIL, n.qk_s, n.qk_r)
        for zb in range(SEQ_N):
            for j in range(MP_N):
                both = n.qkvA[l, zb, pl.ds(BLK * j, SHARE), :]
                vals = n.qkvA[l, zb, pl.ds(BLK * j + SHARE, PACK), :]
                at = ROWS * zb + SHARE * j
                n.q_s[l, pl.ds(at, SHARE), :] = both[:, :HD]
                n.k_s[l, pl.ds(at, SHARE), :] = both[:, HD:]
                n.v_s[l, pl.ds(at, PACK), :] = vals[:, :HD]
                n.v_s[l, pl.ds(at + PACK, PACK), :] = vals[:, HD:]
            both = n.qkvA[l, zb, pl.ds(BLK * MP_N, TAIL), :]
            vals = n.qkvA[l, zb, pl.ds(BLK * MP_N + TAIL, TAIL), :]
            at = ROWS * zb + SHARE * MP_N
            n.q_s[l, pl.ds(at, TAIL), :] = both[:, :HD]
            n.k_s[l, pl.ds(at, TAIL), :] = both[:, HD:]
            n.v_s[l, pl.ds(at, TAIL), :] = vals[:, :HD]
        for i in range(SEQ_N):
            width = ROWS * (i + 1)
            st = dot(n.k_s[l, pl.ds(0, width), :], n.q_s[l, pl.ds(ROWS * i, ROWS), :], 1, 1) * SCORE_SCALE
            key_at = lax.broadcasted_iota(jnp.int32, (ROWS, ROWS), 0)
            query_at = lax.broadcasted_iota(jnp.int32, (ROWS, ROWS), 1)
            causal = key_at <= query_at
            if i == 0:
                st = jnp.where(causal & ((key_at >= TEXT) | (key_at < text_count)), st, -1e30)
            else:
                text_at = lax.broadcasted_iota(jnp.int32, (TEXT, ROWS), 0)
                st = jnp.concatenate([
                    jnp.where(text_at < text_count, st[:TEXT], -1e30),
                    st[TEXT:ROWS * i],
                    jnp.where(causal, st[ROWS * i:], -1e30),
                ], axis=0)
            e = jnp.exp(st - jnp.max(st, axis=0, keepdims=True))
            p = (e * (1.0 / jnp.sum(e, axis=0, keepdims=True))).astype(BF)
            pts[i][l] = p
            o = dot(n.v_s[l, pl.ds(0, width), :], p, 0, 0).T
            for j in range(MP_N):
                n.os_[i, pl.ds(PACK * j, PACK), :] = pack_rows(o[SHARE * j:SHARE * j + SHARE]).astype(BF)
            n.os_[i, pl.ds(PACK * MP_N, TAIL), :] = pad_lanes(o[SHARE * MP_N:]).astype(BF)
        copies = whole_copies(n.os_, n.oA, l, n.o_s, n.o_r)
        for cp in copies:
            cp.start()
        n.oA[l, s] = n.os_[s]
        if first:
            loads[3].wait()
        for cp in copies:
            cp.wait()
        for j in range(MP_N):
            got = [n.oA[l, h, pl.ds(PACK * j, PACK), :] for h in range(SEQ_N)]
            n.att[l, pl.ds(SHARE * j, PACK), :] = jnp.concatenate([g[:, :HD] for g in got], axis=1)
            n.att[l, pl.ds(SHARE * j + PACK, PACK), :] = jnp.concatenate([g[:, HD:] for g in got], axis=1)
        got = [n.oA[l, h, pl.ds(PACK * MP_N, TAIL), :] for h in range(SEQ_N)]
        n.att[l, tail, :] = jnp.concatenate([g[:, :HD] for g in got], axis=1)
        for r in (2, 0, 1):
            send_part(r, dot(n.att[l, share(peers[r]), :], n.wo[l]))
        part = dot(jnp.concatenate([n.att[l, share(m), :], n.att[l, tail, :]], axis=0), n.wo[l])
        send_tail(0, part[SHARE:])
        keep_own(part)
        branch = reduced(0) + n.bo[pl.ds(l, 1), :]
        settled = n.cur[...] + ln(branch, l, 1)
        n.stl[...] = settled
        own_rows = ln(settled, l, 2).astype(BF)
        copies = gather_rows(hin[l], own_rows)
        if first:
            block_send(hin[0], n.hz_s, n.hz_r)
        else:
            partner_copy(hin[1], 0, n.hp_s, n.hp_r).start()
            partner_copy(hin[1], 4, n.hp_s, n.hp_r).start()
        if first:
            loads[4].wait()
            loads[5].wait()
        for pos in range(4):
            if pos > 0:
                copies[pos - 1].wait_recv()
                if not first:
                    partner_copy(hin[1], pos, n.hp_s, n.hp_r).start()
            rows = order_rows(own_rows, pos, hin[l])
            value, slope = gelu_pair(dot(rows, n.wu[l]) + n.bu[pl.ds(l, 1), :])
            value = value.astype(BF)
            j = m if pos == 0 else peers[pos - 1]
            act[l][share(j), :] = value[:SHARE]
            n.gpr[l, share(j), :] = slope[:SHARE]
            part = dot(value, n.wd[l])
            if pos == 0:
                act[l][tail, :] = value[SHARE:]
                n.gpr[l, tail, :] = slope[SHARE:]
                send_tail(1, part[SHARE:])
                keep_own(part)
            else:
                send_part(pos - 1, part)
        for cp in copies:
            cp.wait_send()
        out_branch = reduced(1) + n.bd[pl.ds(l, 1), :]
        n.cur[...] = n.stl[...] + ln(out_branch, l, 3)

    def final_rows(which, stage, value):
        stage[...] = value.astype(BF)
        copies = []
        out = n.out_o.at[pl.ds(ROWS * which, ROWS)]
        for r in range(3):
            copies.append(rcopy(stage.at[pl.ds(0, SHARE)], out.at[share(m)], n.fr_s.at[which, r], n.fr_r.at[which, r], mp_dev(r)))
        copies.append(pltpu.make_async_copy(stage.at[pl.ds(0, SHARE)], out.at[share(m)], n.fl.at[which, 0]))
        copies.append(pltpu.make_async_copy(stage.at[pl.ds(SHARE, TAIL)], out.at[pl.ds(MP_N * SHARE, TAIL)], n.fl.at[which, 1]))
        for cp in copies:
            cp.start()
        return copies

    def backward(l):
        grad_rows = n.grd[...]
        d_ob = ln_back(l, 3, grad_rows).astype(BF)
        copies = gather_rows(dob[l], d_ob)
        if l == 1:
            partner_copy(dob[1], 0, n.dp_s, n.dp_r).start()
            partner_copy(dob[1], 4, n.dp_s, n.dp_r).start()
        else:
            block_send(dob[0], n.dz_s, n.dz_r)
        ln_params(l, 3, grad_rows)
        n.sg[l, pl.ds(9, 1), :] = jnp.sum(d_ob.astype(F32) * counted, axis=0, keepdims=True)
        hook(l, 0)
        for pos in range(4):
            if pos > 0:
                copies[pos - 1].wait_recv()
                if l == 1:
                    partner_copy(dob[1], pos, n.dp_s, n.dp_r).start()
            rows = order_rows(d_ob, pos, dob[l])
            j = m if pos == 0 else peers[pos - 1]
            slope = n.gpr[l, share(j), :]
            if pos == 0:
                slope = jnp.concatenate([slope, n.gpr[l, tail, :]], axis=0)
            d_l = (dot(rows, n.wd[l], 1, 1) * slope).astype(BF)
            n.dlf[share(j), :] = d_l[:SHARE]
            part = dot(d_l, n.wu[l], 1, 1)
            if pos == 0:
                n.dlf[tail, :] = d_l[SHARE:]
                send_tail(0, part[SHARE:])
                keep_own(part)
                if l == 1:
                    others_forward(1)
            else:
                send_part(pos - 1, part)
        for cp in copies:
            cp.wait_send()
        hook(l, 1)
        n.sg[l, pl.ds(10, 1), :] = jnp.sum(n.dlf[:ROWS, :].astype(F32), axis=0, keepdims=True)
        hook(l, 2)
        d_hidden = reduced(0)
        d_settled = grad_rows + ln_back(l, 2, d_hidden)
        d_br = ln_back(l, 1, d_settled).astype(BF)
        copies = gather_rows(n.dbr, d_br)
        n.stl[...] = d_settled
        ln_params(l, 2, d_hidden)
        ln_params(l, 1, d_settled)
        n.sg[l, pl.ds(8, 1), :] = jnp.sum(d_br.astype(F32) * counted, axis=0, keepdims=True)
        hook(l, 3)
        for pos in range(4):
            if pos > 0:
                copies[pos - 1].wait_recv()
            rows = order_rows(d_br, pos, n.dbr)
            j = m if pos == 0 else peers[pos - 1]
            d_at = dot(rows, n.wo[l], 1, 1)
            for h in range(SEQ_N):
                cut = slice(HD * h, HD * h + HD)
                n.ds_[h, chunk_rows(j, PACK), :] = pack_rows(d_at[:SHARE, cut]).astype(BF)
                if pos == 0:
                    n.ds_[h, pl.ds(MP_N * PACK, TAIL), :] = pad_lanes(d_at[SHARE:, cut]).astype(BF)
            chunk_send(n.ds_, n.dA, l, j, pos, PACK, n.do_ss, n.do_r)
            if pos == 0:
                tail_send(n.ds_, n.dA, l, MP_N * PACK, TAIL, n.do_ss, n.do_r)
                if l == 1:
                    others_backward(1)
                    grad_down(1)
                hook(l, 31)
        for cp in copies:
            cp.wait_send()
        hook(l, 4)
        if l == 1:
            grad_up(1)
        else:
            block_pass(dob[0], n.dz_s, n.dz_r, n.df_s, n.df_r)
        grad = dot(n.att[l], n.dbr[...], 0, 0).astype(BF)
        for k in range(8):
            n.gb2[l, k % 2, (k // 2) % 2, k // 4, pl.ds(0, 256), :] = grad[:, 128 * k:128 * k + 128]
        f(0, l, "o")
        hook(l, 5)
        chunk_wait(n.ds_, n.dA, l, PACK, MP_N * PACK, TAIL, n.do_ss, n.do_r)
        for zb in range(SEQ_N):
            for j in range(MP_N):
                vals = n.dA[l, zb, pl.ds(PACK * j, PACK), :]
                at = ROWS * zb + SHARE * j
                n.do_s[pl.ds(at, PACK), :] = vals[:, :HD]
                n.do_s[pl.ds(at + PACK, PACK), :] = vals[:, HD:]
            n.do_s[pl.ds(ROWS * zb + SHARE * MP_N, TAIL), :] = n.dA[l, zb, pl.ds(PACK * MP_N, TAIL), :][:, :HD]
        hook(l, 6)
        for i in reversed(range(SEQ_N)):
            width = ROWS * (i + 1)
            here = pl.ds(ROWS * i, ROWS)
            p = pts[i][l]
            dpt = dot(n.v_s[l, pl.ds(0, width), :], n.do_s[here, :], 1, 1)
            pf = p.astype(F32)
            mean_term = jnp.sum(pf * dpt, axis=0, keepdims=True)
            dst = (pf * (dpt - mean_term)).astype(BF)
            dv = dot(p, n.do_s[here, :])
            dk = dot(dst, n.q_s[l, here, :])
            if i < SEQ_N - 1:
                dv = dv + n.dv_s[pl.ds(0, width), :]
                dk = dk + n.dk_s[pl.ds(0, width), :]
            if i > 0:
                n.dv_s[pl.ds(0, ROWS * i), :] = dv[:ROWS * i]
                n.dk_s[pl.ds(0, ROWS * i), :] = dk[:ROWS * i]
            dq = dot(n.k_s[l, pl.ds(0, width), :], dst, 0, 0).T * SCORE_SCALE
            dk = dk[ROWS * i:] * SCORE_SCALE
            dv = dv[ROWS * i:]
            for j in range(MP_N):
                cut = slice(SHARE * j, SHARE * j + SHARE)
                n.es[i, pl.ds(BLK * j, SHARE), :] = jnp.concatenate([dq[cut], dk[cut]], axis=1).astype(BF)
                n.es[i, pl.ds(BLK * j + SHARE, PACK), :] = pack_rows(dv[cut]).astype(BF)
            cut = slice(SHARE * MP_N, ROWS)
            n.es[i, pl.ds(BLK * MP_N, TAIL), :] = jnp.concatenate([dq[cut], dk[cut]], axis=1).astype(BF)
            n.es[i, pl.ds(BLK * MP_N + TAIL, TAIL), :] = pad_lanes(dv[cut]).astype(BF)
        copies = whole_copies(n.es, n.eA, l, n.e_s, n.e_r)
        for cp in copies:
            cp.start()
        n.eA[l, s] = n.es[s]
        hook(l, 7)
        if l == 1:
            others_forward(0)
        for cp in copies:
            cp.wait()
        hook(l, 70)
        for j in range(MP_N + 1):
            count = SHARE if j < MP_N else TAIL
            both = [n.eA[l, h, pl.ds(BLK * j, count), :] for h in range(SEQ_N)]
            vals = [n.eA[l, h, pl.ds(BLK * j + count, PACK if j < MP_N else TAIL), :] for h in range(SEQ_N)]
            n.dpr[pl.ds(SHARE * j, count), pl.ds(0, COLS)] = jnp.concatenate([g[:, :HD] for g in both], axis=1)
            n.dpr[pl.ds(SHARE * j, count), pl.ds(COLS, COLS)] = jnp.concatenate([g[:, HD:] for g in both], axis=1)
            if j < MP_N:
                n.dpr[pl.ds(SHARE * j, PACK), pl.ds(2 * COLS, COLS)] = jnp.concatenate([g[:, :HD] for g in vals], axis=1)
                n.dpr[pl.ds(SHARE * j + PACK, PACK), pl.ds(2 * COLS, COLS)] = jnp.concatenate([g[:, HD:] for g in vals], axis=1)
            else:
                n.dpr[tail, pl.ds(2 * COLS, COLS)] = jnp.concatenate([g[:, :HD] for g in vals], axis=1)

        def d_norm_part(rows):
            total = dot(rows[:, :COLS], n.wq[l, 0], 1, 1)
            total = total + dot(rows[:, COLS:2 * COLS], n.wq[l, 1], 1, 1)
            return total + dot(rows[:, 2 * COLS:], n.wq[l, 2], 1, 1)

        for r in (2, 0, 1):
            send_part(r, d_norm_part(n.dpr[share(peers[r]), :]))
        part = d_norm_part(jnp.concatenate([n.dpr[share(m), :], n.dpr[tail, :]], axis=0))
        send_tail(1, part[SHARE:])
        keep_own(part)
        grad = dot(n.nrm[l], n.dpr[...], 0, 0).astype(BF)
        for k in range(8):
            for t in range(6):
                n.gb2[l, k % 2, (k // 2) % 2, k // 4, pl.ds(256 + 128 * t, 128), :] = grad[128 * k:128 * k + 128, 128 * t:128 * t + 128]
        f(0, l, "q")
        if l == 0:
            others_backward(0)
            grad_down(0)
            grad_up(0)
        sums = jnp.sum(n.dpr[...].astype(F32), axis=0, keepdims=True)
        blank = jnp.zeros((1, 96), F32)
        for at, lane in ((11, 0), (12, 2 * COLS)):
            pieces = []
            for k in range(8):
                pieces += [sums[:, lane + 32 * k:lane + 32 * k + 32], blank]
            n.sg[l, pl.ds(at, 1), :] = jnp.concatenate(pieces, axis=1)
        n.sg[l, pl.ds(13, 3), :] = jnp.zeros((3, D), F32)
        hook(l, 8)
        d_norm = reduced(1)
        n.grd[...] = n.stl[...] + ln_back(l, 0, d_norm)
        ln_params(l, 0, d_norm)
        hook(l, 9)

    forward(0, True)
    forward(1, False)
    result_copies = final_rows(0, n.resb, n.cur[...])
    loads[6].wait()
    loads[7].wait()
    backward(1)
    backward(0)
    grad_copies = final_rows(1, n.gstb, n.grd[...])

    small = []
    for t, dev in enumerate(group):
        lanes = pl.ds(pl.multiple_of((dev[0] * 2 + dev[1]) * 128, 128), 128)
        cp = rcopy(n.sg.at[:, :, lanes], n.smR.at[t], n.sm_s.at[t], n.sm_r.at[t], dev)
        cp.start()
        small.append(cp)
    hook(2, 0)
    for cp in small:
        cp.wait()
    total = n.sg[:, :, pl.ds(pl.multiple_of((s * 2 + c) * 128, 128), 128)]
    for t in range(7):
        total = total + n.smR[t]
    n.smS[...] = total
    small = []
    for r in range(3):
        cp = rcopy(n.smS, n.smM.at[r], n.sn_s.at[r], n.sn_r.at[r], mp_dev(r))
        cp.start()
        small.append(cp)
    hook(2, 1)
    for cp in small:
        cp.wait()
    shared = lax.broadcasted_iota(jnp.int32, (2, SMALL, 128), 1) < 10
    total = total + jnp.where(shared, n.smM[0] + n.smM[1] + n.smM[2], 0.0)
    high = total.astype(BF)
    rest = (total - high.astype(F32)).astype(BF)
    n.sb[...] = jnp.zeros((16, D), BF)
    for l in range(2):
        n.sb[:, pl.ds(256 * l, 128)] = high[l]
        n.sb[:, pl.ds(256 * l + 128, 128)] = rest[l]
    last = [pltpu.make_async_copy(n.sb, n.out_o.at[pl.ds(OUT_SMALL, 16)], n.so.at[0])]
    last[0].start()
    hook(2, 2)
    for cp in g_out(0) + g_out(1):
        cp.start()
        last.append(cp)
    for cp in last + result_copies + grad_copies:
        cp.wait()


def finish_kernel(packed, res_o, gst_o, gain_o, shift_o, gq_o, qv_o, go_o, bo_o, gu_o, bu_o, gd_o, bd_o):
    res_o[...] = packed[:ROWS, :].astype(F32)
    gst_o[...] = packed[ROWS:2 * ROWS, :].astype(F32)
    for l in range(2):
        for b in range(24):
            lanes = slice(128 * (b // 3), 128 * (b // 3) + 128)
            start = OUT_GRADS + GPIECE * l + 128 * (b % 3)
            value = packed[start:start + 128, lanes].astype(F32)
            if b < 8:
                gd_o[l, 128 * b:128 * b + 128, :] = value
            elif b < 16:
                gu_o[l, :, 128 * (b - 8):128 * (b - 8) + 128] = value
            elif b < 18:
                go_o[l, 128 * (b - 16):128 * (b - 16) + 128, :] = value
            else:
                at = b - 18
                gq_o[l, at // 2, :, 128 * (at % 2):128 * (at % 2) + 128] = value
        small = packed[OUT_SMALL:OUT_SMALL + 16, 256 * l:256 * l + 128].astype(F32)
        small = small + packed[OUT_SMALL:OUT_SMALL + 16, 256 * l + 128:256 * l + 256].astype(F32)
        gain_o[l] = small[0:4]
        shift_o[l] = small[4:8]
        qv_o[l] = small[11:13, :32]
        bo_o[l:l + 1, :] = small[8:9]
        bd_o[l:l + 1, :] = small[9:10]
        bu_o[l:l + 1, :] = small[10:11]


def fused_shards(
    stream, text_len, norm_gain, norm_shift, w_qkv, bias_qv, w_out, bias_out, w_up, bias_up, w_down, bias_down, cotangent
):
    rows = (ROWS, D)
    any_space = pl.BlockSpec(memory_space=pl.ANY)
    vmem = pl.BlockSpec(memory_space=pltpu.VMEM)
    smem = pl.BlockSpec(memory_space=pltpu.SMEM)
    packed = pl.pallas_call(
        fused_kernel,
        out_shape=jax.ShapeDtypeStruct((OUT_ROWS, D), BF),
        in_specs=[smem, any_space, any_space, vmem, vmem, vmem, vmem, vmem, vmem] + [any_space] * 4,
        out_specs=any_space,
        scratch_shapes=[pltpu.VMEM(shape, dtype) for shape, dtype in VMEM_SCRATCH.values()]
        + [pltpu.SemaphoreType.DMA(shape) for shape in DMA_SEMS.values()],
        compiler_params=pltpu.CompilerParams(
            collective_id=0, has_side_effects=True, vmem_limit_bytes=63 * 2**20
        ),
    )(
        text_len,
        stream.reshape(rows),
        cotangent.reshape(rows),
        norm_gain,
        norm_shift,
        bias_qv,
        bias_out,
        bias_up,
        bias_down,
        w_qkv.transpose(0, 2, 1, 3),
        w_out,
        w_up,
        w_down,
    )
    shape = lambda *dims: jax.ShapeDtypeStruct(dims, F32)
    done = pl.pallas_call(
        finish_kernel,
        out_shape=(
            shape(*rows), shape(*rows), shape(2, 4, 128), shape(2, 4, 128), shape(2, 3, 128, COLS), shape(2, 2, 32),
            shape(2, COLS, 128), shape(2, 128), shape(2, 128, FFL), shape(2, 128), shape(2, FFL, 128), shape(2, 128),
        ),
        in_specs=[vmem],
        out_specs=[vmem] * 12,
        compiler_params=pltpu.CompilerParams(vmem_limit_bytes=32 * 2**20),
    )(packed)
    return (
        done[0].reshape(1, ROWS, D),
        done[1].reshape(1, ROWS, D),
        done[2],
        done[3],
        done[4].transpose(0, 2, 1, 3),
    ) + tuple(done[5:])


def solution(mesh):
    return jax.shard_map(
        fused_shards if fits(mesh) else shards,
        mesh=mesh,
        in_specs=(
            P("dp", "seq", None),
            P("dp"),
            P(),
            P(),
            P(None, None, None, "mp"),
            P(None, None, "mp"),
            P(None, "mp", None),
            P(),
            P(None, None, "mp"),
            P(None, "mp"),
            P(None, "mp", None),
            P(),
            P("dp", "seq", None),
        ),
        out_specs=(
            P("dp", "seq", None),
            P("dp", "seq", None),
            P(None, None, ("seq", "dp")),
            P(None, None, ("seq", "dp")),
            P(None, ("seq", "dp"), None, "mp"),
            P(None, None, ("mp", "seq", "dp")),
            P(None, "mp", ("seq", "dp")),
            P(None, ("seq", "dp")),
            P(None, ("seq", "dp"), "mp"),
            P(None, ("mp", "seq", "dp")),
            P(None, "mp", ("seq", "dp")),
            P(None, ("seq", "dp")),
        ),
        check_vma=False,
    )
```

```python
from functools import partial
import math

import jax
import jax.numpy as jnp
from jax import lax
from jax.experimental import pallas as pl
from jax.experimental.pallas import tpu as pltpu
from jax.sharding import PartitionSpec as P

D = 1024
HEADS = 16
TEXT = 64


relax_alpha = 32.0
norm_eps = 1e-05


def layer_norm(row_values, gain_row, shift_row):
    row_mean = jnp.mean(row_values, axis=-1, keepdims=True)
    centred = row_values - row_mean
    variance = jnp.mean(centred * centred, axis=-1, keepdims=True)
    return centred * lax.rsqrt(variance + norm_eps) * gain_row + shift_row


def norm_back(row_values, gain_row, shift_row, grad_rows):
    result_value, pull_back = jax.vjp(layer_norm, row_values, gain_row, shift_row)
    return pull_back(grad_rows)


def reduce_rows(partial_sum):
    return lax.psum_scatter(
        partial_sum.astype(jnp.bfloat16), "mp", scatter_dimension=0, tiled=True
    ).astype(jnp.float32)


def widen_rows(row_values):
    return lax.all_gather(row_values, "mp", axis=0, tiled=True)


def reduce_grads(partial_sum):
    return lax.psum_scatter(
        partial_sum.astype(jnp.bfloat16), "mp", scatter_dimension=0, tiled=True
    ).astype(jnp.float32)


def widen_grads(row_values):
    return lax.all_gather(row_values, "mp", axis=0, tiled=True)


def relaxed_scores(query_heads, key_heads, allowed, score_scale):
    raw_scores = (
        jnp.einsum("sqhe,skhe->shqk", query_heads, key_heads, preferred_element_type=jnp.float32)
        * score_scale
    )
    return jnp.where(allowed, raw_scores / relax_alpha, -1e30)


def shards(
    stream,
    text_len,
    norm_gain,
    norm_shift,
    w_qkv,
    bias_qv,
    w_out,
    bias_out,
    w_up,
    bias_up,
    w_down,
    bias_down,
    cotangent,
):
    seq_count, block_len, model_width = stream.shape
    rows_all = seq_count * block_len
    layers = w_qkv.shape[0]
    local_cols = w_qkv.shape[3]
    head_dim = D // HEADS
    heads_here = local_cols // head_dim
    score_scale = 1.0 / math.sqrt(head_dim)
    share_rows = rows_all // lax.axis_size("mp")
    first_row = lax.axis_index("mp") * share_rows
    block_start = lax.axis_index("seq") * block_len
    seq_span = block_len * lax.axis_size("seq")
    query_pos = block_start + jnp.arange(block_len, dtype=jnp.int32)
    key_pos = jnp.arange(seq_span, dtype=jnp.int32)
    causal = key_pos[None, :] <= query_pos[:, None]
    visible = (key_pos[None, :] >= TEXT) | (key_pos[None, :] < text_len[:, None])
    allowed = causal[None, None] & visible[:, None, None, :]
    flat_rows = stream.reshape(rows_all, model_width)
    grad_rows = cotangent.reshape(rows_all, model_width)
    current = lax.dynamic_slice_in_dim(flat_rows, first_row, share_rows, 0)
    grad_rows = lax.dynamic_slice_in_dim(grad_rows, first_row, share_rows, 0)
    gelu_tanh = partial(jax.nn.gelu, approximate=True)
    kept_state = []
    for layer_at in range(layers):
        gain_rows = norm_gain[layer_at]
        shift_rows = norm_shift[layer_at]
        normed = widen_rows(layer_norm(current, gain_rows[0], shift_rows[0]).astype(jnp.bfloat16))
        projected = jnp.einsum(
            "td,dcf->tcf", normed, w_qkv[layer_at], preferred_element_type=jnp.float32
        )
        queries = (projected[:, 0] + bias_qv[layer_at, 0]).astype(jnp.bfloat16)
        key_rows = projected[:, 1].astype(jnp.bfloat16)
        value_rows = (projected[:, 2] + bias_qv[layer_at, 1]).astype(jnp.bfloat16)
        keys_all, values_all = (
            lax.all_gather(
                key_rows.reshape(seq_count, block_len, local_cols), "seq", axis=1, tiled=True
            ),
            lax.all_gather(
                value_rows.reshape(seq_count, block_len, local_cols), "seq", axis=1, tiled=True
            ),
        )
        query_heads = queries.reshape(seq_count, block_len, heads_here, head_dim)
        key_heads = keys_all.reshape(seq_count, seq_span, heads_here, head_dim)
        value_heads = values_all.reshape(seq_count, seq_span, heads_here, head_dim)
        tempered = relaxed_scores(query_heads, key_heads, allowed, score_scale)
        highest = jnp.max(tempered, axis=-1, keepdims=True)
        exponent = jnp.exp(relax_alpha * (tempered - highest))
        totals = jnp.sum(exponent, axis=-1, keepdims=True)
        log_total = relax_alpha * highest + jnp.log(totals)
        weights = (exponent / totals).astype(jnp.bfloat16)
        attended = jnp.einsum(
            "shqk,skhe->sqhe", weights, value_heads, preferred_element_type=jnp.float32
        )
        attended = attended.astype(jnp.bfloat16).reshape(rows_all, local_cols)
        branch = (
            reduce_rows(jnp.dot(attended, w_out[layer_at], preferred_element_type=jnp.float32))
            + bias_out[layer_at]
        )
        settled = current + layer_norm(branch, gain_rows[1], shift_rows[1])
        hidden_in = widen_rows(
            layer_norm(settled, gain_rows[2], shift_rows[2]).astype(jnp.bfloat16)
        )
        lifted = (
            jnp.dot(hidden_in, w_up[layer_at], preferred_element_type=jnp.float32)
            + bias_up[layer_at]
        )
        activated = gelu_tanh(lifted).astype(jnp.bfloat16)
        output_branch = (
            reduce_rows(jnp.dot(activated, w_down[layer_at], preferred_element_type=jnp.float32))
            + bias_down[layer_at]
        )
        kept_state.append(
            (
                current,
                normed,
                query_heads,
                key_heads,
                value_heads,
                log_total,
                attended,
                branch,
                settled,
                hidden_in,
                lifted,
                activated,
                output_branch,
            )
        )
        current = settled + layer_norm(output_branch, gain_rows[3], shift_rows[3])
    collected = []
    for layer_at in reversed(range(layers)):
        (
            layer_in,
            normed,
            query_heads,
            key_heads,
            value_heads,
            log_total,
            attended,
            branch,
            settled,
            hidden_in,
            lifted,
            activated,
            output_branch,
        ) = kept_state[layer_at]
        gain_rows = norm_gain[layer_at]
        shift_rows = norm_shift[layer_at]
        d_out_branch, gain_three, shift_three = norm_back(
            output_branch, gain_rows[3], shift_rows[3], grad_rows
        )
        d_out_branch = d_out_branch.astype(jnp.bfloat16)
        d_bias_down = jnp.sum(d_out_branch.astype(jnp.float32), axis=0)
        d_down_full = widen_grads(d_out_branch)
        d_w_down = jnp.einsum(
            "tf,td->fd", activated, d_down_full, preferred_element_type=jnp.float32
        )
        d_activated = jnp.einsum(
            "td,fd->tf", d_down_full, w_down[layer_at], preferred_element_type=jnp.float32
        )
        gelu_value, gelu_pull = jax.vjp(gelu_tanh, lifted)
        d_lifted = gelu_pull(d_activated)[0].astype(jnp.bfloat16)
        d_bias_up = jnp.sum(d_lifted.astype(jnp.float32), axis=0)
        d_w_up = jnp.einsum("td,tf->df", hidden_in, d_lifted, preferred_element_type=jnp.float32)
        d_hidden = reduce_grads(
            jnp.einsum("tf,df->td", d_lifted, w_up[layer_at], preferred_element_type=jnp.float32)
        )
        d_norm_two, gain_two, shift_two = norm_back(settled, gain_rows[2], shift_rows[2], d_hidden)
        d_settled = grad_rows + d_norm_two
        d_branch, gain_one, shift_one = norm_back(branch, gain_rows[1], shift_rows[1], d_settled)
        d_branch = d_branch.astype(jnp.bfloat16)
        d_bias_out = jnp.sum(d_branch.astype(jnp.float32), axis=0)
        d_branch_full = widen_grads(d_branch)
        d_w_out = jnp.einsum(
            "tf,td->fd", attended, d_branch_full, preferred_element_type=jnp.float32
        )
        d_attended = jnp.einsum(
            "td,fd->tf", d_branch_full, w_out[layer_at], preferred_element_type=jnp.float32
        )
        d_attended = d_attended.astype(jnp.bfloat16).reshape(
            seq_count, block_len, heads_here, head_dim
        )
        tempered = relaxed_scores(query_heads, key_heads, allowed, score_scale)
        probabilities = jnp.exp(relax_alpha * tempered - log_total)
        d_probs = jnp.einsum(
            "sqhe,skhe->shqk", d_attended, value_heads, preferred_element_type=jnp.float32
        )
        d_values = jnp.einsum(
            "shqk,sqhe->skhe",
            probabilities.astype(jnp.bfloat16),
            d_attended,
            preferred_element_type=jnp.float32,
        )
        mean_term = jnp.sum(probabilities * d_probs, axis=-1, keepdims=True)
        d_raw = (probabilities * (d_probs - mean_term)).astype(jnp.bfloat16)
        d_queries = (
            jnp.einsum("shqk,skhe->sqhe", d_raw, key_heads, preferred_element_type=jnp.float32)
            * score_scale
        )
        d_keys = (
            jnp.einsum("shqk,sqhe->skhe", d_raw, query_heads, preferred_element_type=jnp.float32)
            * score_scale
        )
        d_keys_own, d_values_own = (
            lax.psum_scatter(
                d_keys.reshape(seq_count, seq_span, local_cols).astype(jnp.bfloat16),
                "seq",
                scatter_dimension=1,
                tiled=True,
            ).astype(jnp.float32),
            lax.psum_scatter(
                d_values.reshape(seq_count, seq_span, local_cols).astype(jnp.bfloat16),
                "seq",
                scatter_dimension=1,
                tiled=True,
            ).astype(jnp.float32),
        )
        d_queries = d_queries.reshape(rows_all, local_cols).astype(jnp.bfloat16)
        d_keys_own = d_keys_own.reshape(rows_all, local_cols).astype(jnp.bfloat16)
        d_values_own = d_values_own.reshape(rows_all, local_cols).astype(jnp.bfloat16)
        d_bias_qv = jnp.stack(
            [
                jnp.sum(d_queries.astype(jnp.float32), axis=0),
                jnp.sum(d_values_own.astype(jnp.float32), axis=0),
            ]
        )
        d_projected = jnp.stack([d_queries, d_keys_own, d_values_own], axis=1)
        d_w_qkv = jnp.einsum("td,tcf->dcf", normed, d_projected, preferred_element_type=jnp.float32)
        d_normed = reduce_grads(
            jnp.einsum(
                "tcf,dcf->td", d_projected, w_qkv[layer_at], preferred_element_type=jnp.float32
            )
        )
        d_layer_in, gain_zero, shift_zero = norm_back(
            layer_in, gain_rows[0], shift_rows[0], d_normed
        )
        grad_rows = d_settled + d_layer_in
        collected.append(
            (
                jnp.stack([gain_zero, gain_one, gain_two, gain_three]),
                jnp.stack([shift_zero, shift_one, shift_two, shift_three]),
                d_w_qkv,
                d_bias_qv,
                d_w_out,
                d_bias_out,
                d_w_up,
                d_bias_up,
                d_w_down,
                d_bias_down,
            )
        )
    collected = collected[::-1]
    stacked = tuple((jnp.stack([entry[index_at] for entry in collected]) for index_at in range(10)))
    (
        gain_grads,
        shift_grads,
        grad_qkv,
        grad_qv,
        grad_out_w,
        grad_out_b,
        grad_up_w,
        grad_up_b,
        grad_down_w,
        grad_down_b,
    ) = stacked
    gain_grads, shift_grads, grad_out_b, grad_down_b = (
        lax.psum(gain_grads.astype(jnp.bfloat16), "mp").astype(jnp.float32),
        lax.psum(shift_grads.astype(jnp.bfloat16), "mp").astype(jnp.float32),
        lax.psum(grad_out_b.astype(jnp.bfloat16), "mp").astype(jnp.float32),
        lax.psum(grad_down_b.astype(jnp.bfloat16), "mp").astype(jnp.float32),
    )
    current, grad_rows = (
        lax.all_gather(current.astype(jnp.bfloat16), "mp", axis=0, tiled=True).astype(
            current.dtype
        ),
        lax.all_gather(grad_rows.astype(jnp.bfloat16), "mp", axis=0, tiled=True).astype(
            grad_rows.dtype
        ),
    )
    summed = (
        lax.psum_scatter(
            gain_grads.astype(jnp.bfloat16), ("seq", "dp"), scatter_dimension=2, tiled=True
        ).astype(jnp.float32),
        lax.psum_scatter(
            shift_grads.astype(jnp.bfloat16), ("seq", "dp"), scatter_dimension=2, tiled=True
        ).astype(jnp.float32),
        lax.psum_scatter(
            grad_qkv.astype(jnp.bfloat16), ("seq", "dp"), scatter_dimension=1, tiled=True
        ).astype(jnp.float32),
        lax.psum_scatter(
            grad_qv.astype(jnp.bfloat16), ("seq", "dp"), scatter_dimension=2, tiled=True
        ).astype(jnp.float32),
        lax.psum_scatter(
            grad_out_w.astype(jnp.bfloat16), ("seq", "dp"), scatter_dimension=2, tiled=True
        ).astype(jnp.float32),
        lax.psum_scatter(
            grad_out_b.astype(jnp.bfloat16), ("seq", "dp"), scatter_dimension=1, tiled=True
        ).astype(jnp.float32),
        lax.psum_scatter(
            grad_up_w.astype(jnp.bfloat16), ("seq", "dp"), scatter_dimension=1, tiled=True
        ).astype(jnp.float32),
        lax.psum_scatter(
            grad_up_b.astype(jnp.bfloat16), ("seq", "dp"), scatter_dimension=1, tiled=True
        ).astype(jnp.float32),
        lax.psum_scatter(
            grad_down_w.astype(jnp.bfloat16), ("seq", "dp"), scatter_dimension=2, tiled=True
        ).astype(jnp.float32),
        lax.psum_scatter(
            grad_down_b.astype(jnp.bfloat16), ("seq", "dp"), scatter_dimension=1, tiled=True
        ).astype(jnp.float32),
    )
    result = current.reshape(seq_count, block_len, model_width)
    grad_stream = grad_rows.reshape(seq_count, block_len, model_width)
    return (
        result,
        grad_stream,
        summed[0],
        summed[1],
        summed[2],
        summed[3],
        summed[4],
        summed[5],
        summed[6],
        summed[7],
        summed[8],
        summed[9],
    )


MESH = pl.DeviceIdType.MESH
BF = jnp.bfloat16
F32 = jnp.float32

SEQ_N, DP_N, MP_N = 4, 2, 4
ROWS = 272
SHARE = 64
TAIL = 16
OWN = SHARE + TAIL
HD = 64
COLS = 256
FFL = 1024
PACK = 32
BLK = SHARE + PACK
QKV_ROWS = MP_N * BLK + 2 * TAIL
VP_ROWS = MP_N * PACK + TAIL
SEG = {"d": (0, 1024), "u": (1024, 1024), "o": (2048, 256), "q": (2304, 768)}
SEG_AT = {"d": 0, "u": 1, "o": 2, "q": 3}
GROWS = 3072
GPIECE = GROWS // 8
OUT_GRADS = 2 * ROWS
OUT_SMALL = OUT_GRADS + 2 * GPIECE
OUT_ROWS = OUT_SMALL + 16
SMALL = 16
SQRT_2_PI = math.sqrt(2.0 / math.pi)
SCORE_SCALE = 0.125


def dot(a, b, ca=1, cb=0):
    return lax.dot_general(a, b, (((ca,), (cb,)), ((), ())), preferred_element_type=F32)


def fits(mesh):
    return dict(mesh.shape) == {"seq": SEQ_N, "dp": DP_N, "mp": MP_N}


VMEM_SCRATCH = {
    "wq": ((2, 3, D, COLS), BF),
    "wo": ((2, COLS, D), BF),
    "wu": ((2, D, FFL), BF),
    "wd": ((2, FFL, D), BF),
    "cur": ((OWN, D), F32),
    "grd": ((OWN, D), F32),
    "stl": ((OWN, D), F32),
    "own": ((OWN, D), F32),
    "xh": ((2, 4, OWN, D), F32),
    "rstd": ((2, 4, OWN, 128), F32),
    "nrm0": ((4 * ROWS, D), BF),
    "nrm1": ((ROWS, D), BF),
    "hin0": ((4 * ROWS, D), BF),
    "hin1": ((2 * ROWS, D), BF),
    "act0": ((4 * ROWS, FFL), BF),
    "act1": ((2 * ROWS, FFL), BF),
    "gpr": ((2, ROWS, FFL), F32),
    "gprP": ((3 * ROWS, FFL), BF),
    "dob0": ((4 * ROWS, D), BF),
    "dbr": ((ROWS, D), BF),
    "dlf": ((4 * ROWS, FFL), BF),
    "att": ((2, ROWS, COLS), BF),
    "dpr": ((ROWS, 3 * COLS), BF),
    "qkvA": ((2, SEQ_N, QKV_ROWS, 128), BF),
    "q_s": ((2, SEQ_N * ROWS, HD), BF),
    "k_s": ((2, SEQ_N * ROWS, HD), BF),
    "v_s": ((2, SEQ_N * ROWS, HD), BF),
    "do_s": ((SEQ_N * ROWS, HD), BF),
    "dk_s": ((SEQ_N * ROWS, HD), F32),
    "dv_s": ((SEQ_N * ROWS, HD), F32),
    "pt0": ((2, ROWS, ROWS), BF),
    "pt1": ((2, 2 * ROWS, ROWS), BF),
    "pt2": ((2, 3 * ROWS, ROWS), BF),
    "pt3": ((2, 4 * ROWS, ROWS), BF),
    "oA": ((2, SEQ_N, VP_ROWS, 128), BF),
    "dA": ((2, SEQ_N, VP_ROWS, 128), BF),
    "eA": ((2, SEQ_N, QKV_ROWS, 128), BF),
    "qs": ((SEQ_N, QKV_ROWS, 128), BF),
    "os_": ((SEQ_N, VP_ROWS, 128), BF),
    "ds_": ((SEQ_N, VP_ROWS, 128), BF),
    "es": ((SEQ_N, QKV_ROWS, 128), BF),
    "rsS": ((ROWS, D), BF),
    "rsR": ((3, SHARE, D), BF),
    "rtR": ((2, 3, TAIL, D), BF),
    "eq": ((4 * ROWS, 3 * HD), BF),
    "gq": ((2, SEQ_N, 3 * HD, 128), BF),
    "rAq": ((SEQ_N, 3 * HD, 128), BF),
    "rQ": ((SEQ_N, 3 * HD, 128), BF),
    "gb0": ((2, 2048, 128), BF),
    "gb1": ((2, 2, 2048, 128), BF),
    "rA0": ((2048, 128), BF),
    "gbo": ((2, 2, 2, 2, 256, 128), BF),
    "gbq": ((2, 2, 2, 768, 128), BF),
    "rA1": ((2, 2048, 128), BF),
    "rAo": ((2, 2, 2, 256, 128), BF),
    "rAp": ((2, 2, 768, 128), BF),
    "rBo": ((2, 2, 256, 128), BF),
    "rBq": ((2, 768, 128), BF),
    "rC": ((2, GROWS, 128), BF),
    "ob": ((2, GROWS, 128), BF),
    "sb": ((16, D), BF),
    "sg": ((2, SMALL, D), F32),
    "smR": ((7, 2, SMALL, 128), F32),
    "smS": ((2, SMALL, 128), F32),
    "smM": ((3, 2, SMALL, 128), F32),
    "resb": ((OWN, D), BF),
    "gstb": ((OWN, D), BF),
}
DMA_SEMS = {
    "ld": (16,),
    "ag_s": (3,), "ag_r": (3,),
    "rs_s": (3,), "rs_r": (3,),
    "rt_s": (2, 3), "rt_r": (2, 3),
    "qk_s": (3, 5), "qk_r": (3, 5),
    "do_ss": (3, 5), "do_r": (3, 5),
    "o_s": (3, 5), "o_r": (3, 5),
    "e_s": (3, 5), "e_r": (3, 5),
    "g_s": (2, 5, 4), "g_r": (2, 5, 4),
    "hp_s": (2, 5), "hp_r": (2, 5), "dp_s": (5,), "dp_r": (5,),
    "nz_s": (3, 2), "nz_r": (3, 2), "nf_s": (3, 4), "nf_r": (3, 4),
    "gq_s": (4,), "gq_r": (4,),
    "hz_s": (3, 2), "hz_r": (3, 2), "dz_s": (3, 2), "dz_r": (3, 2),
    "hf_s": (3, 4), "hf_r": (3, 4), "df_s": (3, 4), "df_r": (3, 4),
    "out": (2, 8), "so": (1,),
    "fr_s": (2, 3), "fr_r": (2, 3), "fr_t": (2, 3), "fr_u": (2, 3),
    "fl": (2, 2),
    "sm_s": (7,), "sm_r": (7,), "sn_s": (3,), "sn_r": (3,),
}
SCHEDULE = {
    (1, 7): ("a01d", "a01u",),
    (1, 70): ("f31d", "f41d",),
    (1, 8): ("a01o", "f11o", "f21o", "f31u", "f41u",),
    (1, 9): ("a01q", "f11q", "f21q",),
    (0, 2): ("a11o", "f31o", "a11q", "f31q", "a21o", "a21q",),
    (0, 7): ("a31d", "a31u", "a00o", "f10o", "f20o",),
    (0, 8): ("a10o", "f30o", "a20o",),
    (0, 9): ("a31o", "a31q", "a00d", "a00u",),
    (2, 1): ("a30o",),
}
IN_NAMES = ("tl", "stream", "cot", "gain", "shift", "bqv", "bo", "bu", "bd", "wq_h", "wo_h", "wu_h", "wd_h")
OUT_NAMES = ("out_o",)


class Refs:
    pass


def fused_kernel(*all_refs):
    n = Refs()
    names = IN_NAMES + OUT_NAMES + tuple(VMEM_SCRATCH) + tuple(DMA_SEMS)
    for name, ref in zip(names, all_refs):
        setattr(n, name, ref)
    pts = (n.pt0, n.pt1, n.pt2, n.pt3)
    hin, act, dob = (n.hin0, n.hin1), (n.act0, n.act1), (n.dob0, n.dob0.at[pl.ds(0, 2 * ROWS)])
    nrm = (n.nrm0, n.nrm1)

    s = lax.axis_index("seq")
    c = lax.axis_index("dp")
    m = lax.axis_index("mp")
    mx, my = lax.rem(m, 2), lax.div(m, 2)
    peers = (my * 2 + (1 - mx), (1 - my) * 2 + mx, (1 - my) * 2 + (1 - mx))
    z0, z1 = lax.rem(s, 2), lax.div(s, 2)
    zs = (z1 * 2 + (1 - z0), (1 - z1) * 2 + z0, (1 - z1) * 2 + (1 - z0))

    def mp_dev(r):
        return (s, c, peers[r])

    def z_dev(k):
        return (zs[k], c, m)

    core_dev = (s, 1 - c, m)
    group = [core_dev] + [z_dev(k) for k in range(3)] + [(zs[k], 1 - c, m) for k in range(3)]

    barrier = pltpu.get_barrier_semaphore()
    everyone = group + [mp_dev(r) for r in range(3)]
    for dev in everyone:
        pl.semaphore_signal(barrier, inc=1, device_id=dev, device_id_type=MESH)

    loads = [
        pltpu.make_async_copy(n.stream.at[pl.ds(pl.multiple_of(m * SHARE, SHARE), SHARE)], n.cur.at[pl.ds(0, SHARE)], n.ld.at[0]),
        pltpu.make_async_copy(n.stream.at[pl.ds(MP_N * SHARE, TAIL)], n.cur.at[pl.ds(SHARE, TAIL)], n.ld.at[1]),
        pltpu.make_async_copy(n.wq_h, n.wq, n.ld.at[2]),
        pltpu.make_async_copy(n.wo_h, n.wo, n.ld.at[3]),
        pltpu.make_async_copy(n.wu_h, n.wu, n.ld.at[4]),
        pltpu.make_async_copy(n.wd_h, n.wd, n.ld.at[5]),
        pltpu.make_async_copy(n.cot.at[pl.ds(pl.multiple_of(m * SHARE, SHARE), SHARE)], n.grd.at[pl.ds(0, SHARE)], n.ld.at[6]),
        pltpu.make_async_copy(n.cot.at[pl.ds(MP_N * SHARE, TAIL)], n.grd.at[pl.ds(SHARE, TAIL)], n.ld.at[7]),
    ]
    for cp in loads:
        cp.start()
    loads[0].wait()
    loads[1].wait()

    def rcopy(src, dst, ss, rs, dev):
        return pltpu.make_async_remote_copy(
            src_ref=src, dst_ref=dst, send_sem=ss, recv_sem=rs, device_id=dev, device_id_type=MESH
        )

    def share(j):
        return pl.ds(pl.multiple_of(j * SHARE, SHARE), SHARE)

    tail = pl.ds(MP_N * SHARE, TAIL)

    def ln(v, l, j):
        ce = v - jnp.mean(v, axis=-1, keepdims=True)
        r = lax.rsqrt(jnp.mean(ce * ce, axis=-1, keepdims=True) + norm_eps)
        h = ce * r
        n.xh[l, j] = h
        n.rstd[l, j] = jnp.broadcast_to(r, (OWN, 128))
        return h * n.gain[l, pl.ds(j, 1), :] + n.shift[l, pl.ds(j, 1), :]

    def ln_back(l, j, dy):
        h = n.xh[l, j]
        r = n.rstd[l, j][:, :1]
        t = dy * n.gain[l, pl.ds(j, 1), :]
        m1 = jnp.mean(t, axis=-1, keepdims=True)
        m2 = jnp.mean(t * h, axis=-1, keepdims=True)
        return r * (t - m1 - h * m2)

    row_ids = lax.broadcasted_iota(jnp.int32, (OWN, 1), 0)
    counted = jnp.where((row_ids < SHARE) | (m == 0), 1.0, 0.0).astype(F32)

    def ln_params(l, j, dy):
        dw = dy * counted
        n.sg[l, pl.ds(j, 1), :] = jnp.sum(dw * n.xh[l, j], axis=0, keepdims=True)
        n.sg[l, pl.ds(4 + j, 1), :] = jnp.sum(dw, axis=0, keepdims=True)

    def gather_rows(buf, own_rows):
        buf[share(m), :] = own_rows[:SHARE]
        buf[tail, :] = own_rows[SHARE:]
        copies = []
        for r in range(3):
            cp = rcopy(buf.at[share(m)], buf.at[share(m)], n.ag_s.at[r], n.ag_r.at[r], mp_dev(r))
            cp.start()
            copies.append(cp)
        return copies

    def scatter_copy(r):
        return rcopy(n.rsS.at[share(peers[r])], n.rsR.at[r], n.rs_s.at[r], n.rs_r.at[r], mp_dev(r))

    def tail_copy(turn, r):
        return rcopy(n.rsS.at[tail], n.rtR.at[turn, r], n.rt_s.at[turn, r], n.rt_r.at[turn, r], mp_dev(r))

    def send_part(r, part):
        n.rsS[share(peers[r]), :] = part.astype(BF)
        scatter_copy(r).start()

    def send_tail(turn, part):
        n.rsS[tail, :] = part.astype(BF)
        for r in range(3):
            tail_copy(turn, r).start()

    def keep_own(part):
        n.own[...] = part

    def reduced(turn):
        for r in range(3):
            tail_copy(turn, r).wait_recv()
        for r in range(3):
            scatter_copy(r).wait_recv()
        total = n.own[:SHARE, :]
        rest = n.own[SHARE:, :].astype(BF).astype(F32)
        for r in range(3):
            total = total + n.rsR[r].astype(F32)
            rest = rest + n.rtR[turn, r].astype(F32)
        for r in range(3):
            scatter_copy(r).wait_send()
            tail_copy(turn, r).wait_send()
        return jnp.concatenate([total, rest], axis=0)

    def pack_rows(v):
        return jnp.concatenate([v[:PACK], v[PACK:]], axis=1)

    def pad_lanes(v):
        return jnp.concatenate([v, jnp.zeros_like(v)], axis=1)

    def chunk_rows(j, size):
        return pl.ds(pl.multiple_of(j * size, size), size)

    def chunk_send(stage, dest, l, j, pos, size, ss, rs):
        dest[l, s, chunk_rows(j, size), :] = stage[s, chunk_rows(j, size), :]
        for k in range(3):
            rcopy(
                stage.at[zs[k], chunk_rows(j, size)], dest.at[l, s, chunk_rows(j, size)],
                ss.at[k, pos], rs.at[k, pos], z_dev(k),
            ).start()

    def tail_send(stage, dest, l, start, size, ss, rs):
        dest[l, s, pl.ds(start, size), :] = stage[s, pl.ds(start, size), :]
        for k in range(3):
            rcopy(
                stage.at[zs[k], pl.ds(start, size)], dest.at[l, s, pl.ds(start, size)],
                ss.at[k, 4], rs.at[k, 4], z_dev(k),
            ).start()

    def chunk_wait(stage, dest, l, size, start, tail_size, ss, rs):
        order = (m,) + peers
        for k in range(3):
            for pos in range(4):
                cp = rcopy(
                    stage.at[zs[k], chunk_rows(order[pos], size)], dest.at[l, s, chunk_rows(order[pos], size)],
                    ss.at[k, pos], rs.at[k, pos], z_dev(k),
                )
                cp.wait()
            rcopy(
                stage.at[zs[k], pl.ds(start, tail_size)], dest.at[l, s, pl.ds(start, tail_size)],
                ss.at[k, 4], rs.at[k, 4], z_dev(k),
            ).wait()

    def back_copy(stage, dest, l, k, pos, size, tail_size, ss, rs):
        if pos == 4:
            rows = pl.ds(MP_N * size, tail_size)
        else:
            rows = chunk_rows(m if pos == 0 else peers[pos - 1], size)
        return rcopy(stage.at[zs[k], rows], dest.at[l, s, rows], ss.at[k, pos], rs.at[k, pos], z_dev(k))

    BACK_ORDER = (3, 1, 2, 0, 4)

    def back_send(stage, dest, l, size, tail_size, ss, rs):
        for pos in BACK_ORDER:
            for k in range(3):
                back_copy(stage, dest, l, k, pos, size, tail_size, ss, rs).start()
        dest[l, s] = stage[s]

    def back_wait(stage, dest, l, pos, size, tail_size, ss, rs):
        for k in range(3):
            back_copy(stage, dest, l, k, pos, size, tail_size, ss, rs).wait()

    def side_by_side(pieces, low):
        return jnp.concatenate([g[:, :HD] if low else g[:, HD:] for g in pieces], axis=1)

    def g_parts(l, seg):
        if seg == "o":
            return n.gbo.at[l], n.rAo.at[l], n.rBo.at[l]
        return n.gbq, n.rAp, n.rBq

    def g_copy(phase, l, seg):
        at = SEG_AT[seg]
        start, count = SEG[seg]
        rows = pl.ds(start, count)
        full, got, part = g_parts(l, seg)
        if phase == 0:
            dev = core_dev
            if seg in "du" and l == 0:
                src, dst = n.gb0.at[1 - c, rows], n.rA0.at[rows]
            elif seg in "du":
                src, dst = n.gb1.at[1 - c, :, rows], n.rA1.at[:, rows]
            else:
                src, dst = full.at[1 - c], got
        elif phase <= 2:
            b = 1 - z1 if phase == 1 else z1
            src, dst, dev = full.at[c, 1 - z0, b], part.at[b], z_dev(0)
        else:
            dev = z_dev(1)
            if seg in "du":
                rows = pl.ds(start + 512 * (phase - 3), 512)
                src = n.gb1.at[c, 1 - z1, rows]
            else:
                src = full.at[c, z0, 1 - z1]
            dst = n.rC.at[l, rows]
        return rcopy(src, dst, n.g_s.at[l, phase, at], n.g_r.at[l, phase, at], dev)

    def f(phase, l, seg):
        g_copy(phase, l, seg).start()

    def add_to(ref, got):
        ref[...] = (ref[...].astype(F32) + got[...].astype(F32)).astype(BF)

    def a(phase, l, seg):
        g_copy(phase, l, seg).wait()
        start, count = SEG[seg]
        rows = pl.ds(start, count)
        full, got, part = g_parts(l, seg)
        if phase == 0 and seg in "du" and l == 0:
            n.ob[l, rows, :] = (n.gb0[c, rows, :].astype(F32) + n.rA0[rows, :].astype(F32)).astype(BF)
        elif phase == 0:
            for b in range(2):
                if seg in "du":
                    add_to(n.gb1.at[c, b, rows], n.rA1.at[b, rows])
                else:
                    for i in range(2):
                        add_to(full.at[c, i, b], got.at[i, b])
        elif phase <= 2:
            b = 1 - z1 if phase == 1 else z1
            add_to(full.at[c, z0, b], part.at[b])
        else:
            if seg in "du":
                g_copy(4, l, seg).wait()
                mine = n.gb1[c, z1, rows, :]
            else:
                mine = full[c, z0, z1]
            n.ob[l, rows, :] = (mine.astype(F32) + n.rC[l, rows, :].astype(F32)).astype(BF)

    def partner_copy(buf, pos, ss, rs):
        if pos == 4:
            src, dst = tail, pl.ds(ROWS + MP_N * SHARE, TAIL)
        else:
            j = m if pos == 0 else peers[pos - 1]
            src, dst = share(j), pl.ds(pl.multiple_of(ROWS + j * SHARE, TAIL), SHARE)
        return rcopy(buf.at[src], buf.at[dst], ss.at[pos], rs.at[pos], z_dev(0))

    def block_copies(buf, k, ss, rs):
        at = ROWS * (k + 1)
        return (
            rcopy(buf.at[share(m)], buf.at[pl.ds(pl.multiple_of(at + m * SHARE, TAIL), SHARE)], ss.at[k, 0], rs.at[k, 0], z_dev(k)),
            rcopy(buf.at[tail], buf.at[pl.ds(at + MP_N * SHARE, TAIL)], ss.at[k, 1], rs.at[k, 1], z_dev(k)),
        )

    def pass_copy(buf, k, r, ss, rs):
        at = ROWS * (k + 1)
        if r < 2:
            rows = pl.ds(pl.multiple_of(at + m * SHARE, TAIL), SHARE)
            dev = mp_dev(r)
        else:
            rows = pl.ds(pl.multiple_of(at + peers[r - 2] * SHARE + (r - 2) * (SHARE // 2), TAIL), SHARE // 2)
            dev = mp_dev(3 - r)
        return rcopy(buf.at[rows], buf.at[rows], ss.at[k, r], rs.at[k, r], dev)

    def block_send(buf, ss, rs, which=(0, 1, 2)):
        for k in which:
            for cp in block_copies(buf, k, ss, rs):
                cp.start()

    def block_pass(buf, zss, zrs, ss, rs, which=(0, 1, 2)):
        for k in which:
            for cp in block_copies(buf, k, zss, zrs):
                cp.wait()
            for r in range(2):
                pass_copy(buf, k, r, ss, rs).start()

    def block_pass_on(buf, ss, rs, which=(0, 1, 2)):
        for k in which:
            for r in range(2):
                pass_copy(buf, k, r, ss, rs).wait()
                pass_copy(buf, k, r + 2, ss, rs).start()

    def block_wait(buf, ss, rs, which=(0, 1, 2)):
        for k in which:
            for r in range(2, 4):
                pass_copy(buf, k, r, ss, rs).wait()

    def others_forward(l):
        for pos in range(5):
            partner_copy(hin[l], pos, n.hp_s.at[l], n.hp_r.at[l]).wait()
        if l == 0:
            block_wait(hin[0], n.hf_s, n.hf_r, (1, 2))
        for k in range(3 if l == 0 else 1):
            rows = pl.ds(ROWS * (k + 1), ROWS)
            value, slope = gelu_pair(dot(hin[l][rows, :], n.wu[l]) + n.bu[pl.ds(l, 1), :])
            act[l][rows, :] = value.astype(BF)
            n.gprP[pl.ds(ROWS * k, ROWS), :] = slope.astype(BF)

    def others_backward(l):
        if l == 1:
            for pos in range(5):
                partner_copy(dob[1], pos, n.dp_s, n.dp_r).wait()
        else:
            block_wait(dob[0], n.df_s, n.df_r)
        for k in range(3 if l == 0 else 1):
            rows = pl.ds(ROWS * (k + 1), ROWS)
            n.dlf[rows, :] = (dot(dob[l][rows, :], n.wd[l], 1, 1) * n.gprP[pl.ds(ROWS * k, ROWS), :].astype(F32)).astype(BF)

    def half_columns(ref):
        return jnp.concatenate([ref[:, pl.ds(pl.multiple_of(z0 * 256 + 512 * b, 256), 256)] for b in range(2)], axis=1)

    def own_columns(ref):
        return ref[:, pl.ds(pl.multiple_of(s * 256, 256), 256)]

    def grad_down(l):
        if l == 1:
            grad = dot(act[1][...], half_columns(dob[1]), 0, 0).astype(BF)
            for k in range(4):
                n.gb1[k % 2, k // 2, pl.ds(0, 1024), :] = grad[:, 128 * k:128 * k + 128]
        else:
            grad = dot(own_columns(dob[0]), act[0][...], 0, 0).T.astype(BF)
            for k in range(2):
                n.gb0[k, pl.ds(0, 1024), :] = grad[:, 128 * k:128 * k + 128]
        f(0, l, "d")

    def grad_up(l):
        if l == 1:
            grad = dot(half_columns(hin[1]), n.dlf[:2 * ROWS, :], 0, 0).astype(BF)
        else:
            grad = dot(own_columns(hin[0]), n.dlf[...], 0, 0).astype(BF)
        for k in range(4 if l == 1 else 2):
            for t in range(8):
                piece = grad[128 * k:128 * k + 128, 128 * t:128 * t + 128]
                if l == 1:
                    n.gb1[k % 2, k // 2, pl.ds(1024 + 128 * t, 128), :] = piece
                else:
                    n.gb0[k, pl.ds(1024 + 128 * t, 128), :] = piece
        f(0, l, "u")

    def head_core():
        return rcopy(n.gq.at[1 - c], n.rAq, n.gq_s.at[3], n.gq_r.at[3], core_dev)

    def head_copies():
        return [rcopy(n.gq.at[c, zs[k]], n.rQ.at[s], n.gq_s.at[k], n.gq_r.at[k], z_dev(k)) for k in range(3)]

    def head_grad():
        block_wait(n.nrm0, n.nf_s, n.nf_r)
        grad = dot(n.eq[...], n.nrm0[...], 0, 0).astype(BF)
        for k in range(8):
            n.gq[k % 2, k // 2] = grad[:, 128 * k:128 * k + 128]
        head_core().start()

    def head_grad_send():
        head_core().wait()
        for z in range(SEQ_N):
            add_to(n.gq.at[c, z], n.rAq.at[z])
        for cp in head_copies():
            cp.start()
        n.rQ[s] = n.gq[c, s]

    def head_grad_last():
        for cp in head_copies():
            cp.wait()
        for t in range(6):
            rows = pl.ds(HD * (t // 2), HD)
            both = jnp.concatenate([n.rQ[2 * (t % 2), rows, :], n.rQ[2 * (t % 2) + 1, rows, :]], axis=0)
            n.ob[0, pl.ds(2304 + 128 * t, 128), :] = both.astype(F32).T.astype(BF)

    def hook(l, at):
        for step in SCHEDULE.get((l, at), ()):
            (f if step[0] == "f" else a)(int(step[1]), int(step[2]), step[3])

    def g_out(l):
        return [
            pltpu.make_async_copy(
                n.ob.at[l, pl.ds(GPIECE * t, GPIECE)],
                n.out_o.at[pl.ds(OUT_GRADS + GPIECE * l, GPIECE), pl.ds(128 * t, 128)],
                n.out.at[l, t],
            )
            for t in range(8)
        ]

    text_count = n.tl[0]

    def gelu_pair(u):
        uu = u * u
        t = jnp.tanh(SQRT_2_PI * (u + 0.044715 * u * uu))
        half = 0.5 * (1.0 + t)
        slope = half + 0.5 * u * (1.0 - t * t) * (SQRT_2_PI * (1.0 + 3 * 0.044715 * uu))
        return u * half, slope

    order_rows = lambda own_value, pos, buf: own_value if pos == 0 else buf[share(peers[pos - 1]), :]

    def forward(l, first):
        own_rows = ln(n.cur[...], l, 0).astype(BF)
        if first:
            pl.semaphore_wait(barrier, len(everyone))
        copies = gather_rows(nrm[l], own_rows)
        if first:
            loads[2].wait()
        for pos in range(4):
            if pos > 0:
                copies[pos - 1].wait_recv()
            rows = order_rows(own_rows, pos, nrm[l])
            q = dot(rows, n.wq[l, 0]) + n.bqv[l, pl.ds(0, 1), :]
            k = dot(rows, n.wq[l, 1])
            v = dot(rows, n.wq[l, 2]) + n.bqv[l, pl.ds(1, 1), :]
            j = m if pos == 0 else peers[pos - 1]
            at = pl.multiple_of(j * BLK, BLK)
            for h in range(SEQ_N):
                cut = slice(HD * h, HD * h + HD)
                n.qs[h, pl.ds(at, SHARE), :] = jnp.concatenate([q[:SHARE, cut], k[:SHARE, cut]], axis=1).astype(BF)
                n.qs[h, pl.ds(at + SHARE, PACK), :] = pack_rows(v[:SHARE, cut]).astype(BF)
                if pos == 0:
                    n.qs[h, pl.ds(MP_N * BLK, TAIL), :] = jnp.concatenate([q[SHARE:, cut], k[SHARE:, cut]], axis=1).astype(BF)
                    n.qs[h, pl.ds(MP_N * BLK + TAIL, TAIL), :] = pad_lanes(v[SHARE:, cut]).astype(BF)
            chunk_send(n.qs, n.qkvA, l, j, pos, BLK, n.qk_s, n.qk_r)
            if pos == 0:
                tail_send(n.qs, n.qkvA, l, MP_N * BLK, 2 * TAIL, n.qk_s, n.qk_r)
        for cp in copies:
            cp.wait_send()
        if not first:
            block_pass(hin[0], n.hz_s, n.hz_r, n.hf_s, n.hf_r, (1, 2))
        chunk_wait(n.qs, n.qkvA, l, BLK, MP_N * BLK, 2 * TAIL, n.qk_s, n.qk_r)
        for zb in range(SEQ_N):
            for j in range(MP_N):
                both = n.qkvA[l, zb, pl.ds(BLK * j, SHARE), :]
                vals = n.qkvA[l, zb, pl.ds(BLK * j + SHARE, PACK), :]
                at = ROWS * zb + SHARE * j
                n.q_s[l, pl.ds(at, SHARE), :] = both[:, :HD]
                n.k_s[l, pl.ds(at, SHARE), :] = both[:, HD:]
                n.v_s[l, pl.ds(at, PACK), :] = vals[:, :HD]
                n.v_s[l, pl.ds(at + PACK, PACK), :] = vals[:, HD:]
            both = n.qkvA[l, zb, pl.ds(BLK * MP_N, TAIL), :]
            vals = n.qkvA[l, zb, pl.ds(BLK * MP_N + TAIL, TAIL), :]
            at = ROWS * zb + SHARE * MP_N
            n.q_s[l, pl.ds(at, TAIL), :] = both[:, :HD]
            n.k_s[l, pl.ds(at, TAIL), :] = both[:, HD:]
            n.v_s[l, pl.ds(at, TAIL), :] = vals[:, :HD]
        for i in range(SEQ_N):
            width = ROWS * (i + 1)
            st = dot(n.k_s[l, pl.ds(0, width), :], n.q_s[l, pl.ds(ROWS * i, ROWS), :], 1, 1) * SCORE_SCALE
            key_at = lax.broadcasted_iota(jnp.int32, (ROWS, ROWS), 0)
            query_at = lax.broadcasted_iota(jnp.int32, (ROWS, ROWS), 1)
            causal = key_at <= query_at
            if i == 0:
                st = jnp.where(causal & ((key_at >= TEXT) | (key_at < text_count)), st, -1e30)
            else:
                text_at = lax.broadcasted_iota(jnp.int32, (TEXT, ROWS), 0)
                st = jnp.concatenate([
                    jnp.where(text_at < text_count, st[:TEXT], -1e30),
                    st[TEXT:ROWS * i],
                    jnp.where(causal, st[ROWS * i:], -1e30),
                ], axis=0)
            e = jnp.exp(st - jnp.max(st, axis=0, keepdims=True))
            p = (e * (1.0 / jnp.sum(e, axis=0, keepdims=True))).astype(BF)
            pts[i][l] = p
            o = dot(n.v_s[l, pl.ds(0, width), :], p, 0, 0).T
            for j in range(MP_N):
                n.os_[i, pl.ds(PACK * j, PACK), :] = pack_rows(o[SHARE * j:SHARE * j + SHARE]).astype(BF)
            n.os_[i, pl.ds(PACK * MP_N, TAIL), :] = pad_lanes(o[SHARE * MP_N:]).astype(BF)
        back_send(n.os_, n.oA, l, PACK, TAIL, n.o_s, n.o_r)
        if not first:
            block_pass_on(hin[0], n.hf_s, n.hf_r, (1, 2))
        if first:
            loads[3].wait()
        for pos in BACK_ORDER[:4]:
            back_wait(n.os_, n.oA, l, pos, PACK, TAIL, n.o_s, n.o_r)
            j = m if pos == 0 else peers[pos - 1]
            got = [n.oA[l, h, chunk_rows(j, PACK), :] for h in range(SEQ_N)]
            rows = jnp.concatenate([side_by_side(got, True), side_by_side(got, False)], axis=0)
            n.att[l, share(j), :] = rows
            if pos > 0:
                send_part(pos - 1, dot(rows, n.wo[l]))
            else:
                back_wait(n.os_, n.oA, l, 4, PACK, TAIL, n.o_s, n.o_r)
                got = [n.oA[l, h, pl.ds(PACK * MP_N, TAIL), :] for h in range(SEQ_N)]
                rest = side_by_side(got, True)
                n.att[l, tail, :] = rest
                part = dot(jnp.concatenate([rows, rest], axis=0), n.wo[l])
                send_tail(0, part[SHARE:])
                keep_own(part)
        if not first:
            block_send(n.nrm0, n.nz_s, n.nz_r)
        branch = reduced(0) + n.bo[pl.ds(l, 1), :]
        settled = n.cur[...] + ln(branch, l, 1)
        n.stl[...] = settled
        own_rows = ln(settled, l, 2).astype(BF)
        copies = gather_rows(hin[l], own_rows)
        if first:
            block_send(hin[0], n.hz_s, n.hz_r, (1, 2))
        partner_copy(hin[l], 0, n.hp_s.at[l], n.hp_r.at[l]).start()
        partner_copy(hin[l], 4, n.hp_s.at[l], n.hp_r.at[l]).start()
        if first:
            loads[4].wait()
            loads[5].wait()
        for pos in range(4):
            if pos > 0:
                copies[pos - 1].wait_recv()
                partner_copy(hin[l], pos, n.hp_s.at[l], n.hp_r.at[l]).start()
            rows = order_rows(own_rows, pos, hin[l])
            value, slope = gelu_pair(dot(rows, n.wu[l]) + n.bu[pl.ds(l, 1), :])
            value = value.astype(BF)
            j = m if pos == 0 else peers[pos - 1]
            act[l][share(j), :] = value[:SHARE]
            n.gpr[l, share(j), :] = slope[:SHARE]
            part = dot(value, n.wd[l])
            if pos == 0:
                act[l][tail, :] = value[SHARE:]
                n.gpr[l, tail, :] = slope[SHARE:]
                send_tail(1, part[SHARE:])
                keep_own(part)
            else:
                send_part(pos - 1, part)
        for cp in copies:
            cp.wait_send()
        out_branch = reduced(1) + n.bd[pl.ds(l, 1), :]
        n.cur[...] = n.stl[...] + ln(out_branch, l, 3)

    def final_rows(which, stage, value):
        stage[...] = value.astype(BF)
        copies = []
        out = n.out_o.at[pl.ds(ROWS * which, ROWS)]
        for r in range(3):
            copies.append(rcopy(stage.at[pl.ds(0, SHARE)], out.at[share(m)], n.fr_s.at[which, r], n.fr_r.at[which, r], mp_dev(r)))
        copies.append(pltpu.make_async_copy(stage.at[pl.ds(0, SHARE)], out.at[share(m)], n.fl.at[which, 0]))
        copies.append(pltpu.make_async_copy(stage.at[pl.ds(SHARE, TAIL)], out.at[pl.ds(MP_N * SHARE, TAIL)], n.fl.at[which, 1]))
        for cp in copies:
            cp.start()
        return copies

    def backward(l):
        grad_rows = n.grd[...]
        d_ob = ln_back(l, 3, grad_rows).astype(BF)
        copies = gather_rows(dob[l], d_ob)
        if l == 1:
            partner_copy(dob[1], 0, n.dp_s, n.dp_r).start()
            partner_copy(dob[1], 4, n.dp_s, n.dp_r).start()
        else:
            block_send(dob[0], n.dz_s, n.dz_r)
        ln_params(l, 3, grad_rows)
        n.sg[l, pl.ds(9, 1), :] = jnp.sum(d_ob.astype(F32) * counted, axis=0, keepdims=True)
        hook(l, 0)
        for pos in range(4):
            if pos > 0:
                copies[pos - 1].wait_recv()
                if l == 1:
                    partner_copy(dob[1], pos, n.dp_s, n.dp_r).start()
            rows = order_rows(d_ob, pos, dob[l])
            j = m if pos == 0 else peers[pos - 1]
            slope = n.gpr[l, share(j), :]
            if pos == 0:
                slope = jnp.concatenate([slope, n.gpr[l, tail, :]], axis=0)
            d_l = (dot(rows, n.wd[l], 1, 1) * slope).astype(BF)
            n.dlf[share(j), :] = d_l[:SHARE]
            part = dot(d_l, n.wu[l], 1, 1)
            if pos == 0:
                n.dlf[tail, :] = d_l[SHARE:]
                send_tail(0, part[SHARE:])
                keep_own(part)
                if l == 1:
                    others_forward(1)
            else:
                send_part(pos - 1, part)
        for cp in copies:
            cp.wait_send()
        hook(l, 1)
        n.sg[l, pl.ds(10, 1), :] = jnp.sum(n.dlf[:ROWS, :].astype(F32), axis=0, keepdims=True)
        hook(l, 2)
        d_hidden = reduced(0)
        d_settled = grad_rows + ln_back(l, 2, d_hidden)
        d_br = ln_back(l, 1, d_settled).astype(BF)
        copies = gather_rows(n.dbr, d_br)
        n.stl[...] = d_settled
        ln_params(l, 2, d_hidden)
        ln_params(l, 1, d_settled)
        n.sg[l, pl.ds(8, 1), :] = jnp.sum(d_br.astype(F32) * counted, axis=0, keepdims=True)
        hook(l, 3)
        for pos in range(4):
            if pos > 0:
                copies[pos - 1].wait_recv()
            rows = order_rows(d_br, pos, n.dbr)
            j = m if pos == 0 else peers[pos - 1]
            d_at = dot(rows, n.wo[l], 1, 1)
            for h in range(SEQ_N):
                cut = slice(HD * h, HD * h + HD)
                n.ds_[h, chunk_rows(j, PACK), :] = pack_rows(d_at[:SHARE, cut]).astype(BF)
                if pos == 0:
                    n.ds_[h, pl.ds(MP_N * PACK, TAIL), :] = pad_lanes(d_at[SHARE:, cut]).astype(BF)
            chunk_send(n.ds_, n.dA, l, j, pos, PACK, n.do_ss, n.do_r)
            if pos == 0:
                tail_send(n.ds_, n.dA, l, MP_N * PACK, TAIL, n.do_ss, n.do_r)
                if l == 1:
                    others_backward(1)
                    grad_down(1)
                hook(l, 31)
        for cp in copies:
            cp.wait_send()
        hook(l, 4)
        if l == 1:
            grad_up(1)
            block_pass(n.nrm0, n.nz_s, n.nz_r, n.nf_s, n.nf_r)
        else:
            block_pass(dob[0], n.dz_s, n.dz_r, n.df_s, n.df_r)
        grad = dot(n.att[l], n.dbr[...], 0, 0).astype(BF)
        for k in range(8):
            n.gbo[l, k % 2, (k // 2) % 2, k // 4] = grad[:, 128 * k:128 * k + 128]
        f(0, l, "o")
        hook(l, 5)
        chunk_wait(n.ds_, n.dA, l, PACK, MP_N * PACK, TAIL, n.do_ss, n.do_r)
        for zb in range(SEQ_N):
            for j in range(MP_N):
                vals = n.dA[l, zb, pl.ds(PACK * j, PACK), :]
                at = ROWS * zb + SHARE * j
                n.do_s[pl.ds(at, PACK), :] = vals[:, :HD]
                n.do_s[pl.ds(at + PACK, PACK), :] = vals[:, HD:]
            n.do_s[pl.ds(ROWS * zb + SHARE * MP_N, TAIL), :] = n.dA[l, zb, pl.ds(PACK * MP_N, TAIL), :][:, :HD]
        hook(l, 6)
        for i in reversed(range(SEQ_N)):
            width = ROWS * (i + 1)
            here = pl.ds(ROWS * i, ROWS)
            p = pts[i][l]
            dpt = dot(n.v_s[l, pl.ds(0, width), :], n.do_s[here, :], 1, 1)
            pf = p.astype(F32)
            mean_term = jnp.sum(pf * dpt, axis=0, keepdims=True)
            dst = (pf * (dpt - mean_term)).astype(BF)
            dv = dot(p, n.do_s[here, :])
            dk = dot(dst, n.q_s[l, here, :])
            if i < SEQ_N - 1:
                dv = dv + n.dv_s[pl.ds(0, width), :]
                dk = dk + n.dk_s[pl.ds(0, width), :]
            if i > 0:
                n.dv_s[pl.ds(0, ROWS * i), :] = dv[:ROWS * i]
                n.dk_s[pl.ds(0, ROWS * i), :] = dk[:ROWS * i]
            dq = dot(n.k_s[l, pl.ds(0, width), :], dst, 0, 0).T * SCORE_SCALE
            dk = dk[ROWS * i:] * SCORE_SCALE
            dv = dv[ROWS * i:]
            if l == 0:
                place = (z0 if i % 2 == 0 else 1 - z0) + 2 * (z1 if i < 2 else 1 - z1)
                at = pl.ds(pl.multiple_of(place * ROWS, TAIL), ROWS)
                n.eq[at, pl.ds(0, 2 * HD)] = jnp.concatenate([dq, dk], axis=1).astype(BF)
                n.eq[at, pl.ds(2 * HD, HD)] = dv.astype(BF)
            for j in range(MP_N):
                cut = slice(SHARE * j, SHARE * j + SHARE)
                n.es[i, pl.ds(BLK * j, SHARE), :] = jnp.concatenate([dq[cut], dk[cut]], axis=1).astype(BF)
                n.es[i, pl.ds(BLK * j + SHARE, PACK), :] = pack_rows(dv[cut]).astype(BF)
            cut = slice(SHARE * MP_N, ROWS)
            n.es[i, pl.ds(BLK * MP_N, TAIL), :] = jnp.concatenate([dq[cut], dk[cut]], axis=1).astype(BF)
            n.es[i, pl.ds(BLK * MP_N + TAIL, TAIL), :] = pad_lanes(dv[cut]).astype(BF)
        back_send(n.es, n.eA, l, BLK, 2 * TAIL, n.e_s, n.e_r)
        hook(l, 7)
        if l == 1:
            others_forward(0)
            block_pass_on(n.nrm0, n.nf_s, n.nf_r)
        else:
            head_grad()
            block_pass_on(dob[0], n.df_s, n.df_r)

        def d_norm_part(rows):
            total = dot(rows[0], n.wq[l, 0], 1, 1)
            total = total + dot(rows[1], n.wq[l, 1], 1, 1)
            return total + dot(rows[2], n.wq[l, 2], 1, 1)

        for pos in BACK_ORDER[:4]:
            back_wait(n.es, n.eA, l, pos, BLK, 2 * TAIL, n.e_s, n.e_r)
            j = m if pos == 0 else peers[pos - 1]
            at = pl.multiple_of(j * BLK, BLK)
            both = [n.eA[l, h, pl.ds(at, SHARE), :] for h in range(SEQ_N)]
            vals = [n.eA[l, h, pl.ds(at + SHARE, PACK), :] for h in range(SEQ_N)]
            rows = [side_by_side(both, True), side_by_side(both, False)]
            rows.append(jnp.concatenate([side_by_side(vals, True), side_by_side(vals, False)], axis=0))
            for t in range(3):
                n.dpr[share(j), pl.ds(COLS * t, COLS)] = rows[t]
            if pos > 0:
                send_part(pos - 1, d_norm_part(rows))
            else:
                back_wait(n.es, n.eA, l, 4, BLK, 2 * TAIL, n.e_s, n.e_r)
                both = [n.eA[l, h, pl.ds(BLK * MP_N, TAIL), :] for h in range(SEQ_N)]
                vals = [n.eA[l, h, pl.ds(BLK * MP_N + TAIL, TAIL), :] for h in range(SEQ_N)]
                rest = [side_by_side(both, True), side_by_side(both, False), side_by_side(vals, True)]
                for t in range(3):
                    n.dpr[tail, pl.ds(COLS * t, COLS)] = rest[t]
                part = d_norm_part([jnp.concatenate([rows[t], rest[t]], axis=0) for t in range(3)])
                send_tail(1, part[SHARE:])
                keep_own(part)
        hook(l, 70)
        if l == 0:
            head_grad_send()
        if l == 1:
            grad = dot(nrm[l][...], n.dpr[...], 0, 0).astype(BF)
            for k in range(8):
                for t in range(6):
                    n.gbq[k % 2, (k // 2) % 2, k // 4, pl.ds(128 * t, 128), :] = grad[128 * k:128 * k + 128, 128 * t:128 * t + 128]
            f(0, l, "q")
        else:
            others_backward(0)
            grad_down(0)
            grad_up(0)
        sums = jnp.sum(n.dpr[...].astype(F32), axis=0, keepdims=True)
        blank = jnp.zeros((1, 96), F32)
        for at, lane in ((11, 0), (12, 2 * COLS)):
            pieces = []
            for k in range(8):
                pieces += [sums[:, lane + 32 * k:lane + 32 * k + 32], blank]
            n.sg[l, pl.ds(at, 1), :] = jnp.concatenate(pieces, axis=1)
        n.sg[l, pl.ds(13, 3), :] = jnp.zeros((3, D), F32)
        hook(l, 8)
        d_norm = reduced(1)
        n.grd[...] = n.stl[...] + ln_back(l, 0, d_norm)
        ln_params(l, 0, d_norm)
        hook(l, 9)

    forward(0, True)
    forward(1, False)
    result_copies = final_rows(0, n.resb, n.cur[...])
    loads[6].wait()
    loads[7].wait()
    backward(1)
    backward(0)
    grad_copies = final_rows(1, n.gstb, n.grd[...])

    small = []
    for t, dev in enumerate(group):
        lanes = pl.ds(pl.multiple_of((dev[0] * 2 + dev[1]) * 128, 128), 128)
        cp = rcopy(n.sg.at[:, :, lanes], n.smR.at[t], n.sm_s.at[t], n.sm_r.at[t], dev)
        cp.start()
        small.append(cp)
    hook(2, 0)
    head_grad_last()
    for cp in small:
        cp.wait()
    total = n.sg[:, :, pl.ds(pl.multiple_of((s * 2 + c) * 128, 128), 128)]
    for t in range(7):
        total = total + n.smR[t]
    n.smS[...] = total
    small = []
    for r in range(3):
        cp = rcopy(n.smS, n.smM.at[r], n.sn_s.at[r], n.sn_r.at[r], mp_dev(r))
        cp.start()
        small.append(cp)
    hook(2, 1)
    for cp in small:
        cp.wait()
    shared = lax.broadcasted_iota(jnp.int32, (2, SMALL, 128), 1) < 10
    total = total + jnp.where(shared, n.smM[0] + n.smM[1] + n.smM[2], 0.0)
    high = total.astype(BF)
    rest = (total - high.astype(F32)).astype(BF)
    n.sb[...] = jnp.zeros((16, D), BF)
    for l in range(2):
        n.sb[:, pl.ds(256 * l, 128)] = high[l]
        n.sb[:, pl.ds(256 * l + 128, 128)] = rest[l]
    last = [pltpu.make_async_copy(n.sb, n.out_o.at[pl.ds(OUT_SMALL, 16)], n.so.at[0])]
    last[0].start()
    hook(2, 2)
    for cp in g_out(0) + g_out(1):
        cp.start()
        last.append(cp)
    for cp in last + result_copies + grad_copies:
        cp.wait()


def finish_kernel(packed, res_o, gst_o, gain_o, shift_o, gq_o, qv_o, go_o, bo_o, gu_o, bu_o, gd_o, bd_o):
    res_o[...] = packed[:ROWS, :].astype(F32)
    gst_o[...] = packed[ROWS:2 * ROWS, :].astype(F32)
    for l in range(2):
        for b in range(24):
            lanes = slice(128 * (b // 3), 128 * (b // 3) + 128)
            start = OUT_GRADS + GPIECE * l + 128 * (b % 3)
            value = packed[start:start + 128, lanes].astype(F32)
            if b < 8:
                gd_o[l, 128 * b:128 * b + 128, :] = value
            elif b < 16:
                gu_o[l, :, 128 * (b - 8):128 * (b - 8) + 128] = value
            elif b < 18:
                go_o[l, 128 * (b - 16):128 * (b - 16) + 128, :] = value
            else:
                at = b - 18
                gq_o[l, at // 2, :, 128 * (at % 2):128 * (at % 2) + 128] = value
        small = packed[OUT_SMALL:OUT_SMALL + 16, 256 * l:256 * l + 128].astype(F32)
        small = small + packed[OUT_SMALL:OUT_SMALL + 16, 256 * l + 128:256 * l + 256].astype(F32)
        gain_o[l] = small[0:4]
        shift_o[l] = small[4:8]
        qv_o[l] = small[11:13, :32]
        bo_o[l:l + 1, :] = small[8:9]
        bd_o[l:l + 1, :] = small[9:10]
        bu_o[l:l + 1, :] = small[10:11]


def fused_shards(
    stream, text_len, norm_gain, norm_shift, w_qkv, bias_qv, w_out, bias_out, w_up, bias_up, w_down, bias_down, cotangent
):
    rows = (ROWS, D)
    any_space = pl.BlockSpec(memory_space=pl.ANY)
    vmem = pl.BlockSpec(memory_space=pltpu.VMEM)
    smem = pl.BlockSpec(memory_space=pltpu.SMEM)
    packed = pl.pallas_call(
        fused_kernel,
        out_shape=jax.ShapeDtypeStruct((OUT_ROWS, D), BF),
        in_specs=[smem, any_space, any_space, vmem, vmem, vmem, vmem, vmem, vmem] + [any_space] * 4,
        out_specs=any_space,
        scratch_shapes=[pltpu.VMEM(shape, dtype) for shape, dtype in VMEM_SCRATCH.values()]
        + [pltpu.SemaphoreType.DMA(shape) for shape in DMA_SEMS.values()],
        compiler_params=pltpu.CompilerParams(
            collective_id=0, has_side_effects=True, vmem_limit_bytes=63 * 2**20
        ),
    )(
        text_len,
        stream.reshape(rows),
        cotangent.reshape(rows),
        norm_gain,
        norm_shift,
        bias_qv,
        bias_out,
        bias_up,
        bias_down,
        w_qkv.transpose(0, 2, 1, 3),
        w_out,
        w_up,
        w_down,
    )
    shape = lambda *dims: jax.ShapeDtypeStruct(dims, F32)
    done = pl.pallas_call(
        finish_kernel,
        out_shape=(
            shape(*rows), shape(*rows), shape(2, 4, 128), shape(2, 4, 128), shape(2, 3, 128, COLS), shape(2, 2, 32),
            shape(2, COLS, 128), shape(2, 128), shape(2, 128, FFL), shape(2, 128), shape(2, FFL, 128), shape(2, 128),
        ),
        in_specs=[vmem],
        out_specs=[vmem] * 12,
        compiler_params=pltpu.CompilerParams(vmem_limit_bytes=32 * 2**20),
    )(packed)
    return (
        done[0].reshape(1, ROWS, D),
        done[1].reshape(1, ROWS, D),
        done[2],
        done[3],
        done[4].transpose(0, 2, 1, 3),
    ) + tuple(done[5:])


def solution(mesh):
    return jax.shard_map(
        fused_shards if fits(mesh) else shards,
        mesh=mesh,
        in_specs=(
            P("dp", "seq", None),
            P("dp"),
            P(),
            P(),
            P(None, None, None, "mp"),
            P(None, None, "mp"),
            P(None, "mp", None),
            P(),
            P(None, None, "mp"),
            P(None, "mp"),
            P(None, "mp", None),
            P(),
            P("dp", "seq", None),
        ),
        out_specs=(
            P("dp", "seq", None),
            P("dp", "seq", None),
            P(None, None, ("seq", "dp")),
            P(None, None, ("seq", "dp")),
            P(None, ("seq", "dp"), None, "mp"),
            P(None, None, ("mp", "seq", "dp")),
            P(None, "mp", ("seq", "dp")),
            P(None, ("seq", "dp")),
            P(None, ("seq", "dp"), "mp"),
            P(None, ("mp", "seq", "dp")),
            P(None, "mp", ("seq", "dp")),
            P(None, ("seq", "dp")),
        ),
        check_vma=False,
    )
```

```python
from functools import partial
import math

import jax
import jax.numpy as jnp
from jax import lax
from jax.experimental import pallas as pl
from jax.experimental.pallas import tpu as pltpu
from jax.sharding import PartitionSpec as P

D = 1024
HEADS = 16
TEXT = 64


relax_alpha = 32.0
norm_eps = 1e-05


def layer_norm(row_values, gain_row, shift_row):
    row_mean = jnp.mean(row_values, axis=-1, keepdims=True)
    centred = row_values - row_mean
    variance = jnp.mean(centred * centred, axis=-1, keepdims=True)
    return centred * lax.rsqrt(variance + norm_eps) * gain_row + shift_row


def norm_back(row_values, gain_row, shift_row, grad_rows):
    result_value, pull_back = jax.vjp(layer_norm, row_values, gain_row, shift_row)
    return pull_back(grad_rows)


def reduce_rows(partial_sum):
    return lax.psum_scatter(
        partial_sum.astype(jnp.bfloat16), "mp", scatter_dimension=0, tiled=True
    ).astype(jnp.float32)


def widen_rows(row_values):
    return lax.all_gather(row_values, "mp", axis=0, tiled=True)


def reduce_grads(partial_sum):
    return lax.psum_scatter(
        partial_sum.astype(jnp.bfloat16), "mp", scatter_dimension=0, tiled=True
    ).astype(jnp.float32)


def widen_grads(row_values):
    return lax.all_gather(row_values, "mp", axis=0, tiled=True)


def relaxed_scores(query_heads, key_heads, allowed, score_scale):
    raw_scores = (
        jnp.einsum("sqhe,skhe->shqk", query_heads, key_heads, preferred_element_type=jnp.float32)
        * score_scale
    )
    return jnp.where(allowed, raw_scores / relax_alpha, -1e30)


def shards(
    stream,
    text_len,
    norm_gain,
    norm_shift,
    w_qkv,
    bias_qv,
    w_out,
    bias_out,
    w_up,
    bias_up,
    w_down,
    bias_down,
    cotangent,
):
    seq_count, block_len, model_width = stream.shape
    rows_all = seq_count * block_len
    layers = w_qkv.shape[0]
    local_cols = w_qkv.shape[3]
    head_dim = D // HEADS
    heads_here = local_cols // head_dim
    score_scale = 1.0 / math.sqrt(head_dim)
    share_rows = rows_all // lax.axis_size("mp")
    first_row = lax.axis_index("mp") * share_rows
    block_start = lax.axis_index("seq") * block_len
    seq_span = block_len * lax.axis_size("seq")
    query_pos = block_start + jnp.arange(block_len, dtype=jnp.int32)
    key_pos = jnp.arange(seq_span, dtype=jnp.int32)
    causal = key_pos[None, :] <= query_pos[:, None]
    visible = (key_pos[None, :] >= TEXT) | (key_pos[None, :] < text_len[:, None])
    allowed = causal[None, None] & visible[:, None, None, :]
    flat_rows = stream.reshape(rows_all, model_width)
    grad_rows = cotangent.reshape(rows_all, model_width)
    current = lax.dynamic_slice_in_dim(flat_rows, first_row, share_rows, 0)
    grad_rows = lax.dynamic_slice_in_dim(grad_rows, first_row, share_rows, 0)
    gelu_tanh = partial(jax.nn.gelu, approximate=True)
    kept_state = []
    for layer_at in range(layers):
        gain_rows = norm_gain[layer_at]
        shift_rows = norm_shift[layer_at]
        normed = widen_rows(layer_norm(current, gain_rows[0], shift_rows[0]).astype(jnp.bfloat16))
        projected = jnp.einsum(
            "td,dcf->tcf", normed, w_qkv[layer_at], preferred_element_type=jnp.float32
        )
        queries = (projected[:, 0] + bias_qv[layer_at, 0]).astype(jnp.bfloat16)
        key_rows = projected[:, 1].astype(jnp.bfloat16)
        value_rows = (projected[:, 2] + bias_qv[layer_at, 1]).astype(jnp.bfloat16)
        keys_all, values_all = (
            lax.all_gather(
                key_rows.reshape(seq_count, block_len, local_cols), "seq", axis=1, tiled=True
            ),
            lax.all_gather(
                value_rows.reshape(seq_count, block_len, local_cols), "seq", axis=1, tiled=True
            ),
        )
        query_heads = queries.reshape(seq_count, block_len, heads_here, head_dim)
        key_heads = keys_all.reshape(seq_count, seq_span, heads_here, head_dim)
        value_heads = values_all.reshape(seq_count, seq_span, heads_here, head_dim)
        tempered = relaxed_scores(query_heads, key_heads, allowed, score_scale)
        highest = jnp.max(tempered, axis=-1, keepdims=True)
        exponent = jnp.exp(relax_alpha * (tempered - highest))
        totals = jnp.sum(exponent, axis=-1, keepdims=True)
        log_total = relax_alpha * highest + jnp.log(totals)
        weights = (exponent / totals).astype(jnp.bfloat16)
        attended = jnp.einsum(
            "shqk,skhe->sqhe", weights, value_heads, preferred_element_type=jnp.float32
        )
        attended = attended.astype(jnp.bfloat16).reshape(rows_all, local_cols)
        branch = (
            reduce_rows(jnp.dot(attended, w_out[layer_at], preferred_element_type=jnp.float32))
            + bias_out[layer_at]
        )
        settled = current + layer_norm(branch, gain_rows[1], shift_rows[1])
        hidden_in = widen_rows(
            layer_norm(settled, gain_rows[2], shift_rows[2]).astype(jnp.bfloat16)
        )
        lifted = (
            jnp.dot(hidden_in, w_up[layer_at], preferred_element_type=jnp.float32)
            + bias_up[layer_at]
        )
        activated = gelu_tanh(lifted).astype(jnp.bfloat16)
        output_branch = (
            reduce_rows(jnp.dot(activated, w_down[layer_at], preferred_element_type=jnp.float32))
            + bias_down[layer_at]
        )
        kept_state.append(
            (
                current,
                normed,
                query_heads,
                key_heads,
                value_heads,
                log_total,
                attended,
                branch,
                settled,
                hidden_in,
                lifted,
                activated,
                output_branch,
            )
        )
        current = settled + layer_norm(output_branch, gain_rows[3], shift_rows[3])
    collected = []
    for layer_at in reversed(range(layers)):
        (
            layer_in,
            normed,
            query_heads,
            key_heads,
            value_heads,
            log_total,
            attended,
            branch,
            settled,
            hidden_in,
            lifted,
            activated,
            output_branch,
        ) = kept_state[layer_at]
        gain_rows = norm_gain[layer_at]
        shift_rows = norm_shift[layer_at]
        d_out_branch, gain_three, shift_three = norm_back(
            output_branch, gain_rows[3], shift_rows[3], grad_rows
        )
        d_out_branch = d_out_branch.astype(jnp.bfloat16)
        d_bias_down = jnp.sum(d_out_branch.astype(jnp.float32), axis=0)
        d_down_full = widen_grads(d_out_branch)
        d_w_down = jnp.einsum(
            "tf,td->fd", activated, d_down_full, preferred_element_type=jnp.float32
        )
        d_activated = jnp.einsum(
            "td,fd->tf", d_down_full, w_down[layer_at], preferred_element_type=jnp.float32
        )
        gelu_value, gelu_pull = jax.vjp(gelu_tanh, lifted)
        d_lifted = gelu_pull(d_activated)[0].astype(jnp.bfloat16)
        d_bias_up = jnp.sum(d_lifted.astype(jnp.float32), axis=0)
        d_w_up = jnp.einsum("td,tf->df", hidden_in, d_lifted, preferred_element_type=jnp.float32)
        d_hidden = reduce_grads(
            jnp.einsum("tf,df->td", d_lifted, w_up[layer_at], preferred_element_type=jnp.float32)
        )
        d_norm_two, gain_two, shift_two = norm_back(settled, gain_rows[2], shift_rows[2], d_hidden)
        d_settled = grad_rows + d_norm_two
        d_branch, gain_one, shift_one = norm_back(branch, gain_rows[1], shift_rows[1], d_settled)
        d_branch = d_branch.astype(jnp.bfloat16)
        d_bias_out = jnp.sum(d_branch.astype(jnp.float32), axis=0)
        d_branch_full = widen_grads(d_branch)
        d_w_out = jnp.einsum(
            "tf,td->fd", attended, d_branch_full, preferred_element_type=jnp.float32
        )
        d_attended = jnp.einsum(
            "td,fd->tf", d_branch_full, w_out[layer_at], preferred_element_type=jnp.float32
        )
        d_attended = d_attended.astype(jnp.bfloat16).reshape(
            seq_count, block_len, heads_here, head_dim
        )
        tempered = relaxed_scores(query_heads, key_heads, allowed, score_scale)
        probabilities = jnp.exp(relax_alpha * tempered - log_total)
        d_probs = jnp.einsum(
            "sqhe,skhe->shqk", d_attended, value_heads, preferred_element_type=jnp.float32
        )
        d_values = jnp.einsum(
            "shqk,sqhe->skhe",
            probabilities.astype(jnp.bfloat16),
            d_attended,
            preferred_element_type=jnp.float32,
        )
        mean_term = jnp.sum(probabilities * d_probs, axis=-1, keepdims=True)
        d_raw = (probabilities * (d_probs - mean_term)).astype(jnp.bfloat16)
        d_queries = (
            jnp.einsum("shqk,skhe->sqhe", d_raw, key_heads, preferred_element_type=jnp.float32)
            * score_scale
        )
        d_keys = (
            jnp.einsum("shqk,sqhe->skhe", d_raw, query_heads, preferred_element_type=jnp.float32)
            * score_scale
        )
        d_keys_own, d_values_own = (
            lax.psum_scatter(
                d_keys.reshape(seq_count, seq_span, local_cols).astype(jnp.bfloat16),
                "seq",
                scatter_dimension=1,
                tiled=True,
            ).astype(jnp.float32),
            lax.psum_scatter(
                d_values.reshape(seq_count, seq_span, local_cols).astype(jnp.bfloat16),
                "seq",
                scatter_dimension=1,
                tiled=True,
            ).astype(jnp.float32),
        )
        d_queries = d_queries.reshape(rows_all, local_cols).astype(jnp.bfloat16)
        d_keys_own = d_keys_own.reshape(rows_all, local_cols).astype(jnp.bfloat16)
        d_values_own = d_values_own.reshape(rows_all, local_cols).astype(jnp.bfloat16)
        d_bias_qv = jnp.stack(
            [
                jnp.sum(d_queries.astype(jnp.float32), axis=0),
                jnp.sum(d_values_own.astype(jnp.float32), axis=0),
            ]
        )
        d_projected = jnp.stack([d_queries, d_keys_own, d_values_own], axis=1)
        d_w_qkv = jnp.einsum("td,tcf->dcf", normed, d_projected, preferred_element_type=jnp.float32)
        d_normed = reduce_grads(
            jnp.einsum(
                "tcf,dcf->td", d_projected, w_qkv[layer_at], preferred_element_type=jnp.float32
            )
        )
        d_layer_in, gain_zero, shift_zero = norm_back(
            layer_in, gain_rows[0], shift_rows[0], d_normed
        )
        grad_rows = d_settled + d_layer_in
        collected.append(
            (
                jnp.stack([gain_zero, gain_one, gain_two, gain_three]),
                jnp.stack([shift_zero, shift_one, shift_two, shift_three]),
                d_w_qkv,
                d_bias_qv,
                d_w_out,
                d_bias_out,
                d_w_up,
                d_bias_up,
                d_w_down,
                d_bias_down,
            )
        )
    collected = collected[::-1]
    stacked = tuple((jnp.stack([entry[index_at] for entry in collected]) for index_at in range(10)))
    (
        gain_grads,
        shift_grads,
        grad_qkv,
        grad_qv,
        grad_out_w,
        grad_out_b,
        grad_up_w,
        grad_up_b,
        grad_down_w,
        grad_down_b,
    ) = stacked
    gain_grads, shift_grads, grad_out_b, grad_down_b = (
        lax.psum(gain_grads.astype(jnp.bfloat16), "mp").astype(jnp.float32),
        lax.psum(shift_grads.astype(jnp.bfloat16), "mp").astype(jnp.float32),
        lax.psum(grad_out_b.astype(jnp.bfloat16), "mp").astype(jnp.float32),
        lax.psum(grad_down_b.astype(jnp.bfloat16), "mp").astype(jnp.float32),
    )
    current, grad_rows = (
        lax.all_gather(current.astype(jnp.bfloat16), "mp", axis=0, tiled=True).astype(
            current.dtype
        ),
        lax.all_gather(grad_rows.astype(jnp.bfloat16), "mp", axis=0, tiled=True).astype(
            grad_rows.dtype
        ),
    )
    summed = (
        lax.psum_scatter(
            gain_grads.astype(jnp.bfloat16), ("seq", "dp"), scatter_dimension=2, tiled=True
        ).astype(jnp.float32),
        lax.psum_scatter(
            shift_grads.astype(jnp.bfloat16), ("seq", "dp"), scatter_dimension=2, tiled=True
        ).astype(jnp.float32),
        lax.psum_scatter(
            grad_qkv.astype(jnp.bfloat16), ("seq", "dp"), scatter_dimension=1, tiled=True
        ).astype(jnp.float32),
        lax.psum_scatter(
            grad_qv.astype(jnp.bfloat16), ("seq", "dp"), scatter_dimension=2, tiled=True
        ).astype(jnp.float32),
        lax.psum_scatter(
            grad_out_w.astype(jnp.bfloat16), ("seq", "dp"), scatter_dimension=2, tiled=True
        ).astype(jnp.float32),
        lax.psum_scatter(
            grad_out_b.astype(jnp.bfloat16), ("seq", "dp"), scatter_dimension=1, tiled=True
        ).astype(jnp.float32),
        lax.psum_scatter(
            grad_up_w.astype(jnp.bfloat16), ("seq", "dp"), scatter_dimension=1, tiled=True
        ).astype(jnp.float32),
        lax.psum_scatter(
            grad_up_b.astype(jnp.bfloat16), ("seq", "dp"), scatter_dimension=1, tiled=True
        ).astype(jnp.float32),
        lax.psum_scatter(
            grad_down_w.astype(jnp.bfloat16), ("seq", "dp"), scatter_dimension=2, tiled=True
        ).astype(jnp.float32),
        lax.psum_scatter(
            grad_down_b.astype(jnp.bfloat16), ("seq", "dp"), scatter_dimension=1, tiled=True
        ).astype(jnp.float32),
    )
    result = current.reshape(seq_count, block_len, model_width)
    grad_stream = grad_rows.reshape(seq_count, block_len, model_width)
    return (
        result,
        grad_stream,
        summed[0],
        summed[1],
        summed[2],
        summed[3],
        summed[4],
        summed[5],
        summed[6],
        summed[7],
        summed[8],
        summed[9],
    )


MESH = pl.DeviceIdType.MESH
BF = jnp.bfloat16
F32 = jnp.float32

SEQ_N, DP_N, MP_N = 4, 2, 4
ROWS = 272
SHARE = 64
TAIL = 16
OWN = SHARE + TAIL
HD = 64
COLS = 256
FFL = 1024
PACK = 32
BLK = SHARE + PACK
QKV_ROWS = MP_N * BLK + 2 * TAIL
VP_ROWS = MP_N * PACK + TAIL
SEG = {"d": (0, 1024), "u": (1024, 1024), "o": (2048, 256), "q": (2304, 768)}
SEG_AT = {"d": 0, "u": 1, "o": 2, "q": 3}
GROWS = 3072
GPIECE = GROWS // 8
OUT_GRADS = 2 * ROWS
OUT_SMALL = OUT_GRADS + 2 * GPIECE
OUT_ROWS = OUT_SMALL + 16
SMALL = 16
SQRT_2_PI = math.sqrt(2.0 / math.pi)
SCORE_SCALE = 0.125


def dot(a, b, ca=1, cb=0):
    return lax.dot_general(a, b, (((ca,), (cb,)), ((), ())), preferred_element_type=F32)


def fits(mesh):
    return dict(mesh.shape) == {"seq": SEQ_N, "dp": DP_N, "mp": MP_N}


VMEM_SCRATCH = {
    "wq": ((2, 3, D, COLS), BF),
    "wo": ((2, COLS, D), BF),
    "wu": ((2, D, FFL), BF),
    "wd": ((2, FFL, D), BF),
    "cur": ((OWN, D), F32),
    "grd": ((OWN, D), F32),
    "stl": ((OWN, D), F32),
    "own": ((OWN, D), F32),
    "xh": ((2, 4, OWN, D), F32),
    "rstd": ((2, 4, OWN, 128), F32),
    "nrm0": ((4 * ROWS, D), BF),
    "nrm1": ((ROWS, D), BF),
    "hin0": ((4 * ROWS, D), BF),
    "hin1": ((2 * ROWS, D), BF),
    "act0": ((4 * ROWS, FFL), BF),
    "act1": ((2 * ROWS, FFL), BF),
    "gpr": ((2, ROWS, FFL), F32),
    "gprP": ((3 * ROWS, FFL), BF),
    "dob0": ((4 * ROWS, D), BF),
    "dbr": ((ROWS, D), BF),
    "dlf": ((4 * ROWS, FFL), BF),
    "att": ((2, ROWS, COLS), BF),
    "dpr": ((ROWS, 3 * COLS), BF),
    "qkvA": ((2, SEQ_N, QKV_ROWS, 128), BF),
    "q_s": ((2, SEQ_N * ROWS, HD), BF),
    "k_s": ((2, SEQ_N * ROWS, HD), BF),
    "v_s": ((2, SEQ_N * ROWS, HD), BF),
    "do_s": ((SEQ_N * ROWS, HD), BF),
    "dk_s": ((SEQ_N * ROWS, HD), F32),
    "dv_s": ((SEQ_N * ROWS, HD), F32),
    "pt0": ((2, ROWS, ROWS), BF),
    "pt1": ((2, 2 * ROWS, ROWS), BF),
    "pt2": ((2, 3 * ROWS, ROWS), BF),
    "pt3": ((2, 4 * ROWS, ROWS), BF),
    "oA": ((2, SEQ_N, VP_ROWS, 128), BF),
    "dA": ((2, SEQ_N, VP_ROWS, 128), BF),
    "eA": ((2, SEQ_N, QKV_ROWS, 128), BF),
    "qs": ((SEQ_N, QKV_ROWS, 128), BF),
    "os_": ((SEQ_N, VP_ROWS, 128), BF),
    "ds_": ((SEQ_N, VP_ROWS, 128), BF),
    "es": ((SEQ_N, QKV_ROWS, 128), BF),
    "rsS": ((ROWS, D), BF),
    "rsR": ((3, SHARE, D), BF),
    "rtR": ((2, 3, TAIL, D), BF),
    "eq": ((4 * ROWS, 3 * HD), BF),
    "gq": ((2, SEQ_N, 3 * HD, 128), BF),
    "rAq": ((SEQ_N, 3 * HD, 128), BF),
    "rQ": ((SEQ_N, 3 * HD, 128), BF),
    "gb0": ((2, 2048, 128), BF),
    "gb1": ((2, 2, 2048, 128), BF),
    "rA0": ((2048, 128), BF),
    "gbo": ((2, 2, 2, 2, 256, 128), BF),
    "gbq": ((2, 2, 2, 768, 128), BF),
    "rA1": ((2, 2048, 128), BF),
    "rAo": ((2, 2, 2, 256, 128), BF),
    "rAp": ((2, 2, 768, 128), BF),
    "rBo": ((2, 2, 256, 128), BF),
    "rBq": ((2, 768, 128), BF),
    "rC": ((2, GROWS, 128), BF),
    "ob": ((2, GROWS, 128), BF),
    "sb": ((16, D), BF),
    "sg": ((2, SMALL, D), F32),
    "smR": ((7, 2, SMALL, 128), F32),
    "smS": ((2, SMALL, 128), F32),
    "smM": ((3, 2, SMALL, 128), F32),
    "resb": ((OWN, D), BF),
    "gstb": ((OWN, D), BF),
}
DMA_SEMS = {
    "ld": (16,),
    "ag_s": (3,), "ag_r": (3,),
    "rs_s": (3,), "rs_r": (3,),
    "rt_s": (2, 3), "rt_r": (2, 3),
    "qk_s": (3, 5), "qk_r": (3, 5),
    "do_ss": (3, 5), "do_r": (3, 5),
    "o_s": (3, 5), "o_r": (3, 5),
    "e_s": (3, 5), "e_r": (3, 5),
    "g_s": (2, 5, 4), "g_r": (2, 5, 4),
    "hp_s": (2, 5), "hp_r": (2, 5), "dp_s": (5,), "dp_r": (5,),
    "nz_s": (3, 2), "nz_r": (3, 2), "nf_s": (3, 4), "nf_r": (3, 4),
    "gq_s": (4,), "gq_r": (4,),
    "hz_s": (3, 2), "hz_r": (3, 2), "dz_s": (3, 2), "dz_r": (3, 2),
    "hf_s": (3, 4), "hf_r": (3, 4), "df_s": (3, 4), "df_r": (3, 4),
    "out": (2, 8), "so": (1,),
    "fr_s": (2, 3), "fr_r": (2, 3), "fr_t": (2, 3), "fr_u": (2, 3),
    "fl": (2, 2),
    "sm_s": (7,), "sm_r": (7,), "sn_s": (3,), "sn_r": (3,),
}
SCHEDULE = {
    (1, 7): ("a01d", "f31d", "f41d", "a01u",),
    (1, 70): ("f31u", "f41u",),
    (1, 8): ("a01o", "f11o", "f21o",),
    (1, 9): ("a01q", "f11q", "f21q",),
    (0, 2): ("a11o", "f31o", "a11q", "f31q", "a21o", "a21q",),
    (0, 7): ("a31d", "a31u", "a00o", "f10o", "f20o",),
    (0, 8): ("a10o", "f30o", "a20o",),
    (0, 9): ("a31o", "a31q", "a00d", "a00u",),
    (2, 1): ("a30o",),
}
IN_NAMES = ("tl", "stream", "cot", "gain", "shift", "bqv", "bo", "bu", "bd", "wq_h", "wo_h", "wu_h", "wd_h")
OUT_NAMES = ("out_o",)


class Refs:
    pass


def fused_kernel(*all_refs):
    n = Refs()
    names = IN_NAMES + OUT_NAMES + tuple(VMEM_SCRATCH) + tuple(DMA_SEMS)
    for name, ref in zip(names, all_refs):
        setattr(n, name, ref)
    pts = (n.pt0, n.pt1, n.pt2, n.pt3)
    hin, act, dob = (n.hin0, n.hin1), (n.act0, n.act1), (n.dob0, n.dob0.at[pl.ds(0, 2 * ROWS)])
    nrm = (n.nrm0, n.nrm1)

    s = lax.axis_index("seq")
    c = lax.axis_index("dp")
    m = lax.axis_index("mp")
    mx, my = lax.rem(m, 2), lax.div(m, 2)
    peers = (my * 2 + (1 - mx), (1 - my) * 2 + mx, (1 - my) * 2 + (1 - mx))
    z0, z1 = lax.rem(s, 2), lax.div(s, 2)
    zs = (z1 * 2 + (1 - z0), (1 - z1) * 2 + z0, (1 - z1) * 2 + (1 - z0))

    def mp_dev(r):
        return (s, c, peers[r])

    def z_dev(k):
        return (zs[k], c, m)

    core_dev = (s, 1 - c, m)
    group = [core_dev] + [z_dev(k) for k in range(3)] + [(zs[k], 1 - c, m) for k in range(3)]

    barrier = pltpu.get_barrier_semaphore()
    everyone = group + [mp_dev(r) for r in range(3)]
    for dev in everyone:
        pl.semaphore_signal(barrier, inc=1, device_id=dev, device_id_type=MESH)

    loads = [
        pltpu.make_async_copy(n.stream.at[pl.ds(pl.multiple_of(m * SHARE, SHARE), SHARE)], n.cur.at[pl.ds(0, SHARE)], n.ld.at[0]),
        pltpu.make_async_copy(n.stream.at[pl.ds(MP_N * SHARE, TAIL)], n.cur.at[pl.ds(SHARE, TAIL)], n.ld.at[1]),
        pltpu.make_async_copy(n.wq_h, n.wq, n.ld.at[2]),
        pltpu.make_async_copy(n.wo_h, n.wo, n.ld.at[3]),
        pltpu.make_async_copy(n.wu_h, n.wu, n.ld.at[4]),
        pltpu.make_async_copy(n.wd_h, n.wd, n.ld.at[5]),
        pltpu.make_async_copy(n.cot.at[pl.ds(pl.multiple_of(m * SHARE, SHARE), SHARE)], n.grd.at[pl.ds(0, SHARE)], n.ld.at[6]),
        pltpu.make_async_copy(n.cot.at[pl.ds(MP_N * SHARE, TAIL)], n.grd.at[pl.ds(SHARE, TAIL)], n.ld.at[7]),
    ]
    for cp in loads:
        cp.start()
    loads[0].wait()
    loads[1].wait()

    def rcopy(src, dst, ss, rs, dev):
        return pltpu.make_async_remote_copy(
            src_ref=src, dst_ref=dst, send_sem=ss, recv_sem=rs, device_id=dev, device_id_type=MESH
        )

    def share(j):
        return pl.ds(pl.multiple_of(j * SHARE, SHARE), SHARE)

    tail = pl.ds(MP_N * SHARE, TAIL)

    def ln(v, l, j):
        ce = v - jnp.mean(v, axis=-1, keepdims=True)
        r = lax.rsqrt(jnp.mean(ce * ce, axis=-1, keepdims=True) + norm_eps)
        h = ce * r
        n.xh[l, j] = h
        n.rstd[l, j] = jnp.broadcast_to(r, (OWN, 128))
        return h * n.gain[l, pl.ds(j, 1), :] + n.shift[l, pl.ds(j, 1), :]

    def ln_back(l, j, dy):
        h = n.xh[l, j]
        r = n.rstd[l, j][:, :1]
        t = dy * n.gain[l, pl.ds(j, 1), :]
        m1 = jnp.mean(t, axis=-1, keepdims=True)
        m2 = jnp.mean(t * h, axis=-1, keepdims=True)
        return r * (t - m1 - h * m2)

    row_ids = lax.broadcasted_iota(jnp.int32, (OWN, 1), 0)
    counted = jnp.where((row_ids < SHARE) | (m == 0), 1.0, 0.0).astype(F32)

    def ln_params(l, j, dy):
        dw = dy * counted
        n.sg[l, pl.ds(j, 1), :] = jnp.sum(dw * n.xh[l, j], axis=0, keepdims=True)
        n.sg[l, pl.ds(4 + j, 1), :] = jnp.sum(dw, axis=0, keepdims=True)

    def gather_rows(buf, own_rows):
        buf[share(m), :] = own_rows[:SHARE]
        buf[tail, :] = own_rows[SHARE:]
        copies = []
        for r in range(3):
            cp = rcopy(buf.at[share(m)], buf.at[share(m)], n.ag_s.at[r], n.ag_r.at[r], mp_dev(r))
            cp.start()
            copies.append(cp)
        return copies

    def scatter_copy(r):
        return rcopy(n.rsS.at[share(peers[r])], n.rsR.at[r], n.rs_s.at[r], n.rs_r.at[r], mp_dev(r))

    def tail_copy(turn, r):
        return rcopy(n.rsS.at[tail], n.rtR.at[turn, r], n.rt_s.at[turn, r], n.rt_r.at[turn, r], mp_dev(r))

    def send_part(r, part):
        n.rsS[share(peers[r]), :] = part.astype(BF)
        scatter_copy(r).start()

    def send_tail(turn, part):
        n.rsS[tail, :] = part.astype(BF)
        for r in range(3):
            tail_copy(turn, r).start()

    def keep_own(part):
        n.own[...] = part

    def reduced(turn):
        for r in range(3):
            tail_copy(turn, r).wait_recv()
        for r in range(3):
            scatter_copy(r).wait_recv()
        total = n.own[:SHARE, :]
        rest = n.own[SHARE:, :].astype(BF).astype(F32)
        for r in range(3):
            total = total + n.rsR[r].astype(F32)
            rest = rest + n.rtR[turn, r].astype(F32)
        for r in range(3):
            scatter_copy(r).wait_send()
            tail_copy(turn, r).wait_send()
        return jnp.concatenate([total, rest], axis=0)

    def pack_rows(v):
        return jnp.concatenate([v[:PACK], v[PACK:]], axis=1)

    def pad_lanes(v):
        return jnp.concatenate([v, jnp.zeros_like(v)], axis=1)

    def chunk_rows(j, size):
        return pl.ds(pl.multiple_of(j * size, size), size)

    def chunk_send(stage, dest, l, j, pos, size, ss, rs):
        dest[l, s, chunk_rows(j, size), :] = stage[s, chunk_rows(j, size), :]
        for k in range(3):
            rcopy(
                stage.at[zs[k], chunk_rows(j, size)], dest.at[l, s, chunk_rows(j, size)],
                ss.at[k, pos], rs.at[k, pos], z_dev(k),
            ).start()

    def tail_send(stage, dest, l, start, size, ss, rs):
        dest[l, s, pl.ds(start, size), :] = stage[s, pl.ds(start, size), :]
        for k in range(3):
            rcopy(
                stage.at[zs[k], pl.ds(start, size)], dest.at[l, s, pl.ds(start, size)],
                ss.at[k, 4], rs.at[k, 4], z_dev(k),
            ).start()

    def chunk_wait(stage, dest, l, size, start, tail_size, ss, rs):
        order = (m,) + peers
        for k in range(3):
            for pos in range(4):
                cp = rcopy(
                    stage.at[zs[k], chunk_rows(order[pos], size)], dest.at[l, s, chunk_rows(order[pos], size)],
                    ss.at[k, pos], rs.at[k, pos], z_dev(k),
                )
                cp.wait()
            rcopy(
                stage.at[zs[k], pl.ds(start, tail_size)], dest.at[l, s, pl.ds(start, tail_size)],
                ss.at[k, 4], rs.at[k, 4], z_dev(k),
            ).wait()

    def back_copy(stage, dest, l, k, pos, size, tail_size, ss, rs):
        if pos == 4:
            rows = pl.ds(MP_N * size, tail_size)
        else:
            rows = chunk_rows(m if pos == 0 else peers[pos - 1], size)
        return rcopy(stage.at[zs[k], rows], dest.at[l, s, rows], ss.at[k, pos], rs.at[k, pos], z_dev(k))

    BACK_ORDER = (3, 1, 2, 0, 4)

    def back_send(stage, dest, l, size, tail_size, ss, rs):
        for pos in BACK_ORDER:
            for k in range(3):
                back_copy(stage, dest, l, k, pos, size, tail_size, ss, rs).start()
        dest[l, s] = stage[s]

    def back_wait(stage, dest, l, pos, size, tail_size, ss, rs):
        for k in range(3):
            back_copy(stage, dest, l, k, pos, size, tail_size, ss, rs).wait()

    def side_by_side(pieces, low):
        return jnp.concatenate([g[:, :HD] if low else g[:, HD:] for g in pieces], axis=1)

    def g_parts(l, seg):
        if seg == "o":
            return n.gbo.at[l], n.rAo.at[l], n.rBo.at[l]
        return n.gbq, n.rAp, n.rBq

    def g_copy(phase, l, seg):
        at = SEG_AT[seg]
        start, count = SEG[seg]
        rows = pl.ds(start, count)
        full, got, part = g_parts(l, seg)
        if phase == 0:
            dev = core_dev
            if seg in "du" and l == 0:
                src, dst = n.gb0.at[1 - c, rows], n.rA0.at[rows]
            elif seg in "du":
                src, dst = n.gb1.at[1 - c, :, rows], n.rA1.at[:, rows]
            else:
                src, dst = full.at[1 - c], got
        elif phase <= 2:
            b = 1 - z1 if phase == 1 else z1
            src, dst, dev = full.at[c, 1 - z0, b], part.at[b], z_dev(0)
        else:
            dev = z_dev(1)
            if seg in "du":
                rows = pl.ds(start + 512 * (phase - 3), 512)
                src = n.gb1.at[c, 1 - z1, rows]
            else:
                src = full.at[c, z0, 1 - z1]
            dst = n.rC.at[l, rows]
        return rcopy(src, dst, n.g_s.at[l, phase, at], n.g_r.at[l, phase, at], dev)

    def f(phase, l, seg):
        g_copy(phase, l, seg).start()

    def add_to(ref, got):
        ref[...] = (ref[...].astype(F32) + got[...].astype(F32)).astype(BF)

    def a(phase, l, seg):
        g_copy(phase, l, seg).wait()
        start, count = SEG[seg]
        rows = pl.ds(start, count)
        full, got, part = g_parts(l, seg)
        if phase == 0 and seg in "du" and l == 0:
            n.ob[l, rows, :] = (n.gb0[c, rows, :].astype(F32) + n.rA0[rows, :].astype(F32)).astype(BF)
        elif phase == 0:
            for b in range(2):
                if seg in "du":
                    add_to(n.gb1.at[c, b, rows], n.rA1.at[b, rows])
                else:
                    for i in range(2):
                        add_to(full.at[c, i, b], got.at[i, b])
        elif phase <= 2:
            b = 1 - z1 if phase == 1 else z1
            add_to(full.at[c, z0, b], part.at[b])
        else:
            if seg in "du":
                g_copy(4, l, seg).wait()
                mine = n.gb1[c, z1, rows, :]
            else:
                mine = full[c, z0, z1]
            n.ob[l, rows, :] = (mine.astype(F32) + n.rC[l, rows, :].astype(F32)).astype(BF)

    def partner_copy(buf, pos, ss, rs):
        if pos == 4:
            src, dst = tail, pl.ds(ROWS + MP_N * SHARE, TAIL)
        else:
            j = m if pos == 0 else peers[pos - 1]
            src, dst = share(j), pl.ds(pl.multiple_of(ROWS + j * SHARE, TAIL), SHARE)
        return rcopy(buf.at[src], buf.at[dst], ss.at[pos], rs.at[pos], z_dev(0))

    def block_copies(buf, k, ss, rs):
        at = ROWS * (k + 1)
        return (
            rcopy(buf.at[share(m)], buf.at[pl.ds(pl.multiple_of(at + m * SHARE, TAIL), SHARE)], ss.at[k, 0], rs.at[k, 0], z_dev(k)),
            rcopy(buf.at[tail], buf.at[pl.ds(at + MP_N * SHARE, TAIL)], ss.at[k, 1], rs.at[k, 1], z_dev(k)),
        )

    def pass_copy(buf, k, r, ss, rs):
        at = ROWS * (k + 1)
        if r < 2:
            rows = pl.ds(pl.multiple_of(at + m * SHARE, TAIL), SHARE)
            dev = mp_dev(r)
        else:
            rows = pl.ds(pl.multiple_of(at + peers[r - 2] * SHARE + (r - 2) * (SHARE // 2), TAIL), SHARE // 2)
            dev = mp_dev(3 - r)
        return rcopy(buf.at[rows], buf.at[rows], ss.at[k, r], rs.at[k, r], dev)

    def block_send(buf, ss, rs, which=(0, 1, 2)):
        for k in which:
            for cp in block_copies(buf, k, ss, rs):
                cp.start()

    def block_pass(buf, zss, zrs, ss, rs, which=(0, 1, 2)):
        for k in which:
            for cp in block_copies(buf, k, zss, zrs):
                cp.wait()
            for r in range(2):
                pass_copy(buf, k, r, ss, rs).start()

    def block_pass_on(buf, ss, rs, which=(0, 1, 2)):
        for k in which:
            for r in range(2):
                pass_copy(buf, k, r, ss, rs).wait()
                pass_copy(buf, k, r + 2, ss, rs).start()

    def block_wait(buf, ss, rs, which=(0, 1, 2)):
        for k in which:
            for r in range(2, 4):
                pass_copy(buf, k, r, ss, rs).wait()

    def others_forward(l):
        for pos in range(5):
            partner_copy(hin[l], pos, n.hp_s.at[l], n.hp_r.at[l]).wait()
        if l == 0:
            block_wait(hin[0], n.hf_s, n.hf_r, (1, 2))
        for k in range(3 if l == 0 else 1):
            rows = pl.ds(ROWS * (k + 1), ROWS)
            value, slope = gelu_pair(dot(hin[l][rows, :], n.wu[l]) + n.bu[pl.ds(l, 1), :])
            act[l][rows, :] = value.astype(BF)
            n.gprP[pl.ds(ROWS * k, ROWS), :] = slope.astype(BF)

    def others_backward(l):
        if l == 1:
            for pos in range(5):
                partner_copy(dob[1], pos, n.dp_s, n.dp_r).wait()
        else:
            block_wait(dob[0], n.df_s, n.df_r)
        for k in range(3 if l == 0 else 1):
            rows = pl.ds(ROWS * (k + 1), ROWS)
            n.dlf[rows, :] = (dot(dob[l][rows, :], n.wd[l], 1, 1) * n.gprP[pl.ds(ROWS * k, ROWS), :].astype(F32)).astype(BF)

    def half_columns(ref):
        return jnp.concatenate([ref[:, pl.ds(pl.multiple_of(z0 * 256 + 512 * b, 256), 256)] for b in range(2)], axis=1)

    def own_columns(ref):
        return ref[:, pl.ds(pl.multiple_of(s * 256, 256), 256)]

    def grad_down(l):
        if l == 1:
            grad = dot(act[1][...], half_columns(dob[1]), 0, 0).astype(BF)
            for k in range(4):
                n.gb1[k % 2, k // 2, pl.ds(0, 1024), :] = grad[:, 128 * k:128 * k + 128]
        else:
            grad = dot(own_columns(dob[0]), act[0][...], 0, 0).T.astype(BF)
            for k in range(2):
                n.gb0[k, pl.ds(0, 1024), :] = grad[:, 128 * k:128 * k + 128]
        f(0, l, "d")

    def grad_up(l):
        if l == 1:
            grad = dot(half_columns(hin[1]), n.dlf[:2 * ROWS, :], 0, 0).astype(BF)
        else:
            grad = dot(own_columns(hin[0]), n.dlf[...], 0, 0).astype(BF)
        for k in range(4 if l == 1 else 2):
            for t in range(8):
                piece = grad[128 * k:128 * k + 128, 128 * t:128 * t + 128]
                if l == 1:
                    n.gb1[k % 2, k // 2, pl.ds(1024 + 128 * t, 128), :] = piece
                else:
                    n.gb0[k, pl.ds(1024 + 128 * t, 128), :] = piece
        f(0, l, "u")

    def head_core():
        return rcopy(n.gq.at[1 - c], n.rAq, n.gq_s.at[3], n.gq_r.at[3], core_dev)

    def head_copies():
        return [rcopy(n.gq.at[c, zs[k]], n.rQ.at[s], n.gq_s.at[k], n.gq_r.at[k], z_dev(k)) for k in range(3)]

    def head_grad():
        block_wait(n.nrm0, n.nf_s, n.nf_r)
        grad = dot(n.eq[...], n.nrm0[...], 0, 0).astype(BF)
        for k in range(8):
            n.gq[k % 2, k // 2] = grad[:, 128 * k:128 * k + 128]
        head_core().start()

    def head_grad_send():
        head_core().wait()
        for z in range(SEQ_N):
            add_to(n.gq.at[c, z], n.rAq.at[z])
        for cp in head_copies():
            cp.start()
        n.rQ[s] = n.gq[c, s]

    def head_grad_last():
        for cp in head_copies():
            cp.wait()
        for t in range(6):
            rows = pl.ds(HD * (t // 2), HD)
            both = jnp.concatenate([n.rQ[2 * (t % 2), rows, :], n.rQ[2 * (t % 2) + 1, rows, :]], axis=0)
            n.ob[0, pl.ds(2304 + 128 * t, 128), :] = both.astype(F32).T.astype(BF)

    def hook(l, at):
        for step in SCHEDULE.get((l, at), ()):
            (f if step[0] == "f" else a)(int(step[1]), int(step[2]), step[3])

    def g_out(l):
        return [
            pltpu.make_async_copy(
                n.ob.at[l, pl.ds(GPIECE * t, GPIECE)],
                n.out_o.at[pl.ds(OUT_GRADS + GPIECE * l, GPIECE), pl.ds(128 * t, 128)],
                n.out.at[l, t],
            )
            for t in range(8)
        ]

    text_count = n.tl[0]

    def gelu_pair(u):
        uu = u * u
        t = jnp.tanh(SQRT_2_PI * (u + 0.044715 * u * uu))
        half = 0.5 * (1.0 + t)
        slope = half + 0.5 * u * (1.0 - t * t) * (SQRT_2_PI * (1.0 + 3 * 0.044715 * uu))
        return u * half, slope

    order_rows = lambda own_value, pos, buf: own_value if pos == 0 else buf[share(peers[pos - 1]), :]

    def forward(l, first):
        own_rows = ln(n.cur[...], l, 0).astype(BF)
        if first:
            pl.semaphore_wait(barrier, len(everyone))
        copies = gather_rows(nrm[l], own_rows)
        if first:
            loads[2].wait()
        for pos in range(4):
            if pos > 0:
                copies[pos - 1].wait_recv()
            rows = order_rows(own_rows, pos, nrm[l])
            q = dot(rows, n.wq[l, 0]) + n.bqv[l, pl.ds(0, 1), :]
            k = dot(rows, n.wq[l, 1])
            v = dot(rows, n.wq[l, 2]) + n.bqv[l, pl.ds(1, 1), :]
            j = m if pos == 0 else peers[pos - 1]
            at = pl.multiple_of(j * BLK, BLK)
            for h in range(SEQ_N):
                cut = slice(HD * h, HD * h + HD)
                n.qs[h, pl.ds(at, SHARE), :] = jnp.concatenate([q[:SHARE, cut], k[:SHARE, cut]], axis=1).astype(BF)
                n.qs[h, pl.ds(at + SHARE, PACK), :] = pack_rows(v[:SHARE, cut]).astype(BF)
                if pos == 0:
                    n.qs[h, pl.ds(MP_N * BLK, TAIL), :] = jnp.concatenate([q[SHARE:, cut], k[SHARE:, cut]], axis=1).astype(BF)
                    n.qs[h, pl.ds(MP_N * BLK + TAIL, TAIL), :] = pad_lanes(v[SHARE:, cut]).astype(BF)
            chunk_send(n.qs, n.qkvA, l, j, pos, BLK, n.qk_s, n.qk_r)
            if pos == 0:
                tail_send(n.qs, n.qkvA, l, MP_N * BLK, 2 * TAIL, n.qk_s, n.qk_r)
        for cp in copies:
            cp.wait_send()
        if not first:
            block_pass(hin[0], n.hz_s, n.hz_r, n.hf_s, n.hf_r, (1, 2))
        chunk_wait(n.qs, n.qkvA, l, BLK, MP_N * BLK, 2 * TAIL, n.qk_s, n.qk_r)
        for zb in range(SEQ_N):
            for j in range(MP_N):
                both = n.qkvA[l, zb, pl.ds(BLK * j, SHARE), :]
                vals = n.qkvA[l, zb, pl.ds(BLK * j + SHARE, PACK), :]
                at = ROWS * zb + SHARE * j
                n.q_s[l, pl.ds(at, SHARE), :] = both[:, :HD]
                n.k_s[l, pl.ds(at, SHARE), :] = both[:, HD:]
                n.v_s[l, pl.ds(at, PACK), :] = vals[:, :HD]
                n.v_s[l, pl.ds(at + PACK, PACK), :] = vals[:, HD:]
            both = n.qkvA[l, zb, pl.ds(BLK * MP_N, TAIL), :]
            vals = n.qkvA[l, zb, pl.ds(BLK * MP_N + TAIL, TAIL), :]
            at = ROWS * zb + SHARE * MP_N
            n.q_s[l, pl.ds(at, TAIL), :] = both[:, :HD]
            n.k_s[l, pl.ds(at, TAIL), :] = both[:, HD:]
            n.v_s[l, pl.ds(at, TAIL), :] = vals[:, :HD]
        for i in range(SEQ_N):
            width = ROWS * (i + 1)
            st = dot(n.k_s[l, pl.ds(0, width), :], n.q_s[l, pl.ds(ROWS * i, ROWS), :], 1, 1) * SCORE_SCALE
            key_at = lax.broadcasted_iota(jnp.int32, (ROWS, ROWS), 0)
            query_at = lax.broadcasted_iota(jnp.int32, (ROWS, ROWS), 1)
            causal = key_at <= query_at
            if i == 0:
                st = jnp.where(causal & ((key_at >= TEXT) | (key_at < text_count)), st, -1e30)
            else:
                text_at = lax.broadcasted_iota(jnp.int32, (TEXT, ROWS), 0)
                st = jnp.concatenate([
                    jnp.where(text_at < text_count, st[:TEXT], -1e30),
                    st[TEXT:ROWS * i],
                    jnp.where(causal, st[ROWS * i:], -1e30),
                ], axis=0)
            e = jnp.exp(st - jnp.max(st, axis=0, keepdims=True))
            p = (e * (1.0 / jnp.sum(e, axis=0, keepdims=True))).astype(BF)
            pts[i][l] = p
            o = dot(n.v_s[l, pl.ds(0, width), :], p, 0, 0).T
            for j in range(MP_N):
                n.os_[i, pl.ds(PACK * j, PACK), :] = pack_rows(o[SHARE * j:SHARE * j + SHARE]).astype(BF)
            n.os_[i, pl.ds(PACK * MP_N, TAIL), :] = pad_lanes(o[SHARE * MP_N:]).astype(BF)
        back_send(n.os_, n.oA, l, PACK, TAIL, n.o_s, n.o_r)
        if not first:
            block_pass_on(hin[0], n.hf_s, n.hf_r, (1, 2))
        if first:
            loads[3].wait()
        for pos in BACK_ORDER[:4]:
            back_wait(n.os_, n.oA, l, pos, PACK, TAIL, n.o_s, n.o_r)
            j = m if pos == 0 else peers[pos - 1]
            got = [n.oA[l, h, chunk_rows(j, PACK), :] for h in range(SEQ_N)]
            rows = jnp.concatenate([side_by_side(got, True), side_by_side(got, False)], axis=0)
            n.att[l, share(j), :] = rows
            if pos > 0:
                send_part(pos - 1, dot(rows, n.wo[l]))
            else:
                back_wait(n.os_, n.oA, l, 4, PACK, TAIL, n.o_s, n.o_r)
                got = [n.oA[l, h, pl.ds(PACK * MP_N, TAIL), :] for h in range(SEQ_N)]
                rest = side_by_side(got, True)
                n.att[l, tail, :] = rest
                part = dot(jnp.concatenate([rows, rest], axis=0), n.wo[l])
                send_tail(0, part[SHARE:])
                keep_own(part)
        if not first:
            block_send(n.nrm0, n.nz_s, n.nz_r)
        branch = reduced(0) + n.bo[pl.ds(l, 1), :]
        settled = n.cur[...] + ln(branch, l, 1)
        n.stl[...] = settled
        own_rows = ln(settled, l, 2).astype(BF)
        copies = gather_rows(hin[l], own_rows)
        if first:
            block_send(hin[0], n.hz_s, n.hz_r, (1, 2))
        partner_copy(hin[l], 0, n.hp_s.at[l], n.hp_r.at[l]).start()
        partner_copy(hin[l], 4, n.hp_s.at[l], n.hp_r.at[l]).start()
        if first:
            loads[4].wait()
            loads[5].wait()
        for pos in range(4):
            if pos > 0:
                copies[pos - 1].wait_recv()
                partner_copy(hin[l], pos, n.hp_s.at[l], n.hp_r.at[l]).start()
            rows = order_rows(own_rows, pos, hin[l])
            value, slope = gelu_pair(dot(rows, n.wu[l]) + n.bu[pl.ds(l, 1), :])
            value = value.astype(BF)
            j = m if pos == 0 else peers[pos - 1]
            act[l][share(j), :] = value[:SHARE]
            n.gpr[l, share(j), :] = slope[:SHARE]
            part = dot(value, n.wd[l])
            if pos == 0:
                act[l][tail, :] = value[SHARE:]
                n.gpr[l, tail, :] = slope[SHARE:]
                send_tail(1, part[SHARE:])
                keep_own(part)
            else:
                send_part(pos - 1, part)
        for cp in copies:
            cp.wait_send()
        out_branch = reduced(1) + n.bd[pl.ds(l, 1), :]
        n.cur[...] = n.stl[...] + ln(out_branch, l, 3)

    result_copies = []

    def final_rows(which, stage):
        copies = []
        out = n.out_o.at[pl.ds(ROWS * which, ROWS)]
        for r in range(3):
            copies.append(rcopy(stage.at[pl.ds(0, SHARE)], out.at[share(m)], n.fr_s.at[which, r], n.fr_r.at[which, r], mp_dev(r)))
        copies.append(pltpu.make_async_copy(stage.at[pl.ds(0, SHARE)], out.at[share(m)], n.fl.at[which, 0]))
        copies.append(pltpu.make_async_copy(stage.at[pl.ds(SHARE, TAIL)], out.at[pl.ds(MP_N * SHARE, TAIL)], n.fl.at[which, 1]))
        for cp in copies:
            cp.start()
        return copies

    def backward(l):
        grad_rows = n.grd[...]
        d_ob = ln_back(l, 3, grad_rows).astype(BF)
        copies = gather_rows(dob[l], d_ob)
        if l == 1:
            partner_copy(dob[1], 0, n.dp_s, n.dp_r).start()
            partner_copy(dob[1], 4, n.dp_s, n.dp_r).start()
        else:
            block_send(dob[0], n.dz_s, n.dz_r)
        ln_params(l, 3, grad_rows)
        n.sg[l, pl.ds(9, 1), :] = jnp.sum(d_ob.astype(F32) * counted, axis=0, keepdims=True)
        hook(l, 0)
        for pos in range(4):
            if pos > 0:
                copies[pos - 1].wait_recv()
                if l == 1:
                    partner_copy(dob[1], pos, n.dp_s, n.dp_r).start()
            rows = order_rows(d_ob, pos, dob[l])
            j = m if pos == 0 else peers[pos - 1]
            slope = n.gpr[l, share(j), :]
            if pos == 0:
                slope = jnp.concatenate([slope, n.gpr[l, tail, :]], axis=0)
            d_l = (dot(rows, n.wd[l], 1, 1) * slope).astype(BF)
            n.dlf[share(j), :] = d_l[:SHARE]
            part = dot(d_l, n.wu[l], 1, 1)
            if pos == 0:
                n.dlf[tail, :] = d_l[SHARE:]
                send_tail(0, part[SHARE:])
                keep_own(part)
                if l == 1:
                    others_forward(1)
            else:
                send_part(pos - 1, part)
        for cp in copies:
            cp.wait_send()
        hook(l, 1)
        n.sg[l, pl.ds(10, 1), :] = jnp.sum(n.dlf[:ROWS, :].astype(F32), axis=0, keepdims=True)
        hook(l, 2)
        d_hidden = reduced(0)
        d_settled = grad_rows + ln_back(l, 2, d_hidden)
        d_br = ln_back(l, 1, d_settled).astype(BF)
        copies = gather_rows(n.dbr, d_br)
        n.stl[...] = d_settled
        ln_params(l, 2, d_hidden)
        ln_params(l, 1, d_settled)
        n.sg[l, pl.ds(8, 1), :] = jnp.sum(d_br.astype(F32) * counted, axis=0, keepdims=True)
        hook(l, 3)
        for pos in range(4):
            if pos > 0:
                copies[pos - 1].wait_recv()
            rows = order_rows(d_br, pos, n.dbr)
            j = m if pos == 0 else peers[pos - 1]
            d_at = dot(rows, n.wo[l], 1, 1)
            for h in range(SEQ_N):
                cut = slice(HD * h, HD * h + HD)
                n.ds_[h, chunk_rows(j, PACK), :] = pack_rows(d_at[:SHARE, cut]).astype(BF)
                if pos == 0:
                    n.ds_[h, pl.ds(MP_N * PACK, TAIL), :] = pad_lanes(d_at[SHARE:, cut]).astype(BF)
            chunk_send(n.ds_, n.dA, l, j, pos, PACK, n.do_ss, n.do_r)
            if pos == 0:
                tail_send(n.ds_, n.dA, l, MP_N * PACK, TAIL, n.do_ss, n.do_r)
                if l == 1:
                    others_backward(1)
                    grad_down(1)
                hook(l, 31)
        for cp in copies:
            cp.wait_send()
        hook(l, 4)
        if l == 1:
            grad_up(1)
            block_pass(n.nrm0, n.nz_s, n.nz_r, n.nf_s, n.nf_r)
        else:
            block_pass(dob[0], n.dz_s, n.dz_r, n.df_s, n.df_r)
        grad = dot(n.att[l], n.dbr[...], 0, 0).astype(BF)
        for k in range(8):
            n.gbo[l, k % 2, (k // 2) % 2, k // 4] = grad[:, 128 * k:128 * k + 128]
        f(0, l, "o")
        hook(l, 5)
        chunk_wait(n.ds_, n.dA, l, PACK, MP_N * PACK, TAIL, n.do_ss, n.do_r)
        for zb in range(SEQ_N):
            for j in range(MP_N):
                vals = n.dA[l, zb, pl.ds(PACK * j, PACK), :]
                at = ROWS * zb + SHARE * j
                n.do_s[pl.ds(at, PACK), :] = vals[:, :HD]
                n.do_s[pl.ds(at + PACK, PACK), :] = vals[:, HD:]
            n.do_s[pl.ds(ROWS * zb + SHARE * MP_N, TAIL), :] = n.dA[l, zb, pl.ds(PACK * MP_N, TAIL), :][:, :HD]
        hook(l, 6)
        for i in reversed(range(SEQ_N)):
            width = ROWS * (i + 1)
            here = pl.ds(ROWS * i, ROWS)
            p = pts[i][l]
            dpt = dot(n.v_s[l, pl.ds(0, width), :], n.do_s[here, :], 1, 1)
            pf = p.astype(F32)
            mean_term = jnp.sum(pf * dpt, axis=0, keepdims=True)
            dst = (pf * (dpt - mean_term)).astype(BF)
            dv = dot(p, n.do_s[here, :])
            dk = dot(dst, n.q_s[l, here, :])
            if i < SEQ_N - 1:
                dv = dv + n.dv_s[pl.ds(0, width), :]
                dk = dk + n.dk_s[pl.ds(0, width), :]
            if i > 0:
                n.dv_s[pl.ds(0, ROWS * i), :] = dv[:ROWS * i]
                n.dk_s[pl.ds(0, ROWS * i), :] = dk[:ROWS * i]
            dq = dot(n.k_s[l, pl.ds(0, width), :], dst, 0, 0).T * SCORE_SCALE
            dk = dk[ROWS * i:] * SCORE_SCALE
            dv = dv[ROWS * i:]
            if l == 0:
                place = (z0 if i % 2 == 0 else 1 - z0) + 2 * (z1 if i < 2 else 1 - z1)
                at = pl.ds(pl.multiple_of(place * ROWS, TAIL), ROWS)
                n.eq[at, pl.ds(0, 2 * HD)] = jnp.concatenate([dq, dk], axis=1).astype(BF)
                n.eq[at, pl.ds(2 * HD, HD)] = dv.astype(BF)
            for j in range(MP_N):
                cut = slice(SHARE * j, SHARE * j + SHARE)
                n.es[i, pl.ds(BLK * j, SHARE), :] = jnp.concatenate([dq[cut], dk[cut]], axis=1).astype(BF)
                n.es[i, pl.ds(BLK * j + SHARE, PACK), :] = pack_rows(dv[cut]).astype(BF)
            cut = slice(SHARE * MP_N, ROWS)
            n.es[i, pl.ds(BLK * MP_N, TAIL), :] = jnp.concatenate([dq[cut], dk[cut]], axis=1).astype(BF)
            n.es[i, pl.ds(BLK * MP_N + TAIL, TAIL), :] = pad_lanes(dv[cut]).astype(BF)
        back_send(n.es, n.eA, l, BLK, 2 * TAIL, n.e_s, n.e_r)
        hook(l, 7)
        if l == 1:
            others_forward(0)
            block_pass_on(n.nrm0, n.nf_s, n.nf_r)
        else:
            head_grad()
            block_pass_on(dob[0], n.df_s, n.df_r)

        def d_norm_part(rows):
            total = dot(rows[0], n.wq[l, 0], 1, 1)
            total = total + dot(rows[1], n.wq[l, 1], 1, 1)
            return total + dot(rows[2], n.wq[l, 2], 1, 1)

        for pos in BACK_ORDER[:4]:
            back_wait(n.es, n.eA, l, pos, BLK, 2 * TAIL, n.e_s, n.e_r)
            j = m if pos == 0 else peers[pos - 1]
            at = pl.multiple_of(j * BLK, BLK)
            both = [n.eA[l, h, pl.ds(at, SHARE), :] for h in range(SEQ_N)]
            vals = [n.eA[l, h, pl.ds(at + SHARE, PACK), :] for h in range(SEQ_N)]
            rows = [side_by_side(both, True), side_by_side(both, False)]
            rows.append(jnp.concatenate([side_by_side(vals, True), side_by_side(vals, False)], axis=0))
            for t in range(3):
                n.dpr[share(j), pl.ds(COLS * t, COLS)] = rows[t]
            if pos > 0:
                send_part(pos - 1, d_norm_part(rows))
            else:
                back_wait(n.es, n.eA, l, 4, BLK, 2 * TAIL, n.e_s, n.e_r)
                both = [n.eA[l, h, pl.ds(BLK * MP_N, TAIL), :] for h in range(SEQ_N)]
                vals = [n.eA[l, h, pl.ds(BLK * MP_N + TAIL, TAIL), :] for h in range(SEQ_N)]
                rest = [side_by_side(both, True), side_by_side(both, False), side_by_side(vals, True)]
                for t in range(3):
                    n.dpr[tail, pl.ds(COLS * t, COLS)] = rest[t]
                part = d_norm_part([jnp.concatenate([rows[t], rest[t]], axis=0) for t in range(3)])
                send_tail(1, part[SHARE:])
                keep_own(part)
        hook(l, 70)
        if l == 1:
            result_copies.extend(final_rows(0, n.resb))
        if l == 0:
            head_grad_send()
        if l == 1:
            grad = dot(nrm[l][...], n.dpr[...], 0, 0).astype(BF)
            for k in range(8):
                for t in range(6):
                    n.gbq[k % 2, (k // 2) % 2, k // 4, pl.ds(128 * t, 128), :] = grad[128 * k:128 * k + 128, 128 * t:128 * t + 128]
            f(0, l, "q")
        else:
            others_backward(0)
            grad_down(0)
            grad_up(0)
        sums = jnp.sum(n.dpr[...].astype(F32), axis=0, keepdims=True)
        blank = jnp.zeros((1, 96), F32)
        for at, lane in ((11, 0), (12, 2 * COLS)):
            pieces = []
            for k in range(8):
                pieces += [sums[:, lane + 32 * k:lane + 32 * k + 32], blank]
            n.sg[l, pl.ds(at, 1), :] = jnp.concatenate(pieces, axis=1)
        n.sg[l, pl.ds(13, 3), :] = jnp.zeros((3, D), F32)
        hook(l, 8)
        d_norm = reduced(1)
        n.grd[...] = n.stl[...] + ln_back(l, 0, d_norm)
        ln_params(l, 0, d_norm)
        hook(l, 9)

    forward(0, True)
    forward(1, False)
    n.resb[...] = n.cur[...].astype(BF)
    loads[6].wait()
    loads[7].wait()
    backward(1)
    backward(0)
    n.gstb[...] = n.grd[...].astype(BF)
    grad_copies = final_rows(1, n.gstb)

    small = []
    for t, dev in enumerate(group):
        lanes = pl.ds(pl.multiple_of((dev[0] * 2 + dev[1]) * 128, 128), 128)
        cp = rcopy(n.sg.at[:, :, lanes], n.smR.at[t], n.sm_s.at[t], n.sm_r.at[t], dev)
        cp.start()
        small.append(cp)
    hook(2, 0)
    head_grad_last()
    for cp in small:
        cp.wait()
    total = n.sg[:, :, pl.ds(pl.multiple_of((s * 2 + c) * 128, 128), 128)]
    for t in range(7):
        total = total + n.smR[t]
    n.smS[...] = total
    small = []
    for r in range(3):
        cp = rcopy(n.smS, n.smM.at[r], n.sn_s.at[r], n.sn_r.at[r], mp_dev(r))
        cp.start()
        small.append(cp)
    hook(2, 1)
    for cp in small:
        cp.wait()
    shared = lax.broadcasted_iota(jnp.int32, (2, SMALL, 128), 1) < 10
    total = total + jnp.where(shared, n.smM[0] + n.smM[1] + n.smM[2], 0.0)
    high = total.astype(BF)
    rest = (total - high.astype(F32)).astype(BF)
    n.sb[...] = jnp.zeros((16, D), BF)
    for l in range(2):
        n.sb[:, pl.ds(256 * l, 128)] = high[l]
        n.sb[:, pl.ds(256 * l + 128, 128)] = rest[l]
    last = [pltpu.make_async_copy(n.sb, n.out_o.at[pl.ds(OUT_SMALL, 16)], n.so.at[0])]
    last[0].start()
    hook(2, 2)
    for cp in g_out(0) + g_out(1):
        cp.start()
        last.append(cp)
    for cp in last + result_copies + grad_copies:
        cp.wait()


def finish_kernel(packed, res_o, gst_o, gain_o, shift_o, gq_o, qv_o, go_o, bo_o, gu_o, bu_o, gd_o, bd_o):
    res_o[...] = packed[:ROWS, :].astype(F32)
    gst_o[...] = packed[ROWS:2 * ROWS, :].astype(F32)
    for l in range(2):
        for b in range(24):
            lanes = slice(128 * (b // 3), 128 * (b // 3) + 128)
            start = OUT_GRADS + GPIECE * l + 128 * (b % 3)
            value = packed[start:start + 128, lanes].astype(F32)
            if b < 8:
                gd_o[l, 128 * b:128 * b + 128, :] = value
            elif b < 16:
                gu_o[l, :, 128 * (b - 8):128 * (b - 8) + 128] = value
            elif b < 18:
                go_o[l, 128 * (b - 16):128 * (b - 16) + 128, :] = value
            else:
                at = b - 18
                gq_o[l, at // 2, :, 128 * (at % 2):128 * (at % 2) + 128] = value
        small = packed[OUT_SMALL:OUT_SMALL + 16, 256 * l:256 * l + 128].astype(F32)
        small = small + packed[OUT_SMALL:OUT_SMALL + 16, 256 * l + 128:256 * l + 256].astype(F32)
        gain_o[l] = small[0:4]
        shift_o[l] = small[4:8]
        qv_o[l] = small[11:13, :32]
        bo_o[l:l + 1, :] = small[8:9]
        bd_o[l:l + 1, :] = small[9:10]
        bu_o[l:l + 1, :] = small[10:11]


def fused_shards(
    stream, text_len, norm_gain, norm_shift, w_qkv, bias_qv, w_out, bias_out, w_up, bias_up, w_down, bias_down, cotangent
):
    rows = (ROWS, D)
    any_space = pl.BlockSpec(memory_space=pl.ANY)
    vmem = pl.BlockSpec(memory_space=pltpu.VMEM)
    smem = pl.BlockSpec(memory_space=pltpu.SMEM)
    packed = pl.pallas_call(
        fused_kernel,
        out_shape=jax.ShapeDtypeStruct((OUT_ROWS, D), BF),
        in_specs=[smem, any_space, any_space, vmem, vmem, vmem, vmem, vmem, vmem] + [any_space] * 4,
        out_specs=any_space,
        scratch_shapes=[pltpu.VMEM(shape, dtype) for shape, dtype in VMEM_SCRATCH.values()]
        + [pltpu.SemaphoreType.DMA(shape) for shape in DMA_SEMS.values()],
        compiler_params=pltpu.CompilerParams(
            collective_id=0, has_side_effects=True, vmem_limit_bytes=63 * 2**20
        ),
    )(
        text_len,
        stream.reshape(rows),
        cotangent.reshape(rows),
        norm_gain,
        norm_shift,
        bias_qv,
        bias_out,
        bias_up,
        bias_down,
        w_qkv.transpose(0, 2, 1, 3),
        w_out,
        w_up,
        w_down,
    )
    shape = lambda *dims: jax.ShapeDtypeStruct(dims, F32)
    done = pl.pallas_call(
        finish_kernel,
        out_shape=(
            shape(*rows), shape(*rows), shape(2, 4, 128), shape(2, 4, 128), shape(2, 3, 128, COLS), shape(2, 2, 32),
            shape(2, COLS, 128), shape(2, 128), shape(2, 128, FFL), shape(2, 128), shape(2, FFL, 128), shape(2, 128),
        ),
        in_specs=[vmem],
        out_specs=[vmem] * 12,
        compiler_params=pltpu.CompilerParams(vmem_limit_bytes=32 * 2**20),
    )(packed)
    return (
        done[0].reshape(1, ROWS, D),
        done[1].reshape(1, ROWS, D),
        done[2],
        done[3],
        done[4].transpose(0, 2, 1, 3),
    ) + tuple(done[5:])


def solution(mesh):
    return jax.shard_map(
        fused_shards if fits(mesh) else shards,
        mesh=mesh,
        in_specs=(
            P("dp", "seq", None),
            P("dp"),
            P(),
            P(),
            P(None, None, None, "mp"),
            P(None, None, "mp"),
            P(None, "mp", None),
            P(),
            P(None, None, "mp"),
            P(None, "mp"),
            P(None, "mp", None),
            P(),
            P("dp", "seq", None),
        ),
        out_specs=(
            P("dp", "seq", None),
            P("dp", "seq", None),
            P(None, None, ("seq", "dp")),
            P(None, None, ("seq", "dp")),
            P(None, ("seq", "dp"), None, "mp"),
            P(None, None, ("mp", "seq", "dp")),
            P(None, "mp", ("seq", "dp")),
            P(None, ("seq", "dp")),
            P(None, ("seq", "dp"), "mp"),
            P(None, ("mp", "seq", "dp")),
            P(None, "mp", ("seq", "dp")),
            P(None, ("seq", "dp")),
        ),
        check_vma=False,
    )
```

```python
from functools import partial
import math

import jax
import jax.numpy as jnp
from jax import lax
from jax.experimental import pallas as pl
from jax.experimental.pallas import tpu as pltpu
from jax.sharding import PartitionSpec as P

D = 1024
HEADS = 16
TEXT = 64


relax_alpha = 32.0
norm_eps = 1e-05


def layer_norm(row_values, gain_row, shift_row):
    row_mean = jnp.mean(row_values, axis=-1, keepdims=True)
    centred = row_values - row_mean
    variance = jnp.mean(centred * centred, axis=-1, keepdims=True)
    return centred * lax.rsqrt(variance + norm_eps) * gain_row + shift_row


def norm_back(row_values, gain_row, shift_row, grad_rows):
    result_value, pull_back = jax.vjp(layer_norm, row_values, gain_row, shift_row)
    return pull_back(grad_rows)


def reduce_rows(partial_sum):
    return lax.psum_scatter(
        partial_sum.astype(jnp.bfloat16), "mp", scatter_dimension=0, tiled=True
    ).astype(jnp.float32)


def widen_rows(row_values):
    return lax.all_gather(row_values, "mp", axis=0, tiled=True)


def reduce_grads(partial_sum):
    return lax.psum_scatter(
        partial_sum.astype(jnp.bfloat16), "mp", scatter_dimension=0, tiled=True
    ).astype(jnp.float32)


def widen_grads(row_values):
    return lax.all_gather(row_values, "mp", axis=0, tiled=True)


def relaxed_scores(query_heads, key_heads, allowed, score_scale):
    raw_scores = (
        jnp.einsum("sqhe,skhe->shqk", query_heads, key_heads, preferred_element_type=jnp.float32)
        * score_scale
    )
    return jnp.where(allowed, raw_scores / relax_alpha, -1e30)


def shards(
    stream,
    text_len,
    norm_gain,
    norm_shift,
    w_qkv,
    bias_qv,
    w_out,
    bias_out,
    w_up,
    bias_up,
    w_down,
    bias_down,
    cotangent,
):
    seq_count, block_len, model_width = stream.shape
    rows_all = seq_count * block_len
    layers = w_qkv.shape[0]
    local_cols = w_qkv.shape[3]
    head_dim = D // HEADS
    heads_here = local_cols // head_dim
    score_scale = 1.0 / math.sqrt(head_dim)
    share_rows = rows_all // lax.axis_size("mp")
    first_row = lax.axis_index("mp") * share_rows
    block_start = lax.axis_index("seq") * block_len
    seq_span = block_len * lax.axis_size("seq")
    query_pos = block_start + jnp.arange(block_len, dtype=jnp.int32)
    key_pos = jnp.arange(seq_span, dtype=jnp.int32)
    causal = key_pos[None, :] <= query_pos[:, None]
    visible = (key_pos[None, :] >= TEXT) | (key_pos[None, :] < text_len[:, None])
    allowed = causal[None, None] & visible[:, None, None, :]
    flat_rows = stream.reshape(rows_all, model_width)
    grad_rows = cotangent.reshape(rows_all, model_width)
    current = lax.dynamic_slice_in_dim(flat_rows, first_row, share_rows, 0)
    grad_rows = lax.dynamic_slice_in_dim(grad_rows, first_row, share_rows, 0)
    gelu_tanh = partial(jax.nn.gelu, approximate=True)
    kept_state = []
    for layer_at in range(layers):
        gain_rows = norm_gain[layer_at]
        shift_rows = norm_shift[layer_at]
        normed = widen_rows(layer_norm(current, gain_rows[0], shift_rows[0]).astype(jnp.bfloat16))
        projected = jnp.einsum(
            "td,dcf->tcf", normed, w_qkv[layer_at], preferred_element_type=jnp.float32
        )
        queries = (projected[:, 0] + bias_qv[layer_at, 0]).astype(jnp.bfloat16)
        key_rows = projected[:, 1].astype(jnp.bfloat16)
        value_rows = (projected[:, 2] + bias_qv[layer_at, 1]).astype(jnp.bfloat16)
        keys_all, values_all = (
            lax.all_gather(
                key_rows.reshape(seq_count, block_len, local_cols), "seq", axis=1, tiled=True
            ),
            lax.all_gather(
                value_rows.reshape(seq_count, block_len, local_cols), "seq", axis=1, tiled=True
            ),
        )
        query_heads = queries.reshape(seq_count, block_len, heads_here, head_dim)
        key_heads = keys_all.reshape(seq_count, seq_span, heads_here, head_dim)
        value_heads = values_all.reshape(seq_count, seq_span, heads_here, head_dim)
        tempered = relaxed_scores(query_heads, key_heads, allowed, score_scale)
        highest = jnp.max(tempered, axis=-1, keepdims=True)
        exponent = jnp.exp(relax_alpha * (tempered - highest))
        totals = jnp.sum(exponent, axis=-1, keepdims=True)
        log_total = relax_alpha * highest + jnp.log(totals)
        weights = (exponent / totals).astype(jnp.bfloat16)
        attended = jnp.einsum(
            "shqk,skhe->sqhe", weights, value_heads, preferred_element_type=jnp.float32
        )
        attended = attended.astype(jnp.bfloat16).reshape(rows_all, local_cols)
        branch = (
            reduce_rows(jnp.dot(attended, w_out[layer_at], preferred_element_type=jnp.float32))
            + bias_out[layer_at]
        )
        settled = current + layer_norm(branch, gain_rows[1], shift_rows[1])
        hidden_in = widen_rows(
            layer_norm(settled, gain_rows[2], shift_rows[2]).astype(jnp.bfloat16)
        )
        lifted = (
            jnp.dot(hidden_in, w_up[layer_at], preferred_element_type=jnp.float32)
            + bias_up[layer_at]
        )
        activated = gelu_tanh(lifted).astype(jnp.bfloat16)
        output_branch = (
            reduce_rows(jnp.dot(activated, w_down[layer_at], preferred_element_type=jnp.float32))
            + bias_down[layer_at]
        )
        kept_state.append(
            (
                current,
                normed,
                query_heads,
                key_heads,
                value_heads,
                log_total,
                attended,
                branch,
                settled,
                hidden_in,
                lifted,
                activated,
                output_branch,
            )
        )
        current = settled + layer_norm(output_branch, gain_rows[3], shift_rows[3])
    collected = []
    for layer_at in reversed(range(layers)):
        (
            layer_in,
            normed,
            query_heads,
            key_heads,
            value_heads,
            log_total,
            attended,
            branch,
            settled,
            hidden_in,
            lifted,
            activated,
            output_branch,
        ) = kept_state[layer_at]
        gain_rows = norm_gain[layer_at]
        shift_rows = norm_shift[layer_at]
        d_out_branch, gain_three, shift_three = norm_back(
            output_branch, gain_rows[3], shift_rows[3], grad_rows
        )
        d_out_branch = d_out_branch.astype(jnp.bfloat16)
        d_bias_down = jnp.sum(d_out_branch.astype(jnp.float32), axis=0)
        d_down_full = widen_grads(d_out_branch)
        d_w_down = jnp.einsum(
            "tf,td->fd", activated, d_down_full, preferred_element_type=jnp.float32
        )
        d_activated = jnp.einsum(
            "td,fd->tf", d_down_full, w_down[layer_at], preferred_element_type=jnp.float32
        )
        gelu_value, gelu_pull = jax.vjp(gelu_tanh, lifted)
        d_lifted = gelu_pull(d_activated)[0].astype(jnp.bfloat16)
        d_bias_up = jnp.sum(d_lifted.astype(jnp.float32), axis=0)
        d_w_up = jnp.einsum("td,tf->df", hidden_in, d_lifted, preferred_element_type=jnp.float32)
        d_hidden = reduce_grads(
            jnp.einsum("tf,df->td", d_lifted, w_up[layer_at], preferred_element_type=jnp.float32)
        )
        d_norm_two, gain_two, shift_two = norm_back(settled, gain_rows[2], shift_rows[2], d_hidden)
        d_settled = grad_rows + d_norm_two
        d_branch, gain_one, shift_one = norm_back(branch, gain_rows[1], shift_rows[1], d_settled)
        d_branch = d_branch.astype(jnp.bfloat16)
        d_bias_out = jnp.sum(d_branch.astype(jnp.float32), axis=0)
        d_branch_full = widen_grads(d_branch)
        d_w_out = jnp.einsum(
            "tf,td->fd", attended, d_branch_full, preferred_element_type=jnp.float32
        )
        d_attended = jnp.einsum(
            "td,fd->tf", d_branch_full, w_out[layer_at], preferred_element_type=jnp.float32
        )
        d_attended = d_attended.astype(jnp.bfloat16).reshape(
            seq_count, block_len, heads_here, head_dim
        )
        tempered = relaxed_scores(query_heads, key_heads, allowed, score_scale)
        probabilities = jnp.exp(relax_alpha * tempered - log_total)
        d_probs = jnp.einsum(
            "sqhe,skhe->shqk", d_attended, value_heads, preferred_element_type=jnp.float32
        )
        d_values = jnp.einsum(
            "shqk,sqhe->skhe",
            probabilities.astype(jnp.bfloat16),
            d_attended,
            preferred_element_type=jnp.float32,
        )
        mean_term = jnp.sum(probabilities * d_probs, axis=-1, keepdims=True)
        d_raw = (probabilities * (d_probs - mean_term)).astype(jnp.bfloat16)
        d_queries = (
            jnp.einsum("shqk,skhe->sqhe", d_raw, key_heads, preferred_element_type=jnp.float32)
            * score_scale
        )
        d_keys = (
            jnp.einsum("shqk,sqhe->skhe", d_raw, query_heads, preferred_element_type=jnp.float32)
            * score_scale
        )
        d_keys_own, d_values_own = (
            lax.psum_scatter(
                d_keys.reshape(seq_count, seq_span, local_cols).astype(jnp.bfloat16),
                "seq",
                scatter_dimension=1,
                tiled=True,
            ).astype(jnp.float32),
            lax.psum_scatter(
                d_values.reshape(seq_count, seq_span, local_cols).astype(jnp.bfloat16),
                "seq",
                scatter_dimension=1,
                tiled=True,
            ).astype(jnp.float32),
        )
        d_queries = d_queries.reshape(rows_all, local_cols).astype(jnp.bfloat16)
        d_keys_own = d_keys_own.reshape(rows_all, local_cols).astype(jnp.bfloat16)
        d_values_own = d_values_own.reshape(rows_all, local_cols).astype(jnp.bfloat16)
        d_bias_qv = jnp.stack(
            [
                jnp.sum(d_queries.astype(jnp.float32), axis=0),
                jnp.sum(d_values_own.astype(jnp.float32), axis=0),
            ]
        )
        d_projected = jnp.stack([d_queries, d_keys_own, d_values_own], axis=1)
        d_w_qkv = jnp.einsum("td,tcf->dcf", normed, d_projected, preferred_element_type=jnp.float32)
        d_normed = reduce_grads(
            jnp.einsum(
                "tcf,dcf->td", d_projected, w_qkv[layer_at], preferred_element_type=jnp.float32
            )
        )
        d_layer_in, gain_zero, shift_zero = norm_back(
            layer_in, gain_rows[0], shift_rows[0], d_normed
        )
        grad_rows = d_settled + d_layer_in
        collected.append(
            (
                jnp.stack([gain_zero, gain_one, gain_two, gain_three]),
                jnp.stack([shift_zero, shift_one, shift_two, shift_three]),
                d_w_qkv,
                d_bias_qv,
                d_w_out,
                d_bias_out,
                d_w_up,
                d_bias_up,
                d_w_down,
                d_bias_down,
            )
        )
    collected = collected[::-1]
    stacked = tuple((jnp.stack([entry[index_at] for entry in collected]) for index_at in range(10)))
    (
        gain_grads,
        shift_grads,
        grad_qkv,
        grad_qv,
        grad_out_w,
        grad_out_b,
        grad_up_w,
        grad_up_b,
        grad_down_w,
        grad_down_b,
    ) = stacked
    gain_grads, shift_grads, grad_out_b, grad_down_b = (
        lax.psum(gain_grads.astype(jnp.bfloat16), "mp").astype(jnp.float32),
        lax.psum(shift_grads.astype(jnp.bfloat16), "mp").astype(jnp.float32),
        lax.psum(grad_out_b.astype(jnp.bfloat16), "mp").astype(jnp.float32),
        lax.psum(grad_down_b.astype(jnp.bfloat16), "mp").astype(jnp.float32),
    )
    current, grad_rows = (
        lax.all_gather(current.astype(jnp.bfloat16), "mp", axis=0, tiled=True).astype(
            current.dtype
        ),
        lax.all_gather(grad_rows.astype(jnp.bfloat16), "mp", axis=0, tiled=True).astype(
            grad_rows.dtype
        ),
    )
    summed = (
        lax.psum_scatter(
            gain_grads.astype(jnp.bfloat16), ("seq", "dp"), scatter_dimension=2, tiled=True
        ).astype(jnp.float32),
        lax.psum_scatter(
            shift_grads.astype(jnp.bfloat16), ("seq", "dp"), scatter_dimension=2, tiled=True
        ).astype(jnp.float32),
        lax.psum_scatter(
            grad_qkv.astype(jnp.bfloat16), ("seq", "dp"), scatter_dimension=1, tiled=True
        ).astype(jnp.float32),
        lax.psum_scatter(
            grad_qv.astype(jnp.bfloat16), ("seq", "dp"), scatter_dimension=2, tiled=True
        ).astype(jnp.float32),
        lax.psum_scatter(
            grad_out_w.astype(jnp.bfloat16), ("seq", "dp"), scatter_dimension=2, tiled=True
        ).astype(jnp.float32),
        lax.psum_scatter(
            grad_out_b.astype(jnp.bfloat16), ("seq", "dp"), scatter_dimension=1, tiled=True
        ).astype(jnp.float32),
        lax.psum_scatter(
            grad_up_w.astype(jnp.bfloat16), ("seq", "dp"), scatter_dimension=1, tiled=True
        ).astype(jnp.float32),
        lax.psum_scatter(
            grad_up_b.astype(jnp.bfloat16), ("seq", "dp"), scatter_dimension=1, tiled=True
        ).astype(jnp.float32),
        lax.psum_scatter(
            grad_down_w.astype(jnp.bfloat16), ("seq", "dp"), scatter_dimension=2, tiled=True
        ).astype(jnp.float32),
        lax.psum_scatter(
            grad_down_b.astype(jnp.bfloat16), ("seq", "dp"), scatter_dimension=1, tiled=True
        ).astype(jnp.float32),
    )
    result = current.reshape(seq_count, block_len, model_width)
    grad_stream = grad_rows.reshape(seq_count, block_len, model_width)
    return (
        result,
        grad_stream,
        summed[0],
        summed[1],
        summed[2],
        summed[3],
        summed[4],
        summed[5],
        summed[6],
        summed[7],
        summed[8],
        summed[9],
    )


MESH = pl.DeviceIdType.MESH
BF = jnp.bfloat16
F32 = jnp.float32

SEQ_N, DP_N, MP_N = 4, 2, 4
ROWS = 272
SHARE = 64
TAIL = 16
OWN = SHARE + TAIL
HD = 64
COLS = 256
FFL = 1024
PACK = 32
BLK = SHARE + PACK
QKV_ROWS = MP_N * BLK + 2 * TAIL
VP_ROWS = MP_N * PACK + TAIL
SEG = {"d": (0, 1024), "u": (1024, 1024), "o": (2048, 256), "q": (2304, 768)}
SEG_AT = {"d": 0, "u": 1, "o": 2, "q": 3}
GROWS = 3072
GPIECE = GROWS // 8
OUT_GRADS = 2 * ROWS
OUT_SMALL = OUT_GRADS + 2 * GPIECE
OUT_ROWS = OUT_SMALL + 16
SMALL = 16
SQRT_2_PI = math.sqrt(2.0 / math.pi)
SCORE_SCALE = 0.125


def dot(a, b, ca=1, cb=0):
    return lax.dot_general(a, b, (((ca,), (cb,)), ((), ())), preferred_element_type=F32)


def fits(mesh):
    return dict(mesh.shape) == {"seq": SEQ_N, "dp": DP_N, "mp": MP_N}


VMEM_SCRATCH = {
    "wq": ((2, 3, D, COLS), BF),
    "wo": ((2, COLS, D), BF),
    "wu": ((2, D, FFL), BF),
    "wd": ((2, FFL, D), BF),
    "cur": ((OWN, D), F32),
    "grd": ((OWN, D), F32),
    "stl": ((OWN, D), F32),
    "own": ((OWN, D), F32),
    "xh": ((2, 4, OWN, D), F32),
    "rstd": ((2, 4, OWN, 128), F32),
    "nrm0": ((4 * ROWS, D), BF),
    "nrm1": ((ROWS, D), BF),
    "hin0": ((4 * ROWS, D), BF),
    "hin1": ((2 * ROWS, D), BF),
    "act0": ((4 * ROWS, FFL), BF),
    "act1": ((2 * ROWS, FFL), BF),
    "gpr": ((2, ROWS, FFL), F32),
    "gprP": ((3 * ROWS, FFL), BF),
    "dob0": ((4 * ROWS, D), BF),
    "dbr": ((ROWS, D), BF),
    "dlf": ((4 * ROWS, FFL), BF),
    "att": ((2, ROWS, COLS), BF),
    "dpr": ((ROWS, 3 * COLS), BF),
    "qkvA": ((2, SEQ_N, QKV_ROWS, 128), BF),
    "q_s": ((2, SEQ_N * ROWS, HD), BF),
    "k_s": ((2, SEQ_N * ROWS, HD), BF),
    "v_s": ((2, SEQ_N * ROWS, HD), BF),
    "do_s": ((SEQ_N * ROWS, HD), BF),
    "dk_s": ((SEQ_N * ROWS, HD), F32),
    "dv_s": ((SEQ_N * ROWS, HD), F32),
    "pt0": ((2, ROWS, ROWS), BF),
    "pt1": ((2, 2 * ROWS, ROWS), BF),
    "pt2": ((2, 3 * ROWS, ROWS), BF),
    "pt3": ((2, 4 * ROWS, ROWS), BF),
    "oA": ((2, SEQ_N, VP_ROWS, 128), BF),
    "dA": ((2, SEQ_N, VP_ROWS, 128), BF),
    "eA": ((2, SEQ_N, QKV_ROWS, 128), BF),
    "qs": ((SEQ_N, QKV_ROWS, 128), BF),
    "os_": ((SEQ_N, VP_ROWS, 128), BF),
    "ds_": ((SEQ_N, VP_ROWS, 128), BF),
    "es": ((SEQ_N, QKV_ROWS, 128), BF),
    "rsS": ((ROWS, D), BF),
    "rsR": ((3, SHARE, D), BF),
    "rtR": ((2, 3, TAIL, D), BF),
    "eq": ((4 * ROWS, 3 * HD), BF),
    "gq": ((2, SEQ_N, 3 * HD, 128), BF),
    "rAq": ((SEQ_N, 3 * HD, 128), BF),
    "rQ": ((SEQ_N, 3 * HD, 128), BF),
    "gb0": ((2, 2048, 128), BF),
    "gb1": ((2, 2, 2048, 128), BF),
    "rA0": ((2048, 128), BF),
    "gbo": ((2, 2, 2, 2, 256, 128), BF),
    "gbq": ((2, 2, 2, 768, 128), BF),
    "rA1": ((2, 2048, 128), BF),
    "rAo": ((2, 2, 2, 256, 128), BF),
    "rAp": ((2, 2, 768, 128), BF),
    "rBo": ((2, 2, 256, 128), BF),
    "rBq": ((2, 768, 128), BF),
    "rC": ((2, GROWS, 128), BF),
    "ob": ((2, GROWS, 128), BF),
    "sb": ((16, D), BF),
    "sg": ((2, SMALL, D), F32),
    "smR": ((7, 2, SMALL, 128), F32),
    "smS": ((2, SMALL, 128), F32),
    "smM": ((3, 2, SMALL, 128), F32),
    "resb": ((OWN, D), BF),
    "gstb": ((OWN, D), BF),
}
DMA_SEMS = {
    "ld": (16,),
    "ag_s": (3,), "ag_r": (3,),
    "rs_s": (3,), "rs_r": (3,),
    "rt_s": (2, 3), "rt_r": (2, 3),
    "qk_s": (3, 5), "qk_r": (3, 5),
    "do_ss": (3, 5), "do_r": (3, 5),
    "o_s": (3, 5), "o_r": (3, 5),
    "e_s": (3, 5), "e_r": (3, 5),
    "g_s": (2, 5, 4), "g_r": (2, 5, 4),
    "hp_s": (2, 5), "hp_r": (2, 5), "dp_s": (5,), "dp_r": (5,),
    "nz_s": (3, 2), "nz_r": (3, 2), "nf_s": (3, 4), "nf_r": (3, 4),
    "gq_s": (4,), "gq_r": (4,),
    "hz_s": (3, 2), "hz_r": (3, 2), "dz_s": (3, 2), "dz_r": (3, 2),
    "hf_s": (3, 4), "hf_r": (3, 4), "df_s": (3, 4), "df_r": (3, 4),
    "out": (2, 8), "so": (1,),
    "fr_s": (2, 3), "fr_r": (2, 3), "fr_t": (2, 3), "fr_u": (2, 3),
    "fl": (2, 2),
    "sm_s": (7,), "sm_r": (7,), "sn_s": (3,), "sn_r": (3,),
}
SCHEDULE = {
    (1, 7): ("a01d", "f31d", "f41d", "a01u",),
    (1, 70): ("f31u", "f41u",),
    (1, 8): ("a01o", "f11o", "f21o",),
    (1, 9): ("a01q", "f11q", "f21q",),
    (0, 2): ("a11o", "f31o", "a11q", "f31q", "a21o", "a21q",),
    (0, 7): ("a31d", "a31u", "a00o", "f10o", "f20o",),
    (0, 8): ("a10o", "f30o", "a20o",),
    (0, 9): ("a31o", "a31q",),
    (2, 1): ("a30o", "a00d", "a00u"),
}
IN_NAMES = ("tl", "stream", "cot", "gain", "shift", "bqv", "bo", "bu", "bd", "wq_h", "wo_h", "wu_h", "wd_h")
OUT_NAMES = ("out_o",)


class Refs:
    pass


def fused_kernel(*all_refs):
    n = Refs()
    names = IN_NAMES + OUT_NAMES + tuple(VMEM_SCRATCH) + tuple(DMA_SEMS)
    for name, ref in zip(names, all_refs):
        setattr(n, name, ref)
    pts = (n.pt0, n.pt1, n.pt2, n.pt3)
    hin, act, dob = (n.hin0, n.hin1), (n.act0, n.act1), (n.dob0, n.dob0.at[pl.ds(0, 2 * ROWS)])
    nrm = (n.nrm0, n.nrm1)

    s = lax.axis_index("seq")
    c = lax.axis_index("dp")
    m = lax.axis_index("mp")
    mx, my = lax.rem(m, 2), lax.div(m, 2)
    peers = (my * 2 + (1 - mx), (1 - my) * 2 + mx, (1 - my) * 2 + (1 - mx))
    z0, z1 = lax.rem(s, 2), lax.div(s, 2)
    zs = (z1 * 2 + (1 - z0), (1 - z1) * 2 + z0, (1 - z1) * 2 + (1 - z0))

    def mp_dev(r):
        return (s, c, peers[r])

    def z_dev(k):
        return (zs[k], c, m)

    core_dev = (s, 1 - c, m)
    group = [core_dev] + [z_dev(k) for k in range(3)] + [(zs[k], 1 - c, m) for k in range(3)]

    barrier = pltpu.get_barrier_semaphore()
    everyone = group + [mp_dev(r) for r in range(3)]
    for dev in everyone:
        pl.semaphore_signal(barrier, inc=1, device_id=dev, device_id_type=MESH)

    loads = [
        pltpu.make_async_copy(n.stream.at[pl.ds(pl.multiple_of(m * SHARE, SHARE), SHARE)], n.cur.at[pl.ds(0, SHARE)], n.ld.at[0]),
        pltpu.make_async_copy(n.stream.at[pl.ds(MP_N * SHARE, TAIL)], n.cur.at[pl.ds(SHARE, TAIL)], n.ld.at[1]),
        pltpu.make_async_copy(n.wq_h, n.wq, n.ld.at[2]),
        pltpu.make_async_copy(n.wo_h, n.wo, n.ld.at[3]),
        pltpu.make_async_copy(n.wu_h, n.wu, n.ld.at[4]),
        pltpu.make_async_copy(n.wd_h, n.wd, n.ld.at[5]),
        pltpu.make_async_copy(n.cot.at[pl.ds(pl.multiple_of(m * SHARE, SHARE), SHARE)], n.grd.at[pl.ds(0, SHARE)], n.ld.at[6]),
        pltpu.make_async_copy(n.cot.at[pl.ds(MP_N * SHARE, TAIL)], n.grd.at[pl.ds(SHARE, TAIL)], n.ld.at[7]),
    ]
    for cp in loads:
        cp.start()
    loads[0].wait()
    loads[1].wait()

    def rcopy(src, dst, ss, rs, dev):
        return pltpu.make_async_remote_copy(
            src_ref=src, dst_ref=dst, send_sem=ss, recv_sem=rs, device_id=dev, device_id_type=MESH
        )

    def share(j):
        return pl.ds(pl.multiple_of(j * SHARE, SHARE), SHARE)

    tail = pl.ds(MP_N * SHARE, TAIL)

    def ln(v, l, j):
        ce = v - jnp.mean(v, axis=-1, keepdims=True)
        r = lax.rsqrt(jnp.mean(ce * ce, axis=-1, keepdims=True) + norm_eps)
        h = ce * r
        n.xh[l, j] = h
        n.rstd[l, j] = jnp.broadcast_to(r, (OWN, 128))
        return h * n.gain[l, pl.ds(j, 1), :] + n.shift[l, pl.ds(j, 1), :]

    def ln_back(l, j, dy):
        h = n.xh[l, j]
        r = n.rstd[l, j][:, :1]
        t = dy * n.gain[l, pl.ds(j, 1), :]
        m1 = jnp.mean(t, axis=-1, keepdims=True)
        m2 = jnp.mean(t * h, axis=-1, keepdims=True)
        return r * (t - m1 - h * m2)

    row_ids = lax.broadcasted_iota(jnp.int32, (OWN, 1), 0)
    counted = jnp.where((row_ids < SHARE) | (m == 0), 1.0, 0.0).astype(F32)

    def ln_params(l, j, dy):
        dw = dy * counted
        n.sg[l, pl.ds(j, 1), :] = jnp.sum(dw * n.xh[l, j], axis=0, keepdims=True)
        n.sg[l, pl.ds(4 + j, 1), :] = jnp.sum(dw, axis=0, keepdims=True)

    def gather_rows(buf, own_rows):
        buf[share(m), :] = own_rows[:SHARE]
        buf[tail, :] = own_rows[SHARE:]
        copies = []
        for r in range(3):
            cp = rcopy(buf.at[share(m)], buf.at[share(m)], n.ag_s.at[r], n.ag_r.at[r], mp_dev(r))
            cp.start()
            copies.append(cp)
        return copies

    def scatter_copy(r):
        return rcopy(n.rsS.at[share(peers[r])], n.rsR.at[r], n.rs_s.at[r], n.rs_r.at[r], mp_dev(r))

    def tail_copy(turn, r):
        return rcopy(n.rsS.at[tail], n.rtR.at[turn, r], n.rt_s.at[turn, r], n.rt_r.at[turn, r], mp_dev(r))

    def send_part(r, part):
        n.rsS[share(peers[r]), :] = part.astype(BF)
        scatter_copy(r).start()

    def send_tail(turn, part):
        n.rsS[tail, :] = part.astype(BF)
        for r in range(3):
            tail_copy(turn, r).start()

    def keep_own(part):
        n.own[...] = part

    def reduced(turn):
        for r in range(3):
            tail_copy(turn, r).wait_recv()
        for r in range(3):
            scatter_copy(r).wait_recv()
        total = n.own[:SHARE, :]
        rest = n.own[SHARE:, :].astype(BF).astype(F32)
        for r in range(3):
            total = total + n.rsR[r].astype(F32)
            rest = rest + n.rtR[turn, r].astype(F32)
        for r in range(3):
            scatter_copy(r).wait_send()
            tail_copy(turn, r).wait_send()
        return jnp.concatenate([total, rest], axis=0)

    def pack_rows(v):
        return jnp.concatenate([v[:PACK], v[PACK:]], axis=1)

    def pad_lanes(v):
        return jnp.concatenate([v, jnp.zeros_like(v)], axis=1)

    def chunk_rows(j, size):
        return pl.ds(pl.multiple_of(j * size, size), size)

    def chunk_send(stage, dest, l, j, pos, size, ss, rs):
        dest[l, s, chunk_rows(j, size), :] = stage[s, chunk_rows(j, size), :]
        for k in range(3):
            rcopy(
                stage.at[zs[k], chunk_rows(j, size)], dest.at[l, s, chunk_rows(j, size)],
                ss.at[k, pos], rs.at[k, pos], z_dev(k),
            ).start()

    def tail_send(stage, dest, l, start, size, ss, rs):
        dest[l, s, pl.ds(start, size), :] = stage[s, pl.ds(start, size), :]
        for k in range(3):
            rcopy(
                stage.at[zs[k], pl.ds(start, size)], dest.at[l, s, pl.ds(start, size)],
                ss.at[k, 4], rs.at[k, 4], z_dev(k),
            ).start()

    def chunk_wait(stage, dest, l, size, start, tail_size, ss, rs):
        order = (m,) + peers
        for k in range(3):
            for pos in range(4):
                cp = rcopy(
                    stage.at[zs[k], chunk_rows(order[pos], size)], dest.at[l, s, chunk_rows(order[pos], size)],
                    ss.at[k, pos], rs.at[k, pos], z_dev(k),
                )
                cp.wait()
            rcopy(
                stage.at[zs[k], pl.ds(start, tail_size)], dest.at[l, s, pl.ds(start, tail_size)],
                ss.at[k, 4], rs.at[k, 4], z_dev(k),
            ).wait()

    def back_copy(stage, dest, l, k, pos, size, tail_size, ss, rs):
        if pos == 4:
            rows = pl.ds(MP_N * size, tail_size)
        else:
            rows = chunk_rows(m if pos == 0 else peers[pos - 1], size)
        return rcopy(stage.at[zs[k], rows], dest.at[l, s, rows], ss.at[k, pos], rs.at[k, pos], z_dev(k))

    BACK_ORDER = (3, 1, 2, 0, 4)

    def back_send(stage, dest, l, size, tail_size, ss, rs):
        for pos in BACK_ORDER:
            for k in range(3):
                back_copy(stage, dest, l, k, pos, size, tail_size, ss, rs).start()
        dest[l, s] = stage[s]

    def back_wait(stage, dest, l, pos, size, tail_size, ss, rs):
        for k in range(3):
            back_copy(stage, dest, l, k, pos, size, tail_size, ss, rs).wait()

    def side_by_side(pieces, low):
        return jnp.concatenate([g[:, :HD] if low else g[:, HD:] for g in pieces], axis=1)

    def g_parts(l, seg):
        if seg == "o":
            return n.gbo.at[l], n.rAo.at[l], n.rBo.at[l]
        return n.gbq, n.rAp, n.rBq

    def g_copy(phase, l, seg):
        at = SEG_AT[seg]
        start, count = SEG[seg]
        rows = pl.ds(start, count)
        full, got, part = g_parts(l, seg)
        if phase == 0:
            dev = core_dev
            if seg in "du" and l == 0:
                src, dst = n.gb0.at[1 - c, rows], n.rA0.at[rows]
            elif seg in "du":
                src, dst = n.gb1.at[1 - c, :, rows], n.rA1.at[:, rows]
            else:
                src, dst = full.at[1 - c], got
        elif phase <= 2:
            b = 1 - z1 if phase == 1 else z1
            src, dst, dev = full.at[c, 1 - z0, b], part.at[b], z_dev(0)
        else:
            dev = z_dev(1)
            if seg in "du":
                rows = pl.ds(start + 512 * (phase - 3), 512)
                src = n.gb1.at[c, 1 - z1, rows]
            else:
                src = full.at[c, z0, 1 - z1]
            dst = n.rC.at[l, rows]
        return rcopy(src, dst, n.g_s.at[l, phase, at], n.g_r.at[l, phase, at], dev)

    def f(phase, l, seg):
        g_copy(phase, l, seg).start()

    def add_to(ref, got):
        ref[...] = (ref[...].astype(F32) + got[...].astype(F32)).astype(BF)

    def a(phase, l, seg):
        g_copy(phase, l, seg).wait()
        start, count = SEG[seg]
        rows = pl.ds(start, count)
        full, got, part = g_parts(l, seg)
        if phase == 0 and seg in "du" and l == 0:
            n.ob[l, rows, :] = (n.gb0[c, rows, :].astype(F32) + n.rA0[rows, :].astype(F32)).astype(BF)
        elif phase == 0:
            for b in range(2):
                if seg in "du":
                    add_to(n.gb1.at[c, b, rows], n.rA1.at[b, rows])
                else:
                    for i in range(2):
                        add_to(full.at[c, i, b], got.at[i, b])
        elif phase <= 2:
            b = 1 - z1 if phase == 1 else z1
            add_to(full.at[c, z0, b], part.at[b])
        else:
            if seg in "du":
                g_copy(4, l, seg).wait()
                mine = n.gb1[c, z1, rows, :]
            else:
                mine = full[c, z0, z1]
            n.ob[l, rows, :] = (mine.astype(F32) + n.rC[l, rows, :].astype(F32)).astype(BF)

    def partner_copy(buf, pos, ss, rs):
        if pos == 4:
            src, dst = tail, pl.ds(ROWS + MP_N * SHARE, TAIL)
        else:
            j = m if pos == 0 else peers[pos - 1]
            src, dst = share(j), pl.ds(pl.multiple_of(ROWS + j * SHARE, TAIL), SHARE)
        return rcopy(buf.at[src], buf.at[dst], ss.at[pos], rs.at[pos], z_dev(0))

    def block_copies(buf, k, ss, rs):
        at = ROWS * (k + 1)
        return (
            rcopy(buf.at[share(m)], buf.at[pl.ds(pl.multiple_of(at + m * SHARE, TAIL), SHARE)], ss.at[k, 0], rs.at[k, 0], z_dev(k)),
            rcopy(buf.at[tail], buf.at[pl.ds(at + MP_N * SHARE, TAIL)], ss.at[k, 1], rs.at[k, 1], z_dev(k)),
        )

    def pass_copy(buf, k, r, ss, rs):
        at = ROWS * (k + 1)
        if r < 2:
            rows = pl.ds(pl.multiple_of(at + m * SHARE, TAIL), SHARE)
            dev = mp_dev(r)
        else:
            rows = pl.ds(pl.multiple_of(at + peers[r - 2] * SHARE + (r - 2) * (SHARE // 2), TAIL), SHARE // 2)
            dev = mp_dev(3 - r)
        return rcopy(buf.at[rows], buf.at[rows], ss.at[k, r], rs.at[k, r], dev)

    def block_send(buf, ss, rs, which=(0, 1, 2)):
        for k in which:
            for cp in block_copies(buf, k, ss, rs):
                cp.start()

    def block_pass(buf, zss, zrs, ss, rs, which=(0, 1, 2)):
        for k in which:
            for cp in block_copies(buf, k, zss, zrs):
                cp.wait()
            for r in range(2):
                pass_copy(buf, k, r, ss, rs).start()

    def block_pass_on(buf, ss, rs, which=(0, 1, 2)):
        for k in which:
            for r in range(2):
                pass_copy(buf, k, r, ss, rs).wait()
                pass_copy(buf, k, r + 2, ss, rs).start()

    def block_wait(buf, ss, rs, which=(0, 1, 2)):
        for k in which:
            for r in range(2, 4):
                pass_copy(buf, k, r, ss, rs).wait()

    def others_forward(l):
        for pos in range(5):
            partner_copy(hin[l], pos, n.hp_s.at[l], n.hp_r.at[l]).wait()
        if l == 0:
            block_wait(hin[0], n.hf_s, n.hf_r, (1, 2))
        for k in range(3 if l == 0 else 1):
            rows = pl.ds(ROWS * (k + 1), ROWS)
            value, slope = gelu_pair(dot(hin[l][rows, :], n.wu[l]) + n.bu[pl.ds(l, 1), :])
            act[l][rows, :] = value.astype(BF)
            n.gprP[pl.ds(ROWS * k, ROWS), :] = slope.astype(BF)

    def others_backward(l):
        if l == 1:
            for pos in range(5):
                partner_copy(dob[1], pos, n.dp_s, n.dp_r).wait()
        else:
            block_wait(dob[0], n.df_s, n.df_r)
        for k in range(3 if l == 0 else 1):
            rows = pl.ds(ROWS * (k + 1), ROWS)
            n.dlf[rows, :] = (dot(dob[l][rows, :], n.wd[l], 1, 1) * n.gprP[pl.ds(ROWS * k, ROWS), :].astype(F32)).astype(BF)

    def half_columns(ref):
        return jnp.concatenate([ref[:, pl.ds(pl.multiple_of(z0 * 256 + 512 * b, 256), 256)] for b in range(2)], axis=1)

    def own_columns(ref):
        return ref[:, pl.ds(pl.multiple_of(s * 256, 256), 256)]

    def grad_down(l):
        if l == 1:
            grad = dot(act[1][...], half_columns(dob[1]), 0, 0).astype(BF)
            for k in range(4):
                n.gb1[k % 2, k // 2, pl.ds(0, 1024), :] = grad[:, 128 * k:128 * k + 128]
        else:
            grad = dot(own_columns(dob[0]), act[0][...], 0, 0).T.astype(BF)
            for k in range(2):
                n.gb0[k, pl.ds(0, 1024), :] = grad[:, 128 * k:128 * k + 128]
        f(0, l, "d")

    def grad_up(l):
        if l == 1:
            grad = dot(half_columns(hin[1]), n.dlf[:2 * ROWS, :], 0, 0).astype(BF)
        else:
            grad = dot(own_columns(hin[0]), n.dlf[...], 0, 0).astype(BF)
        for k in range(4 if l == 1 else 2):
            for t in range(8):
                piece = grad[128 * k:128 * k + 128, 128 * t:128 * t + 128]
                if l == 1:
                    n.gb1[k % 2, k // 2, pl.ds(1024 + 128 * t, 128), :] = piece
                else:
                    n.gb0[k, pl.ds(1024 + 128 * t, 128), :] = piece
        f(0, l, "u")

    def head_core():
        return rcopy(n.gq.at[1 - c], n.rAq, n.gq_s.at[3], n.gq_r.at[3], core_dev)

    def head_copies():
        return [rcopy(n.gq.at[c, zs[k]], n.rQ.at[s], n.gq_s.at[k], n.gq_r.at[k], z_dev(k)) for k in range(3)]

    def head_grad():
        block_wait(n.nrm0, n.nf_s, n.nf_r)
        grad = dot(n.eq[...], n.nrm0[...], 0, 0).astype(BF)
        for k in range(8):
            n.gq[k % 2, k // 2] = grad[:, 128 * k:128 * k + 128]
        head_core().start()

    def head_grad_send():
        head_core().wait()
        for z in range(SEQ_N):
            add_to(n.gq.at[c, z], n.rAq.at[z])
        for cp in head_copies():
            cp.start()
        n.rQ[s] = n.gq[c, s]

    def head_grad_last():
        for cp in head_copies():
            cp.wait()
        for t in range(6):
            rows = pl.ds(HD * (t // 2), HD)
            both = jnp.concatenate([n.rQ[2 * (t % 2), rows, :], n.rQ[2 * (t % 2) + 1, rows, :]], axis=0)
            n.ob[0, pl.ds(2304 + 128 * t, 128), :] = both.astype(F32).T.astype(BF)

    def hook(l, at):
        for step in SCHEDULE.get((l, at), ()):
            (f if step[0] == "f" else a)(int(step[1]), int(step[2]), step[3])

    def g_out(l):
        return [
            pltpu.make_async_copy(
                n.ob.at[l, pl.ds(GPIECE * t, GPIECE)],
                n.out_o.at[pl.ds(OUT_GRADS + GPIECE * l, GPIECE), pl.ds(128 * t, 128)],
                n.out.at[l, t],
            )
            for t in range(8)
        ]

    text_count = n.tl[0]

    def gelu_pair(u):
        uu = u * u
        t = jnp.tanh(SQRT_2_PI * (u + 0.044715 * u * uu))
        half = 0.5 * (1.0 + t)
        slope = half + 0.5 * u * (1.0 - t * t) * (SQRT_2_PI * (1.0 + 3 * 0.044715 * uu))
        return u * half, slope

    order_rows = lambda own_value, pos, buf: own_value if pos == 0 else buf[share(peers[pos - 1]), :]

    def forward(l, first):
        own_rows = ln(n.cur[...], l, 0).astype(BF)
        if first:
            pl.semaphore_wait(barrier, len(everyone))
        copies = gather_rows(nrm[l], own_rows)
        if first:
            loads[2].wait()
        for pos in range(4):
            if pos > 0:
                copies[pos - 1].wait_recv()
            rows = order_rows(own_rows, pos, nrm[l])
            q = dot(rows, n.wq[l, 0]) + n.bqv[l, pl.ds(0, 1), :]
            k = dot(rows, n.wq[l, 1])
            v = dot(rows, n.wq[l, 2]) + n.bqv[l, pl.ds(1, 1), :]
            j = m if pos == 0 else peers[pos - 1]
            at = pl.multiple_of(j * BLK, BLK)
            for h in range(SEQ_N):
                cut = slice(HD * h, HD * h + HD)
                n.qs[h, pl.ds(at, SHARE), :] = jnp.concatenate([q[:SHARE, cut], k[:SHARE, cut]], axis=1).astype(BF)
                n.qs[h, pl.ds(at + SHARE, PACK), :] = pack_rows(v[:SHARE, cut]).astype(BF)
                if pos == 0:
                    n.qs[h, pl.ds(MP_N * BLK, TAIL), :] = jnp.concatenate([q[SHARE:, cut], k[SHARE:, cut]], axis=1).astype(BF)
                    n.qs[h, pl.ds(MP_N * BLK + TAIL, TAIL), :] = pad_lanes(v[SHARE:, cut]).astype(BF)
            chunk_send(n.qs, n.qkvA, l, j, pos, BLK, n.qk_s, n.qk_r)
            if pos == 0:
                tail_send(n.qs, n.qkvA, l, MP_N * BLK, 2 * TAIL, n.qk_s, n.qk_r)
        for cp in copies:
            cp.wait_send()
        if not first:
            block_pass(hin[0], n.hz_s, n.hz_r, n.hf_s, n.hf_r, (1, 2))
        chunk_wait(n.qs, n.qkvA, l, BLK, MP_N * BLK, 2 * TAIL, n.qk_s, n.qk_r)
        for zb in range(SEQ_N):
            for j in range(MP_N):
                both = n.qkvA[l, zb, pl.ds(BLK * j, SHARE), :]
                vals = n.qkvA[l, zb, pl.ds(BLK * j + SHARE, PACK), :]
                at = ROWS * zb + SHARE * j
                n.q_s[l, pl.ds(at, SHARE), :] = both[:, :HD]
                n.k_s[l, pl.ds(at, SHARE), :] = both[:, HD:]
                n.v_s[l, pl.ds(at, PACK), :] = vals[:, :HD]
                n.v_s[l, pl.ds(at + PACK, PACK), :] = vals[:, HD:]
            both = n.qkvA[l, zb, pl.ds(BLK * MP_N, TAIL), :]
            vals = n.qkvA[l, zb, pl.ds(BLK * MP_N + TAIL, TAIL), :]
            at = ROWS * zb + SHARE * MP_N
            n.q_s[l, pl.ds(at, TAIL), :] = both[:, :HD]
            n.k_s[l, pl.ds(at, TAIL), :] = both[:, HD:]
            n.v_s[l, pl.ds(at, TAIL), :] = vals[:, :HD]
        for i in range(SEQ_N):
            width = ROWS * (i + 1)
            st = dot(n.k_s[l, pl.ds(0, width), :], n.q_s[l, pl.ds(ROWS * i, ROWS), :], 1, 1) * SCORE_SCALE
            key_at = lax.broadcasted_iota(jnp.int32, (ROWS, ROWS), 0)
            query_at = lax.broadcasted_iota(jnp.int32, (ROWS, ROWS), 1)
            causal = key_at <= query_at
            if i == 0:
                st = jnp.where(causal & ((key_at >= TEXT) | (key_at < text_count)), st, -1e30)
            else:
                text_at = lax.broadcasted_iota(jnp.int32, (TEXT, ROWS), 0)
                st = jnp.concatenate([
                    jnp.where(text_at < text_count, st[:TEXT], -1e30),
                    st[TEXT:ROWS * i],
                    jnp.where(causal, st[ROWS * i:], -1e30),
                ], axis=0)
            e = jnp.exp(st - jnp.max(st, axis=0, keepdims=True))
            p = (e * (1.0 / jnp.sum(e, axis=0, keepdims=True))).astype(BF)
            pts[i][l] = p
            o = dot(n.v_s[l, pl.ds(0, width), :], p, 0, 0).T
            for j in range(MP_N):
                n.os_[i, pl.ds(PACK * j, PACK), :] = pack_rows(o[SHARE * j:SHARE * j + SHARE]).astype(BF)
            n.os_[i, pl.ds(PACK * MP_N, TAIL), :] = pad_lanes(o[SHARE * MP_N:]).astype(BF)
        back_send(n.os_, n.oA, l, PACK, TAIL, n.o_s, n.o_r)
        if not first:
            block_pass_on(hin[0], n.hf_s, n.hf_r, (1, 2))
        if first:
            loads[3].wait()
        for pos in BACK_ORDER[:4]:
            back_wait(n.os_, n.oA, l, pos, PACK, TAIL, n.o_s, n.o_r)
            j = m if pos == 0 else peers[pos - 1]
            got = [n.oA[l, h, chunk_rows(j, PACK), :] for h in range(SEQ_N)]
            rows = jnp.concatenate([side_by_side(got, True), side_by_side(got, False)], axis=0)
            n.att[l, share(j), :] = rows
            if pos > 0:
                send_part(pos - 1, dot(rows, n.wo[l]))
            else:
                back_wait(n.os_, n.oA, l, 4, PACK, TAIL, n.o_s, n.o_r)
                got = [n.oA[l, h, pl.ds(PACK * MP_N, TAIL), :] for h in range(SEQ_N)]
                rest = side_by_side(got, True)
                n.att[l, tail, :] = rest
                part = dot(jnp.concatenate([rows, rest], axis=0), n.wo[l])
                send_tail(0, part[SHARE:])
                keep_own(part)
        if not first:
            block_send(n.nrm0, n.nz_s, n.nz_r)
        branch = reduced(0) + n.bo[pl.ds(l, 1), :]
        settled = n.cur[...] + ln(branch, l, 1)
        n.stl[...] = settled
        own_rows = ln(settled, l, 2).astype(BF)
        copies = gather_rows(hin[l], own_rows)
        if first:
            block_send(hin[0], n.hz_s, n.hz_r, (1, 2))
        partner_copy(hin[l], 0, n.hp_s.at[l], n.hp_r.at[l]).start()
        partner_copy(hin[l], 4, n.hp_s.at[l], n.hp_r.at[l]).start()
        if first:
            loads[4].wait()
            loads[5].wait()
        for pos in range(4):
            if pos > 0:
                copies[pos - 1].wait_recv()
                partner_copy(hin[l], pos, n.hp_s.at[l], n.hp_r.at[l]).start()
            rows = order_rows(own_rows, pos, hin[l])
            value, slope = gelu_pair(dot(rows, n.wu[l]) + n.bu[pl.ds(l, 1), :])
            value = value.astype(BF)
            j = m if pos == 0 else peers[pos - 1]
            act[l][share(j), :] = value[:SHARE]
            n.gpr[l, share(j), :] = slope[:SHARE]
            part = dot(value, n.wd[l])
            if pos == 0:
                act[l][tail, :] = value[SHARE:]
                n.gpr[l, tail, :] = slope[SHARE:]
                send_tail(1, part[SHARE:])
                keep_own(part)
            else:
                send_part(pos - 1, part)
        for cp in copies:
            cp.wait_send()
        out_branch = reduced(1) + n.bd[pl.ds(l, 1), :]
        n.cur[...] = n.stl[...] + ln(out_branch, l, 3)

    result_copies = []

    def final_rows(which, stage):
        copies = []
        out = n.out_o.at[pl.ds(ROWS * which, ROWS)]
        for r in range(3):
            copies.append(rcopy(stage.at[pl.ds(0, SHARE)], out.at[share(m)], n.fr_s.at[which, r], n.fr_r.at[which, r], mp_dev(r)))
        copies.append(pltpu.make_async_copy(stage.at[pl.ds(0, SHARE)], out.at[share(m)], n.fl.at[which, 0]))
        copies.append(pltpu.make_async_copy(stage.at[pl.ds(SHARE, TAIL)], out.at[pl.ds(MP_N * SHARE, TAIL)], n.fl.at[which, 1]))
        for cp in copies:
            cp.start()
        return copies

    def backward(l):
        grad_rows = n.grd[...]
        d_ob = ln_back(l, 3, grad_rows).astype(BF)
        copies = gather_rows(dob[l], d_ob)
        if l == 1:
            partner_copy(dob[1], 0, n.dp_s, n.dp_r).start()
            partner_copy(dob[1], 4, n.dp_s, n.dp_r).start()
        else:
            block_send(dob[0], n.dz_s, n.dz_r)
        ln_params(l, 3, grad_rows)
        n.sg[l, pl.ds(9, 1), :] = jnp.sum(d_ob.astype(F32) * counted, axis=0, keepdims=True)
        hook(l, 0)
        for pos in range(4):
            if pos > 0:
                copies[pos - 1].wait_recv()
                if l == 1:
                    partner_copy(dob[1], pos, n.dp_s, n.dp_r).start()
            rows = order_rows(d_ob, pos, dob[l])
            j = m if pos == 0 else peers[pos - 1]
            slope = n.gpr[l, share(j), :]
            if pos == 0:
                slope = jnp.concatenate([slope, n.gpr[l, tail, :]], axis=0)
            d_l = (dot(rows, n.wd[l], 1, 1) * slope).astype(BF)
            n.dlf[share(j), :] = d_l[:SHARE]
            part = dot(d_l, n.wu[l], 1, 1)
            if pos == 0:
                n.dlf[tail, :] = d_l[SHARE:]
                send_tail(0, part[SHARE:])
                keep_own(part)
                if l == 1:
                    others_forward(1)
            else:
                send_part(pos - 1, part)
        for cp in copies:
            cp.wait_send()
        hook(l, 1)
        n.sg[l, pl.ds(10, 1), :] = jnp.sum(n.dlf[:ROWS, :].astype(F32), axis=0, keepdims=True)
        hook(l, 2)
        d_hidden = reduced(0)
        d_settled = grad_rows + ln_back(l, 2, d_hidden)
        d_br = ln_back(l, 1, d_settled).astype(BF)
        copies = gather_rows(n.dbr, d_br)
        n.stl[...] = d_settled
        ln_params(l, 2, d_hidden)
        ln_params(l, 1, d_settled)
        n.sg[l, pl.ds(8, 1), :] = jnp.sum(d_br.astype(F32) * counted, axis=0, keepdims=True)
        hook(l, 3)
        for pos in range(4):
            if pos > 0:
                copies[pos - 1].wait_recv()
            rows = order_rows(d_br, pos, n.dbr)
            j = m if pos == 0 else peers[pos - 1]
            d_at = dot(rows, n.wo[l], 1, 1)
            for h in range(SEQ_N):
                cut = slice(HD * h, HD * h + HD)
                n.ds_[h, chunk_rows(j, PACK), :] = pack_rows(d_at[:SHARE, cut]).astype(BF)
                if pos == 0:
                    n.ds_[h, pl.ds(MP_N * PACK, TAIL), :] = pad_lanes(d_at[SHARE:, cut]).astype(BF)
            chunk_send(n.ds_, n.dA, l, j, pos, PACK, n.do_ss, n.do_r)
            if pos == 0:
                tail_send(n.ds_, n.dA, l, MP_N * PACK, TAIL, n.do_ss, n.do_r)
                if l == 1:
                    others_backward(1)
                    grad_down(1)
                hook(l, 31)
        for cp in copies:
            cp.wait_send()
        hook(l, 4)
        if l == 1:
            grad_up(1)
            block_pass(n.nrm0, n.nz_s, n.nz_r, n.nf_s, n.nf_r)
        else:
            block_pass(dob[0], n.dz_s, n.dz_r, n.df_s, n.df_r)
        grad = dot(n.att[l], n.dbr[...], 0, 0).astype(BF)
        for k in range(8):
            n.gbo[l, k % 2, (k // 2) % 2, k // 4] = grad[:, 128 * k:128 * k + 128]
        f(0, l, "o")
        hook(l, 5)
        chunk_wait(n.ds_, n.dA, l, PACK, MP_N * PACK, TAIL, n.do_ss, n.do_r)
        for zb in range(SEQ_N):
            for j in range(MP_N):
                vals = n.dA[l, zb, pl.ds(PACK * j, PACK), :]
                at = ROWS * zb + SHARE * j
                n.do_s[pl.ds(at, PACK), :] = vals[:, :HD]
                n.do_s[pl.ds(at + PACK, PACK), :] = vals[:, HD:]
            n.do_s[pl.ds(ROWS * zb + SHARE * MP_N, TAIL), :] = n.dA[l, zb, pl.ds(PACK * MP_N, TAIL), :][:, :HD]
        hook(l, 6)
        for i in reversed(range(SEQ_N)):
            width = ROWS * (i + 1)
            here = pl.ds(ROWS * i, ROWS)
            p = pts[i][l]
            dpt = dot(n.v_s[l, pl.ds(0, width), :], n.do_s[here, :], 1, 1)
            pf = p.astype(F32)
            mean_term = jnp.sum(pf * dpt, axis=0, keepdims=True)
            dst = (pf * (dpt - mean_term)).astype(BF)
            dv = dot(p, n.do_s[here, :])
            dk = dot(dst, n.q_s[l, here, :])
            if i < SEQ_N - 1:
                dv = dv + n.dv_s[pl.ds(0, width), :]
                dk = dk + n.dk_s[pl.ds(0, width), :]
            if i > 0:
                n.dv_s[pl.ds(0, ROWS * i), :] = dv[:ROWS * i]
                n.dk_s[pl.ds(0, ROWS * i), :] = dk[:ROWS * i]
            dq = dot(n.k_s[l, pl.ds(0, width), :], dst, 0, 0).T * SCORE_SCALE
            dk = dk[ROWS * i:] * SCORE_SCALE
            dv = dv[ROWS * i:]
            if l == 0:
                place = (z0 if i % 2 == 0 else 1 - z0) + 2 * (z1 if i < 2 else 1 - z1)
                at = pl.ds(pl.multiple_of(place * ROWS, TAIL), ROWS)
                n.eq[at, pl.ds(0, 2 * HD)] = jnp.concatenate([dq, dk], axis=1).astype(BF)
                n.eq[at, pl.ds(2 * HD, HD)] = dv.astype(BF)
            for j in range(MP_N):
                cut = slice(SHARE * j, SHARE * j + SHARE)
                n.es[i, pl.ds(BLK * j, SHARE), :] = jnp.concatenate([dq[cut], dk[cut]], axis=1).astype(BF)
                n.es[i, pl.ds(BLK * j + SHARE, PACK), :] = pack_rows(dv[cut]).astype(BF)
            cut = slice(SHARE * MP_N, ROWS)
            n.es[i, pl.ds(BLK * MP_N, TAIL), :] = jnp.concatenate([dq[cut], dk[cut]], axis=1).astype(BF)
            n.es[i, pl.ds(BLK * MP_N + TAIL, TAIL), :] = pad_lanes(dv[cut]).astype(BF)
        back_send(n.es, n.eA, l, BLK, 2 * TAIL, n.e_s, n.e_r)
        hook(l, 7)
        if l == 1:
            others_forward(0)
            block_pass_on(n.nrm0, n.nf_s, n.nf_r)
        else:
            head_grad()
            block_pass_on(dob[0], n.df_s, n.df_r)

        def d_norm_part(rows):
            total = dot(rows[0], n.wq[l, 0], 1, 1)
            total = total + dot(rows[1], n.wq[l, 1], 1, 1)
            return total + dot(rows[2], n.wq[l, 2], 1, 1)

        for pos in BACK_ORDER[:4]:
            back_wait(n.es, n.eA, l, pos, BLK, 2 * TAIL, n.e_s, n.e_r)
            j = m if pos == 0 else peers[pos - 1]
            at = pl.multiple_of(j * BLK, BLK)
            both = [n.eA[l, h, pl.ds(at, SHARE), :] for h in range(SEQ_N)]
            vals = [n.eA[l, h, pl.ds(at + SHARE, PACK), :] for h in range(SEQ_N)]
            rows = [side_by_side(both, True), side_by_side(both, False)]
            rows.append(jnp.concatenate([side_by_side(vals, True), side_by_side(vals, False)], axis=0))
            for t in range(3):
                n.dpr[share(j), pl.ds(COLS * t, COLS)] = rows[t]
            if pos > 0:
                send_part(pos - 1, d_norm_part(rows))
            else:
                back_wait(n.es, n.eA, l, 4, BLK, 2 * TAIL, n.e_s, n.e_r)
                both = [n.eA[l, h, pl.ds(BLK * MP_N, TAIL), :] for h in range(SEQ_N)]
                vals = [n.eA[l, h, pl.ds(BLK * MP_N + TAIL, TAIL), :] for h in range(SEQ_N)]
                rest = [side_by_side(both, True), side_by_side(both, False), side_by_side(vals, True)]
                for t in range(3):
                    n.dpr[tail, pl.ds(COLS * t, COLS)] = rest[t]
                part = d_norm_part([jnp.concatenate([rows[t], rest[t]], axis=0) for t in range(3)])
                send_tail(1, part[SHARE:])
                keep_own(part)
        hook(l, 70)
        if l == 1:
            result_copies.extend(final_rows(0, n.resb))
        if l == 0:
            head_grad_send()
        if l == 1:
            grad = dot(nrm[l][...], n.dpr[...], 0, 0).astype(BF)
            for k in range(8):
                for t in range(6):
                    n.gbq[k % 2, (k // 2) % 2, k // 4, pl.ds(128 * t, 128), :] = grad[128 * k:128 * k + 128, 128 * t:128 * t + 128]
            f(0, l, "q")
        sums = jnp.sum(n.dpr[...].astype(F32), axis=0, keepdims=True)
        blank = jnp.zeros((1, 96), F32)
        for at, lane in ((11, 0), (12, 2 * COLS)):
            pieces = []
            for k in range(8):
                pieces += [sums[:, lane + 32 * k:lane + 32 * k + 32], blank]
            n.sg[l, pl.ds(at, 1), :] = jnp.concatenate(pieces, axis=1)
        n.sg[l, pl.ds(13, 3), :] = jnp.zeros((3, D), F32)
        hook(l, 8)
        d_norm = reduced(1)
        n.grd[...] = n.stl[...] + ln_back(l, 0, d_norm)
        ln_params(l, 0, d_norm)
        hook(l, 9)

    forward(0, True)
    forward(1, False)
    n.resb[...] = n.cur[...].astype(BF)
    loads[6].wait()
    loads[7].wait()
    backward(1)
    backward(0)
    n.gstb[...] = n.grd[...].astype(BF)
    grad_copies = final_rows(1, n.gstb)

    small = []
    for t, dev in enumerate(group):
        lanes = pl.ds(pl.multiple_of((dev[0] * 2 + dev[1]) * 128, 128), 128)
        cp = rcopy(n.sg.at[:, :, lanes], n.smR.at[t], n.sm_s.at[t], n.sm_r.at[t], dev)
        cp.start()
        small.append(cp)
    others_backward(0)
    grad_down(0)
    grad_up(0)
    hook(2, 0)
    head_grad_last()
    for cp in small:
        cp.wait()
    total = n.sg[:, :, pl.ds(pl.multiple_of((s * 2 + c) * 128, 128), 128)]
    for t in range(7):
        total = total + n.smR[t]
    n.smS[...] = total
    small = []
    for r in range(3):
        cp = rcopy(n.smS, n.smM.at[r], n.sn_s.at[r], n.sn_r.at[r], mp_dev(r))
        cp.start()
        small.append(cp)
    hook(2, 1)
    for cp in small:
        cp.wait()
    shared = lax.broadcasted_iota(jnp.int32, (2, SMALL, 128), 1) < 10
    total = total + jnp.where(shared, n.smM[0] + n.smM[1] + n.smM[2], 0.0)
    high = total.astype(BF)
    rest = (total - high.astype(F32)).astype(BF)
    n.sb[...] = jnp.zeros((16, D), BF)
    for l in range(2):
        n.sb[:, pl.ds(256 * l, 128)] = high[l]
        n.sb[:, pl.ds(256 * l + 128, 128)] = rest[l]
    last = [pltpu.make_async_copy(n.sb, n.out_o.at[pl.ds(OUT_SMALL, 16)], n.so.at[0])]
    last[0].start()
    hook(2, 2)
    for cp in g_out(0) + g_out(1):
        cp.start()
        last.append(cp)
    for cp in last + result_copies + grad_copies:
        cp.wait()


def finish_kernel(packed, res_o, gst_o, gain_o, shift_o, gq_o, qv_o, go_o, bo_o, gu_o, bu_o, gd_o, bd_o):
    res_o[...] = packed[:ROWS, :].astype(F32)
    gst_o[...] = packed[ROWS:2 * ROWS, :].astype(F32)
    for l in range(2):
        for b in range(24):
            lanes = slice(128 * (b // 3), 128 * (b // 3) + 128)
            start = OUT_GRADS + GPIECE * l + 128 * (b % 3)
            value = packed[start:start + 128, lanes].astype(F32)
            if b < 8:
                gd_o[l, 128 * b:128 * b + 128, :] = value
            elif b < 16:
                gu_o[l, :, 128 * (b - 8):128 * (b - 8) + 128] = value
            elif b < 18:
                go_o[l, 128 * (b - 16):128 * (b - 16) + 128, :] = value
            else:
                at = b - 18
                gq_o[l, at // 2, :, 128 * (at % 2):128 * (at % 2) + 128] = value
        small = packed[OUT_SMALL:OUT_SMALL + 16, 256 * l:256 * l + 128].astype(F32)
        small = small + packed[OUT_SMALL:OUT_SMALL + 16, 256 * l + 128:256 * l + 256].astype(F32)
        gain_o[l] = small[0:4]
        shift_o[l] = small[4:8]
        qv_o[l] = small[11:13, :32]
        bo_o[l:l + 1, :] = small[8:9]
        bd_o[l:l + 1, :] = small[9:10]
        bu_o[l:l + 1, :] = small[10:11]


def fused_shards(
    stream, text_len, norm_gain, norm_shift, w_qkv, bias_qv, w_out, bias_out, w_up, bias_up, w_down, bias_down, cotangent
):
    rows = (ROWS, D)
    any_space = pl.BlockSpec(memory_space=pl.ANY)
    vmem = pl.BlockSpec(memory_space=pltpu.VMEM)
    smem = pl.BlockSpec(memory_space=pltpu.SMEM)
    packed = pl.pallas_call(
        fused_kernel,
        out_shape=jax.ShapeDtypeStruct((OUT_ROWS, D), BF),
        in_specs=[smem, any_space, any_space, vmem, vmem, vmem, vmem, vmem, vmem] + [any_space] * 4,
        out_specs=any_space,
        scratch_shapes=[pltpu.VMEM(shape, dtype) for shape, dtype in VMEM_SCRATCH.values()]
        + [pltpu.SemaphoreType.DMA(shape) for shape in DMA_SEMS.values()],
        compiler_params=pltpu.CompilerParams(
            collective_id=0, has_side_effects=True, vmem_limit_bytes=63 * 2**20
        ),
    )(
        text_len,
        stream.reshape(rows),
        cotangent.reshape(rows),
        norm_gain,
        norm_shift,
        bias_qv,
        bias_out,
        bias_up,
        bias_down,
        w_qkv.transpose(0, 2, 1, 3),
        w_out,
        w_up,
        w_down,
    )
    shape = lambda *dims: jax.ShapeDtypeStruct(dims, F32)
    done = pl.pallas_call(
        finish_kernel,
        out_shape=(
            shape(*rows), shape(*rows), shape(2, 4, 128), shape(2, 4, 128), shape(2, 3, 128, COLS), shape(2, 2, 32),
            shape(2, COLS, 128), shape(2, 128), shape(2, 128, FFL), shape(2, 128), shape(2, FFL, 128), shape(2, 128),
        ),
        in_specs=[vmem],
        out_specs=[vmem] * 12,
        compiler_params=pltpu.CompilerParams(vmem_limit_bytes=32 * 2**20),
    )(packed)
    return (
        done[0].reshape(1, ROWS, D),
        done[1].reshape(1, ROWS, D),
        done[2],
        done[3],
        done[4].transpose(0, 2, 1, 3),
    ) + tuple(done[5:])


def solution(mesh):
    return jax.shard_map(
        fused_shards if fits(mesh) else shards,
        mesh=mesh,
        in_specs=(
            P("dp", "seq", None),
            P("dp"),
            P(),
            P(),
            P(None, None, None, "mp"),
            P(None, None, "mp"),
            P(None, "mp", None),
            P(),
            P(None, None, "mp"),
            P(None, "mp"),
            P(None, "mp", None),
            P(),
            P("dp", "seq", None),
        ),
        out_specs=(
            P("dp", "seq", None),
            P("dp", "seq", None),
            P(None, None, ("seq", "dp")),
            P(None, None, ("seq", "dp")),
            P(None, ("seq", "dp"), None, "mp"),
            P(None, None, ("mp", "seq", "dp")),
            P(None, "mp", ("seq", "dp")),
            P(None, ("seq", "dp")),
            P(None, ("seq", "dp"), "mp"),
            P(None, ("mp", "seq", "dp")),
            P(None, "mp", ("seq", "dp")),
            P(None, ("seq", "dp")),
        ),
        check_vma=False,
    )
```

```python
from functools import partial
import math

import jax
import jax.numpy as jnp
from jax import lax
from jax.experimental import pallas as pl
from jax.experimental.pallas import tpu as pltpu
from jax.sharding import PartitionSpec as P

D = 1024
HEADS = 16
TEXT = 64


relax_alpha = 32.0
norm_eps = 1e-05


def layer_norm(row_values, gain_row, shift_row):
    row_mean = jnp.mean(row_values, axis=-1, keepdims=True)
    centred = row_values - row_mean
    variance = jnp.mean(centred * centred, axis=-1, keepdims=True)
    return centred * lax.rsqrt(variance + norm_eps) * gain_row + shift_row


def norm_back(row_values, gain_row, shift_row, grad_rows):
    result_value, pull_back = jax.vjp(layer_norm, row_values, gain_row, shift_row)
    return pull_back(grad_rows)


def reduce_rows(partial_sum):
    return lax.psum_scatter(
        partial_sum.astype(jnp.bfloat16), "mp", scatter_dimension=0, tiled=True
    ).astype(jnp.float32)


def widen_rows(row_values):
    return lax.all_gather(row_values, "mp", axis=0, tiled=True)


def reduce_grads(partial_sum):
    return lax.psum_scatter(
        partial_sum.astype(jnp.bfloat16), "mp", scatter_dimension=0, tiled=True
    ).astype(jnp.float32)


def widen_grads(row_values):
    return lax.all_gather(row_values, "mp", axis=0, tiled=True)


def relaxed_scores(query_heads, key_heads, allowed, score_scale):
    raw_scores = (
        jnp.einsum("sqhe,skhe->shqk", query_heads, key_heads, preferred_element_type=jnp.float32)
        * score_scale
    )
    return jnp.where(allowed, raw_scores / relax_alpha, -1e30)


def shards(
    stream,
    text_len,
    norm_gain,
    norm_shift,
    w_qkv,
    bias_qv,
    w_out,
    bias_out,
    w_up,
    bias_up,
    w_down,
    bias_down,
    cotangent,
):
    seq_count, block_len, model_width = stream.shape
    rows_all = seq_count * block_len
    layers = w_qkv.shape[0]
    local_cols = w_qkv.shape[3]
    head_dim = D // HEADS
    heads_here = local_cols // head_dim
    score_scale = 1.0 / math.sqrt(head_dim)
    share_rows = rows_all // lax.axis_size("mp")
    first_row = lax.axis_index("mp") * share_rows
    block_start = lax.axis_index("seq") * block_len
    seq_span = block_len * lax.axis_size("seq")
    query_pos = block_start + jnp.arange(block_len, dtype=jnp.int32)
    key_pos = jnp.arange(seq_span, dtype=jnp.int32)
    causal = key_pos[None, :] <= query_pos[:, None]
    visible = (key_pos[None, :] >= TEXT) | (key_pos[None, :] < text_len[:, None])
    allowed = causal[None, None] & visible[:, None, None, :]
    flat_rows = stream.reshape(rows_all, model_width)
    grad_rows = cotangent.reshape(rows_all, model_width)
    current = lax.dynamic_slice_in_dim(flat_rows, first_row, share_rows, 0)
    grad_rows = lax.dynamic_slice_in_dim(grad_rows, first_row, share_rows, 0)
    gelu_tanh = partial(jax.nn.gelu, approximate=True)
    kept_state = []
    for layer_at in range(layers):
        gain_rows = norm_gain[layer_at]
        shift_rows = norm_shift[layer_at]
        normed = widen_rows(layer_norm(current, gain_rows[0], shift_rows[0]).astype(jnp.bfloat16))
        projected = jnp.einsum(
            "td,dcf->tcf", normed, w_qkv[layer_at], preferred_element_type=jnp.float32
        )
        queries = (projected[:, 0] + bias_qv[layer_at, 0]).astype(jnp.bfloat16)
        key_rows = projected[:, 1].astype(jnp.bfloat16)
        value_rows = (projected[:, 2] + bias_qv[layer_at, 1]).astype(jnp.bfloat16)
        keys_all, values_all = (
            lax.all_gather(
                key_rows.reshape(seq_count, block_len, local_cols), "seq", axis=1, tiled=True
            ),
            lax.all_gather(
                value_rows.reshape(seq_count, block_len, local_cols), "seq", axis=1, tiled=True
            ),
        )
        query_heads = queries.reshape(seq_count, block_len, heads_here, head_dim)
        key_heads = keys_all.reshape(seq_count, seq_span, heads_here, head_dim)
        value_heads = values_all.reshape(seq_count, seq_span, heads_here, head_dim)
        tempered = relaxed_scores(query_heads, key_heads, allowed, score_scale)
        highest = jnp.max(tempered, axis=-1, keepdims=True)
        exponent = jnp.exp(relax_alpha * (tempered - highest))
        totals = jnp.sum(exponent, axis=-1, keepdims=True)
        log_total = relax_alpha * highest + jnp.log(totals)
        weights = (exponent / totals).astype(jnp.bfloat16)
        attended = jnp.einsum(
            "shqk,skhe->sqhe", weights, value_heads, preferred_element_type=jnp.float32
        )
        attended = attended.astype(jnp.bfloat16).reshape(rows_all, local_cols)
        branch = (
            reduce_rows(jnp.dot(attended, w_out[layer_at], preferred_element_type=jnp.float32))
            + bias_out[layer_at]
        )
        settled = current + layer_norm(branch, gain_rows[1], shift_rows[1])
        hidden_in = widen_rows(
            layer_norm(settled, gain_rows[2], shift_rows[2]).astype(jnp.bfloat16)
        )
        lifted = (
            jnp.dot(hidden_in, w_up[layer_at], preferred_element_type=jnp.float32)
            + bias_up[layer_at]
        )
        activated = gelu_tanh(lifted).astype(jnp.bfloat16)
        output_branch = (
            reduce_rows(jnp.dot(activated, w_down[layer_at], preferred_element_type=jnp.float32))
            + bias_down[layer_at]
        )
        kept_state.append(
            (
                current,
                normed,
                query_heads,
                key_heads,
                value_heads,
                log_total,
                attended,
                branch,
                settled,
                hidden_in,
                lifted,
                activated,
                output_branch,
            )
        )
        current = settled + layer_norm(output_branch, gain_rows[3], shift_rows[3])
    collected = []
    for layer_at in reversed(range(layers)):
        (
            layer_in,
            normed,
            query_heads,
            key_heads,
            value_heads,
            log_total,
            attended,
            branch,
            settled,
            hidden_in,
            lifted,
            activated,
            output_branch,
        ) = kept_state[layer_at]
        gain_rows = norm_gain[layer_at]
        shift_rows = norm_shift[layer_at]
        d_out_branch, gain_three, shift_three = norm_back(
            output_branch, gain_rows[3], shift_rows[3], grad_rows
        )
        d_out_branch = d_out_branch.astype(jnp.bfloat16)
        d_bias_down = jnp.sum(d_out_branch.astype(jnp.float32), axis=0)
        d_down_full = widen_grads(d_out_branch)
        d_w_down = jnp.einsum(
            "tf,td->fd", activated, d_down_full, preferred_element_type=jnp.float32
        )
        d_activated = jnp.einsum(
            "td,fd->tf", d_down_full, w_down[layer_at], preferred_element_type=jnp.float32
        )
        gelu_value, gelu_pull = jax.vjp(gelu_tanh, lifted)
        d_lifted = gelu_pull(d_activated)[0].astype(jnp.bfloat16)
        d_bias_up = jnp.sum(d_lifted.astype(jnp.float32), axis=0)
        d_w_up = jnp.einsum("td,tf->df", hidden_in, d_lifted, preferred_element_type=jnp.float32)
        d_hidden = reduce_grads(
            jnp.einsum("tf,df->td", d_lifted, w_up[layer_at], preferred_element_type=jnp.float32)
        )
        d_norm_two, gain_two, shift_two = norm_back(settled, gain_rows[2], shift_rows[2], d_hidden)
        d_settled = grad_rows + d_norm_two
        d_branch, gain_one, shift_one = norm_back(branch, gain_rows[1], shift_rows[1], d_settled)
        d_branch = d_branch.astype(jnp.bfloat16)
        d_bias_out = jnp.sum(d_branch.astype(jnp.float32), axis=0)
        d_branch_full = widen_grads(d_branch)
        d_w_out = jnp.einsum(
            "tf,td->fd", attended, d_branch_full, preferred_element_type=jnp.float32
        )
        d_attended = jnp.einsum(
            "td,fd->tf", d_branch_full, w_out[layer_at], preferred_element_type=jnp.float32
        )
        d_attended = d_attended.astype(jnp.bfloat16).reshape(
            seq_count, block_len, heads_here, head_dim
        )
        tempered = relaxed_scores(query_heads, key_heads, allowed, score_scale)
        probabilities = jnp.exp(relax_alpha * tempered - log_total)
        d_probs = jnp.einsum(
            "sqhe,skhe->shqk", d_attended, value_heads, preferred_element_type=jnp.float32
        )
        d_values = jnp.einsum(
            "shqk,sqhe->skhe",
            probabilities.astype(jnp.bfloat16),
            d_attended,
            preferred_element_type=jnp.float32,
        )
        mean_term = jnp.sum(probabilities * d_probs, axis=-1, keepdims=True)
        d_raw = (probabilities * (d_probs - mean_term)).astype(jnp.bfloat16)
        d_queries = (
            jnp.einsum("shqk,skhe->sqhe", d_raw, key_heads, preferred_element_type=jnp.float32)
            * score_scale
        )
        d_keys = (
            jnp.einsum("shqk,sqhe->skhe", d_raw, query_heads, preferred_element_type=jnp.float32)
            * score_scale
        )
        d_keys_own, d_values_own = (
            lax.psum_scatter(
                d_keys.reshape(seq_count, seq_span, local_cols).astype(jnp.bfloat16),
                "seq",
                scatter_dimension=1,
                tiled=True,
            ).astype(jnp.float32),
            lax.psum_scatter(
                d_values.reshape(seq_count, seq_span, local_cols).astype(jnp.bfloat16),
                "seq",
                scatter_dimension=1,
                tiled=True,
            ).astype(jnp.float32),
        )
        d_queries = d_queries.reshape(rows_all, local_cols).astype(jnp.bfloat16)
        d_keys_own = d_keys_own.reshape(rows_all, local_cols).astype(jnp.bfloat16)
        d_values_own = d_values_own.reshape(rows_all, local_cols).astype(jnp.bfloat16)
        d_bias_qv = jnp.stack(
            [
                jnp.sum(d_queries.astype(jnp.float32), axis=0),
                jnp.sum(d_values_own.astype(jnp.float32), axis=0),
            ]
        )
        d_projected = jnp.stack([d_queries, d_keys_own, d_values_own], axis=1)
        d_w_qkv = jnp.einsum("td,tcf->dcf", normed, d_projected, preferred_element_type=jnp.float32)
        d_normed = reduce_grads(
            jnp.einsum(
                "tcf,dcf->td", d_projected, w_qkv[layer_at], preferred_element_type=jnp.float32
            )
        )
        d_layer_in, gain_zero, shift_zero = norm_back(
            layer_in, gain_rows[0], shift_rows[0], d_normed
        )
        grad_rows = d_settled + d_layer_in
        collected.append(
            (
                jnp.stack([gain_zero, gain_one, gain_two, gain_three]),
                jnp.stack([shift_zero, shift_one, shift_two, shift_three]),
                d_w_qkv,
                d_bias_qv,
                d_w_out,
                d_bias_out,
                d_w_up,
                d_bias_up,
                d_w_down,
                d_bias_down,
            )
        )
    collected = collected[::-1]
    stacked = tuple((jnp.stack([entry[index_at] for entry in collected]) for index_at in range(10)))
    (
        gain_grads,
        shift_grads,
        grad_qkv,
        grad_qv,
        grad_out_w,
        grad_out_b,
        grad_up_w,
        grad_up_b,
        grad_down_w,
        grad_down_b,
    ) = stacked
    gain_grads, shift_grads, grad_out_b, grad_down_b = (
        lax.psum(gain_grads.astype(jnp.bfloat16), "mp").astype(jnp.float32),
        lax.psum(shift_grads.astype(jnp.bfloat16), "mp").astype(jnp.float32),
        lax.psum(grad_out_b.astype(jnp.bfloat16), "mp").astype(jnp.float32),
        lax.psum(grad_down_b.astype(jnp.bfloat16), "mp").astype(jnp.float32),
    )
    current, grad_rows = (
        lax.all_gather(current.astype(jnp.bfloat16), "mp", axis=0, tiled=True).astype(
            current.dtype
        ),
        lax.all_gather(grad_rows.astype(jnp.bfloat16), "mp", axis=0, tiled=True).astype(
            grad_rows.dtype
        ),
    )
    summed = (
        lax.psum_scatter(
            gain_grads.astype(jnp.bfloat16), ("seq", "dp"), scatter_dimension=2, tiled=True
        ).astype(jnp.float32),
        lax.psum_scatter(
            shift_grads.astype(jnp.bfloat16), ("seq", "dp"), scatter_dimension=2, tiled=True
        ).astype(jnp.float32),
        lax.psum_scatter(
            grad_qkv.astype(jnp.bfloat16), ("seq", "dp"), scatter_dimension=1, tiled=True
        ).astype(jnp.float32),
        lax.psum_scatter(
            grad_qv.astype(jnp.bfloat16), ("seq", "dp"), scatter_dimension=2, tiled=True
        ).astype(jnp.float32),
        lax.psum_scatter(
            grad_out_w.astype(jnp.bfloat16), ("seq", "dp"), scatter_dimension=2, tiled=True
        ).astype(jnp.float32),
        lax.psum_scatter(
            grad_out_b.astype(jnp.bfloat16), ("seq", "dp"), scatter_dimension=1, tiled=True
        ).astype(jnp.float32),
        lax.psum_scatter(
            grad_up_w.astype(jnp.bfloat16), ("seq", "dp"), scatter_dimension=1, tiled=True
        ).astype(jnp.float32),
        lax.psum_scatter(
            grad_up_b.astype(jnp.bfloat16), ("seq", "dp"), scatter_dimension=1, tiled=True
        ).astype(jnp.float32),
        lax.psum_scatter(
            grad_down_w.astype(jnp.bfloat16), ("seq", "dp"), scatter_dimension=2, tiled=True
        ).astype(jnp.float32),
        lax.psum_scatter(
            grad_down_b.astype(jnp.bfloat16), ("seq", "dp"), scatter_dimension=1, tiled=True
        ).astype(jnp.float32),
    )
    result = current.reshape(seq_count, block_len, model_width)
    grad_stream = grad_rows.reshape(seq_count, block_len, model_width)
    return (
        result,
        grad_stream,
        summed[0],
        summed[1],
        summed[2],
        summed[3],
        summed[4],
        summed[5],
        summed[6],
        summed[7],
        summed[8],
        summed[9],
    )


MESH = pl.DeviceIdType.MESH
BF = jnp.bfloat16
F32 = jnp.float32

SEQ_N, DP_N, MP_N = 4, 2, 4
ROWS = 272
SHARE = 64
TAIL = 16
OWN = SHARE + TAIL
HD = 64
COLS = 256
FFL = 1024
PACK = 32
BLK = SHARE + PACK
QKV_ROWS = MP_N * BLK + 2 * TAIL
VP_ROWS = MP_N * PACK + TAIL
SEG = {"d": (0, 1024), "u": (1024, 1024), "o": (2048, 256), "q": (2304, 768)}
SEG_AT = {"d": 0, "u": 1, "o": 2, "q": 3}
GROWS = 3072
GPIECE = GROWS // 8
OUT_GRADS = 2 * ROWS
OUT_SMALL = OUT_GRADS + 2 * GPIECE
OUT_ROWS = OUT_SMALL + 16
SMALL = 16
SQRT_2_PI = math.sqrt(2.0 / math.pi)
SCORE_SCALE = 0.125


def dot(a, b, ca=1, cb=0):
    return lax.dot_general(a, b, (((ca,), (cb,)), ((), ())), preferred_element_type=F32)


def fits(mesh):
    return dict(mesh.shape) == {"seq": SEQ_N, "dp": DP_N, "mp": MP_N}


VMEM_SCRATCH = {
    "wq": ((2, 3, D, COLS), BF),
    "wo": ((2, COLS, D), BF),
    "wu": ((2, D, FFL), BF),
    "wd": ((2, FFL, D), BF),
    "cur": ((OWN, D), F32),
    "grd": ((OWN, D), F32),
    "stl": ((OWN, D), F32),
    "own": ((OWN, D), F32),
    "xh": ((2, 4, OWN, D), F32),
    "rstd": ((2, 4, OWN, 128), F32),
    "nrm0": ((4 * ROWS, D), BF),
    "nrm1": ((ROWS, D), BF),
    "hin0": ((4 * ROWS, D), BF),
    "hin1": ((2 * ROWS, D), BF),
    "act0": ((4 * ROWS, FFL), BF),
    "act1": ((2 * ROWS, FFL), BF),
    "gpr": ((2, ROWS, FFL), F32),
    "gprP": ((3 * ROWS, FFL), BF),
    "dob0": ((4 * ROWS, D), BF),
    "dbr": ((ROWS, D), BF),
    "dlf": ((4 * ROWS, FFL), BF),
    "att": ((2, ROWS, COLS), BF),
    "dpr": ((ROWS, 3 * COLS), BF),
    "qkvA": ((2, SEQ_N, QKV_ROWS, 128), BF),
    "q_s": ((2, SEQ_N * ROWS, HD), BF),
    "k_s": ((2, SEQ_N * ROWS, HD), BF),
    "v_s": ((2, SEQ_N * ROWS, HD), BF),
    "do_s": ((SEQ_N * ROWS, HD), BF),
    "dk_s": ((SEQ_N * ROWS, HD), F32),
    "dv_s": ((SEQ_N * ROWS, HD), F32),
    "pt0": ((2, ROWS, ROWS), BF),
    "pt1": ((2, 2 * ROWS, ROWS), BF),
    "pt2": ((2, 3 * ROWS, ROWS), BF),
    "pt3": ((2, 4 * ROWS, ROWS), BF),
    "oA": ((2, SEQ_N, VP_ROWS, 128), BF),
    "dA": ((2, SEQ_N, VP_ROWS, 128), BF),
    "eA": ((2, SEQ_N, QKV_ROWS, 128), BF),
    "qs": ((SEQ_N, QKV_ROWS, 128), BF),
    "os_": ((SEQ_N, VP_ROWS, 128), BF),
    "ds_": ((SEQ_N, VP_ROWS, 128), BF),
    "es": ((SEQ_N, QKV_ROWS, 128), BF),
    "rsS": ((ROWS, D), BF),
    "rsR": ((3, SHARE, D), BF),
    "rtR": ((2, 3, TAIL, D), BF),
    "eq": ((4 * ROWS, 3 * HD), BF),
    "gq": ((2, SEQ_N, 3 * HD, 128), BF),
    "rAq": ((SEQ_N, 3 * HD, 128), BF),
    "rQ": ((SEQ_N, 3 * HD, 128), BF),
    "gb0": ((2, 2048, 128), BF),
    "gb1": ((2, 2, 2048, 128), BF),
    "rA0": ((2048, 128), BF),
    "gbo": ((2, 2, 2, 2, 256, 128), BF),
    "gbq": ((2, 2, 2, 768, 128), BF),
    "rA1": ((2, 2048, 128), BF),
    "rAo": ((2, 2, 2, 256, 128), BF),
    "rAp": ((2, 2, 768, 128), BF),
    "rBo": ((2, 2, 256, 128), BF),
    "rBq": ((2, 768, 128), BF),
    "rC": ((2, GROWS, 128), BF),
    "ob": ((2, GROWS, 128), BF),
    "sb": ((16, D), BF),
    "sg": ((2, SMALL, D), F32),
    "smR": ((7, 2, SMALL, 128), F32),
    "smS": ((2, SMALL, 128), F32),
    "smM": ((3, 2, SMALL, 128), F32),
    "resb": ((OWN, D), BF),
    "gstb": ((OWN, D), BF),
}
DMA_SEMS = {
    "ld": (16,),
    "ag_s": (3,), "ag_r": (3,),
    "rs_s": (3,), "rs_r": (3,),
    "rt_s": (2, 3), "rt_r": (2, 3),
    "qk_s": (3, 5), "qk_r": (3, 5),
    "do_ss": (3, 5), "do_r": (3, 5),
    "o_s": (3, 5), "o_r": (3, 5),
    "e_s": (3, 5), "e_r": (3, 5),
    "g_s": (2, 5, 4), "g_r": (2, 5, 4),
    "hp_s": (2, 5), "hp_r": (2, 5), "dp_s": (5,), "dp_r": (5,),
    "nz_s": (3, 2), "nz_r": (3, 2), "nf_s": (3, 4), "nf_r": (3, 4),
    "gq_s": (4,), "gq_r": (4,),
    "hz_s": (3, 2), "hz_r": (3, 2), "dz_s": (3, 2), "dz_r": (3, 2),
    "hf_s": (3, 4), "hf_r": (3, 4), "df_s": (3, 4), "df_r": (3, 4),
    "out": (2, 8), "so": (1,),
    "fr_s": (2, 3), "fr_r": (2, 3), "fr_t": (2, 3), "fr_u": (2, 3),
    "fl": (2, 2),
    "sm_s": (7,), "sm_r": (7,), "sn_s": (3,), "sn_r": (3,),
}
SCHEDULE = {
    (1, 7): ("a01u",),
    (1, 70): ("f31u", "f41u",),
    (1, 8): ("a01o", "f11o", "f21o",),
    (1, 9): ("a01q", "f11q", "f21q",),
    (0, 2): ("a11o", "f31o", "a11q", "f31q", "a21o", "a21q",),
    (0, 7): ("a31d", "a31u", "a00o", "f10o", "f20o",),
    (0, 8): ("a10o", "f30o", "a20o",),
    (0, 9): ("a31o", "a31q",),
    (2, 1): ("a30o", "a00d", "a00u",),
    (1, 4): ("a01d", "f31d", "f41d",),
}
IN_NAMES = ("tl", "stream", "cot", "gain", "shift", "bqv", "bo", "bu", "bd", "wq_h", "wo_h", "wu_h", "wd_h")
OUT_NAMES = ("out_o",)


class Refs:
    pass


def fused_kernel(*all_refs):
    n = Refs()
    names = IN_NAMES + OUT_NAMES + tuple(VMEM_SCRATCH) + tuple(DMA_SEMS)
    for name, ref in zip(names, all_refs):
        setattr(n, name, ref)
    pts = (n.pt0, n.pt1, n.pt2, n.pt3)
    hin, act, dob = (n.hin0, n.hin1), (n.act0, n.act1), (n.dob0, n.dob0.at[pl.ds(0, 2 * ROWS)])
    nrm = (n.nrm0, n.nrm1)

    s = lax.axis_index("seq")
    c = lax.axis_index("dp")
    m = lax.axis_index("mp")
    mx, my = lax.rem(m, 2), lax.div(m, 2)
    peers = (my * 2 + (1 - mx), (1 - my) * 2 + mx, (1 - my) * 2 + (1 - mx))
    z0, z1 = lax.rem(s, 2), lax.div(s, 2)
    zs = (z1 * 2 + (1 - z0), (1 - z1) * 2 + z0, (1 - z1) * 2 + (1 - z0))

    def mp_dev(r):
        return (s, c, peers[r])

    def z_dev(k):
        return (zs[k], c, m)

    core_dev = (s, 1 - c, m)
    group = [core_dev] + [z_dev(k) for k in range(3)] + [(zs[k], 1 - c, m) for k in range(3)]

    barrier = pltpu.get_barrier_semaphore()
    everyone = group + [mp_dev(r) for r in range(3)]
    for dev in everyone:
        pl.semaphore_signal(barrier, inc=1, device_id=dev, device_id_type=MESH)

    loads = [
        pltpu.make_async_copy(n.stream.at[pl.ds(pl.multiple_of(m * SHARE, SHARE), SHARE)], n.cur.at[pl.ds(0, SHARE)], n.ld.at[0]),
        pltpu.make_async_copy(n.stream.at[pl.ds(MP_N * SHARE, TAIL)], n.cur.at[pl.ds(SHARE, TAIL)], n.ld.at[1]),
        pltpu.make_async_copy(n.wq_h, n.wq, n.ld.at[2]),
        pltpu.make_async_copy(n.wo_h, n.wo, n.ld.at[3]),
        pltpu.make_async_copy(n.wu_h, n.wu, n.ld.at[4]),
        pltpu.make_async_copy(n.wd_h, n.wd, n.ld.at[5]),
        pltpu.make_async_copy(n.cot.at[pl.ds(pl.multiple_of(m * SHARE, SHARE), SHARE)], n.grd.at[pl.ds(0, SHARE)], n.ld.at[6]),
        pltpu.make_async_copy(n.cot.at[pl.ds(MP_N * SHARE, TAIL)], n.grd.at[pl.ds(SHARE, TAIL)], n.ld.at[7]),
    ]
    for cp in loads[:3]:
        cp.start()
    for cp in loads[:2]:
        cp.wait()
    for cp in loads[3:]:
        cp.start()

    def rcopy(src, dst, ss, rs, dev):
        return pltpu.make_async_remote_copy(
            src_ref=src, dst_ref=dst, send_sem=ss, recv_sem=rs, device_id=dev, device_id_type=MESH
        )

    def share(j):
        return pl.ds(pl.multiple_of(j * SHARE, SHARE), SHARE)

    tail = pl.ds(MP_N * SHARE, TAIL)

    def ln(v, l, j):
        ce = v - jnp.mean(v, axis=-1, keepdims=True)
        r = lax.rsqrt(jnp.mean(ce * ce, axis=-1, keepdims=True) + norm_eps)
        h = ce * r
        n.xh[l, j] = h
        n.rstd[l, j] = jnp.broadcast_to(r, (OWN, 128))
        return h * n.gain[l, pl.ds(j, 1), :] + n.shift[l, pl.ds(j, 1), :]

    def ln_back(l, j, dy):
        h = n.xh[l, j]
        r = n.rstd[l, j][:, :1]
        t = dy * n.gain[l, pl.ds(j, 1), :]
        m1 = jnp.mean(t, axis=-1, keepdims=True)
        m2 = jnp.mean(t * h, axis=-1, keepdims=True)
        return r * (t - m1 - h * m2)

    row_ids = lax.broadcasted_iota(jnp.int32, (OWN, 1), 0)
    counted = jnp.where((row_ids < SHARE) | (m == 0), 1.0, 0.0).astype(F32)

    def ln_params(l, j, dy):
        dw = dy * counted
        n.sg[l, pl.ds(j, 1), :] = jnp.sum(dw * n.xh[l, j], axis=0, keepdims=True)
        n.sg[l, pl.ds(4 + j, 1), :] = jnp.sum(dw, axis=0, keepdims=True)

    def gather_rows(buf, own_rows):
        buf[share(m), :] = own_rows[:SHARE]
        buf[tail, :] = own_rows[SHARE:]
        copies = []
        for r in range(3):
            cp = rcopy(buf.at[share(m)], buf.at[share(m)], n.ag_s.at[r], n.ag_r.at[r], mp_dev(r))
            cp.start()
            copies.append(cp)
        return copies

    def scatter_copy(r):
        return rcopy(n.rsS.at[share(peers[r])], n.rsR.at[r], n.rs_s.at[r], n.rs_r.at[r], mp_dev(r))

    def tail_copy(turn, r):
        return rcopy(n.rsS.at[tail], n.rtR.at[turn, r], n.rt_s.at[turn, r], n.rt_r.at[turn, r], mp_dev(r))

    def send_part(r, part):
        n.rsS[share(peers[r]), :] = part.astype(BF)
        scatter_copy(r).start()

    def send_tail(turn, part):
        n.rsS[tail, :] = part.astype(BF)
        for r in range(3):
            tail_copy(turn, r).start()

    def keep_own(part):
        n.own[...] = part

    def reduced(turn):
        for r in range(3):
            tail_copy(turn, r).wait_recv()
        for r in range(3):
            scatter_copy(r).wait_recv()
        total = n.own[:SHARE, :]
        rest = n.own[SHARE:, :].astype(BF).astype(F32)
        for r in range(3):
            total = total + n.rsR[r].astype(F32)
            rest = rest + n.rtR[turn, r].astype(F32)
        for r in range(3):
            scatter_copy(r).wait_send()
            tail_copy(turn, r).wait_send()
        return jnp.concatenate([total, rest], axis=0)

    def pack_rows(v):
        return jnp.concatenate([v[:PACK], v[PACK:]], axis=1)

    def pad_lanes(v):
        return jnp.concatenate([v, jnp.zeros_like(v)], axis=1)

    def chunk_rows(j, size):
        return pl.ds(pl.multiple_of(j * size, size), size)

    def chunk_send(stage, dest, l, j, pos, size, ss, rs):
        dest[l, s, chunk_rows(j, size), :] = stage[s, chunk_rows(j, size), :]
        for k in range(3):
            rcopy(
                stage.at[zs[k], chunk_rows(j, size)], dest.at[l, s, chunk_rows(j, size)],
                ss.at[k, pos], rs.at[k, pos], z_dev(k),
            ).start()

    def tail_send(stage, dest, l, start, size, ss, rs):
        dest[l, s, pl.ds(start, size), :] = stage[s, pl.ds(start, size), :]
        for k in range(3):
            rcopy(
                stage.at[zs[k], pl.ds(start, size)], dest.at[l, s, pl.ds(start, size)],
                ss.at[k, 4], rs.at[k, 4], z_dev(k),
            ).start()

    def chunk_wait(stage, dest, l, size, start, tail_size, ss, rs):
        order = (m,) + peers
        for k in range(3):
            for pos in range(4):
                cp = rcopy(
                    stage.at[zs[k], chunk_rows(order[pos], size)], dest.at[l, s, chunk_rows(order[pos], size)],
                    ss.at[k, pos], rs.at[k, pos], z_dev(k),
                )
                cp.wait()
            rcopy(
                stage.at[zs[k], pl.ds(start, tail_size)], dest.at[l, s, pl.ds(start, tail_size)],
                ss.at[k, 4], rs.at[k, 4], z_dev(k),
            ).wait()

    def back_copy(stage, dest, l, k, pos, size, tail_size, ss, rs):
        if pos == 4:
            rows = pl.ds(MP_N * size, tail_size)
        else:
            rows = chunk_rows(m if pos == 0 else peers[pos - 1], size)
        return rcopy(stage.at[zs[k], rows], dest.at[l, s, rows], ss.at[k, pos], rs.at[k, pos], z_dev(k))

    BACK_ORDER = (3, 1, 2, 0, 4)

    def back_send(stage, dest, l, size, tail_size, ss, rs):
        for pos in BACK_ORDER:
            for k in range(3):
                back_copy(stage, dest, l, k, pos, size, tail_size, ss, rs).start()
        dest[l, s] = stage[s]

    def back_wait(stage, dest, l, pos, size, tail_size, ss, rs):
        for k in range(3):
            back_copy(stage, dest, l, k, pos, size, tail_size, ss, rs).wait()

    def side_by_side(pieces, low):
        return jnp.concatenate([g[:, :HD] if low else g[:, HD:] for g in pieces], axis=1)

    def g_parts(l, seg):
        if seg == "o":
            return n.gbo.at[l], n.rAo.at[l], n.rBo.at[l]
        return n.gbq, n.rAp, n.rBq

    def g_copy(phase, l, seg):
        at = SEG_AT[seg]
        start, count = SEG[seg]
        rows = pl.ds(start, count)
        full, got, part = g_parts(l, seg)
        if phase == 0:
            dev = core_dev
            if seg in "du" and l == 0:
                src, dst = n.gb0.at[1 - c, rows], n.rA0.at[rows]
            elif seg in "du":
                src, dst = n.gb1.at[1 - c, :, rows], n.rA1.at[:, rows]
            else:
                src, dst = full.at[1 - c], got
        elif phase <= 2:
            b = 1 - z1 if phase == 1 else z1
            src, dst, dev = full.at[c, 1 - z0, b], part.at[b], z_dev(0)
        else:
            dev = z_dev(1)
            if seg in "du":
                rows = pl.ds(start + 512 * (phase - 3), 512)
                src = n.gb1.at[c, 1 - z1, rows]
            else:
                src = full.at[c, z0, 1 - z1]
            dst = n.rC.at[l, rows]
        return rcopy(src, dst, n.g_s.at[l, phase, at], n.g_r.at[l, phase, at], dev)

    def f(phase, l, seg):
        g_copy(phase, l, seg).start()

    def add_to(ref, got):
        ref[...] = (ref[...].astype(F32) + got[...].astype(F32)).astype(BF)

    def a(phase, l, seg):
        g_copy(phase, l, seg).wait()
        start, count = SEG[seg]
        rows = pl.ds(start, count)
        full, got, part = g_parts(l, seg)
        if phase == 0 and seg in "du" and l == 0:
            n.ob[l, rows, :] = (n.gb0[c, rows, :].astype(F32) + n.rA0[rows, :].astype(F32)).astype(BF)
        elif phase == 0:
            for b in range(2):
                if seg in "du":
                    add_to(n.gb1.at[c, b, rows], n.rA1.at[b, rows])
                else:
                    for i in range(2):
                        add_to(full.at[c, i, b], got.at[i, b])
        elif phase <= 2:
            b = 1 - z1 if phase == 1 else z1
            add_to(full.at[c, z0, b], part.at[b])
        else:
            if seg in "du":
                g_copy(4, l, seg).wait()
                mine = n.gb1[c, z1, rows, :]
            else:
                mine = full[c, z0, z1]
            n.ob[l, rows, :] = (mine.astype(F32) + n.rC[l, rows, :].astype(F32)).astype(BF)

    def partner_copy(buf, pos, ss, rs):
        if pos == 4:
            src, dst = tail, pl.ds(ROWS + MP_N * SHARE, TAIL)
        else:
            j = m if pos == 0 else peers[pos - 1]
            src, dst = share(j), pl.ds(pl.multiple_of(ROWS + j * SHARE, TAIL), SHARE)
        return rcopy(buf.at[src], buf.at[dst], ss.at[pos], rs.at[pos], z_dev(0))

    def block_copies(buf, k, ss, rs):
        at = ROWS * (k + 1)
        return (
            rcopy(buf.at[share(m)], buf.at[pl.ds(pl.multiple_of(at + m * SHARE, TAIL), SHARE)], ss.at[k, 0], rs.at[k, 0], z_dev(k)),
            rcopy(buf.at[tail], buf.at[pl.ds(at + MP_N * SHARE, TAIL)], ss.at[k, 1], rs.at[k, 1], z_dev(k)),
        )

    def pass_copy(buf, k, r, ss, rs):
        at = ROWS * (k + 1)
        if r < 2:
            rows = pl.ds(pl.multiple_of(at + m * SHARE, TAIL), SHARE)
            dev = mp_dev(r)
        else:
            rows = pl.ds(pl.multiple_of(at + peers[r - 2] * SHARE + (r - 2) * (SHARE // 2), TAIL), SHARE // 2)
            dev = mp_dev(3 - r)
        return rcopy(buf.at[rows], buf.at[rows], ss.at[k, r], rs.at[k, r], dev)

    def block_send(buf, ss, rs, which=(0, 1, 2)):
        for k in which:
            for cp in block_copies(buf, k, ss, rs):
                cp.start()

    def block_pass(buf, zss, zrs, ss, rs, which=(0, 1, 2)):
        for k in which:
            for cp in block_copies(buf, k, zss, zrs):
                cp.wait()
            for r in range(2):
                pass_copy(buf, k, r, ss, rs).start()

    def block_pass_on(buf, ss, rs, which=(0, 1, 2)):
        for k in which:
            for r in range(2):
                pass_copy(buf, k, r, ss, rs).wait()
                pass_copy(buf, k, r + 2, ss, rs).start()

    def block_wait(buf, ss, rs, which=(0, 1, 2)):
        for k in which:
            for r in range(2, 4):
                pass_copy(buf, k, r, ss, rs).wait()

    def others_forward(l):
        for pos in range(5):
            partner_copy(hin[l], pos, n.hp_s.at[l], n.hp_r.at[l]).wait()
        if l == 0:
            block_wait(hin[0], n.hf_s, n.hf_r, (1, 2))
        for k in range(3 if l == 0 else 1):
            rows = pl.ds(ROWS * (k + 1), ROWS)
            value, slope = gelu_pair(dot(hin[l][rows, :], n.wu[l]) + n.bu[pl.ds(l, 1), :])
            act[l][rows, :] = value.astype(BF)
            n.gprP[pl.ds(ROWS * k, ROWS), :] = slope.astype(BF)

    def others_backward(l):
        if l == 1:
            for pos in range(5):
                partner_copy(dob[1], pos, n.dp_s, n.dp_r).wait()
        else:
            block_wait(dob[0], n.df_s, n.df_r)
        for k in range(3 if l == 0 else 1):
            rows = pl.ds(ROWS * (k + 1), ROWS)
            n.dlf[rows, :] = (dot(dob[l][rows, :], n.wd[l], 1, 1) * n.gprP[pl.ds(ROWS * k, ROWS), :].astype(F32)).astype(BF)

    def half_columns(ref):
        return jnp.concatenate([ref[:, pl.ds(pl.multiple_of(z0 * 256 + 512 * b, 256), 256)] for b in range(2)], axis=1)

    def own_columns(ref):
        return ref[:, pl.ds(pl.multiple_of(s * 256, 256), 256)]

    def grad_down(l):
        if l == 1:
            grad = dot(act[1][...], half_columns(dob[1]), 0, 0).astype(BF)
            for k in range(4):
                n.gb1[k % 2, k // 2, pl.ds(0, 1024), :] = grad[:, 128 * k:128 * k + 128]
        else:
            grad = dot(own_columns(dob[0]), act[0][...], 0, 0).T.astype(BF)
            for k in range(2):
                n.gb0[k, pl.ds(0, 1024), :] = grad[:, 128 * k:128 * k + 128]
        f(0, l, "d")

    def grad_up(l):
        if l == 1:
            grad = dot(half_columns(hin[1]), n.dlf[:2 * ROWS, :], 0, 0).astype(BF)
        else:
            grad = dot(own_columns(hin[0]), n.dlf[...], 0, 0).astype(BF)
        for k in range(4 if l == 1 else 2):
            for t in range(8):
                piece = grad[128 * k:128 * k + 128, 128 * t:128 * t + 128]
                if l == 1:
                    n.gb1[k % 2, k // 2, pl.ds(1024 + 128 * t, 128), :] = piece
                else:
                    n.gb0[k, pl.ds(1024 + 128 * t, 128), :] = piece
        f(0, l, "u")

    def head_core():
        return rcopy(n.gq.at[1 - c], n.rAq, n.gq_s.at[3], n.gq_r.at[3], core_dev)

    def head_copies():
        return [rcopy(n.gq.at[c, zs[k]], n.rQ.at[s], n.gq_s.at[k], n.gq_r.at[k], z_dev(k)) for k in range(3)]

    def head_grad():
        block_wait(n.nrm0, n.nf_s, n.nf_r)
        grad = dot(n.eq[...], n.nrm0[...], 0, 0).astype(BF)
        for k in range(8):
            n.gq[k % 2, k // 2] = grad[:, 128 * k:128 * k + 128]
        head_core().start()

    def head_grad_send():
        head_core().wait()
        for z in range(SEQ_N):
            add_to(n.gq.at[c, z], n.rAq.at[z])
        for cp in head_copies():
            cp.start()
        n.rQ[s] = n.gq[c, s]

    def head_grad_last():
        for cp in head_copies():
            cp.wait()
        for t in range(6):
            rows = pl.ds(HD * (t // 2), HD)
            both = jnp.concatenate([n.rQ[2 * (t % 2), rows, :], n.rQ[2 * (t % 2) + 1, rows, :]], axis=0)
            n.ob[0, pl.ds(2304 + 128 * t, 128), :] = both.astype(F32).T.astype(BF)

    def hook(l, at):
        for step in SCHEDULE.get((l, at), ()):
            (f if step[0] == "f" else a)(int(step[1]), int(step[2]), step[3])

    def g_out(l):
        return [
            pltpu.make_async_copy(
                n.ob.at[l, pl.ds(GPIECE * t, GPIECE)],
                n.out_o.at[pl.ds(OUT_GRADS + GPIECE * l, GPIECE), pl.ds(128 * t, 128)],
                n.out.at[l, t],
            )
            for t in range(8)
        ]

    text_count = n.tl[0]

    def gelu_pair(u):
        uu = u * u
        t = jnp.tanh(SQRT_2_PI * (u + 0.044715 * u * uu))
        half = 0.5 * (1.0 + t)
        slope = half + 0.5 * u * (1.0 - t * t) * (SQRT_2_PI * (1.0 + 3 * 0.044715 * uu))
        return u * half, slope

    order_rows = lambda own_value, pos, buf: own_value if pos == 0 else buf[share(peers[pos - 1]), :]

    def forward(l, first):
        own_rows = ln(n.cur[...], l, 0).astype(BF)
        if first:
            pl.semaphore_wait(barrier, len(everyone))
        copies = gather_rows(nrm[l], own_rows)
        if first:
            loads[2].wait()
        for pos in range(4):
            if pos > 0:
                copies[pos - 1].wait_recv()
            rows = order_rows(own_rows, pos, nrm[l])
            q = dot(rows, n.wq[l, 0]) + n.bqv[l, pl.ds(0, 1), :]
            k = dot(rows, n.wq[l, 1])
            v = dot(rows, n.wq[l, 2]) + n.bqv[l, pl.ds(1, 1), :]
            j = m if pos == 0 else peers[pos - 1]
            at = pl.multiple_of(j * BLK, BLK)
            for h in range(SEQ_N):
                cut = slice(HD * h, HD * h + HD)
                n.qs[h, pl.ds(at, SHARE), :] = jnp.concatenate([q[:SHARE, cut], k[:SHARE, cut]], axis=1).astype(BF)
                n.qs[h, pl.ds(at + SHARE, PACK), :] = pack_rows(v[:SHARE, cut]).astype(BF)
                if pos == 0:
                    n.qs[h, pl.ds(MP_N * BLK, TAIL), :] = jnp.concatenate([q[SHARE:, cut], k[SHARE:, cut]], axis=1).astype(BF)
                    n.qs[h, pl.ds(MP_N * BLK + TAIL, TAIL), :] = pad_lanes(v[SHARE:, cut]).astype(BF)
            chunk_send(n.qs, n.qkvA, l, j, pos, BLK, n.qk_s, n.qk_r)
            if pos == 0:
                tail_send(n.qs, n.qkvA, l, MP_N * BLK, 2 * TAIL, n.qk_s, n.qk_r)
        for cp in copies:
            cp.wait_send()
        if not first:
            block_pass(hin[0], n.hz_s, n.hz_r, n.hf_s, n.hf_r, (1, 2))
        chunk_wait(n.qs, n.qkvA, l, BLK, MP_N * BLK, 2 * TAIL, n.qk_s, n.qk_r)
        for zb in range(SEQ_N):
            for j in range(MP_N):
                both = n.qkvA[l, zb, pl.ds(BLK * j, SHARE), :]
                vals = n.qkvA[l, zb, pl.ds(BLK * j + SHARE, PACK), :]
                at = ROWS * zb + SHARE * j
                n.q_s[l, pl.ds(at, SHARE), :] = both[:, :HD]
                n.k_s[l, pl.ds(at, SHARE), :] = both[:, HD:]
                n.v_s[l, pl.ds(at, PACK), :] = vals[:, :HD]
                n.v_s[l, pl.ds(at + PACK, PACK), :] = vals[:, HD:]
            both = n.qkvA[l, zb, pl.ds(BLK * MP_N, TAIL), :]
            vals = n.qkvA[l, zb, pl.ds(BLK * MP_N + TAIL, TAIL), :]
            at = ROWS * zb + SHARE * MP_N
            n.q_s[l, pl.ds(at, TAIL), :] = both[:, :HD]
            n.k_s[l, pl.ds(at, TAIL), :] = both[:, HD:]
            n.v_s[l, pl.ds(at, TAIL), :] = vals[:, :HD]
        for i in range(SEQ_N):
            width = ROWS * (i + 1)
            st = dot(n.k_s[l, pl.ds(0, width), :], n.q_s[l, pl.ds(ROWS * i, ROWS), :], 1, 1) * SCORE_SCALE
            key_at = lax.broadcasted_iota(jnp.int32, (ROWS, ROWS), 0)
            query_at = lax.broadcasted_iota(jnp.int32, (ROWS, ROWS), 1)
            causal = key_at <= query_at
            if i == 0:
                st = jnp.where(causal & ((key_at >= TEXT) | (key_at < text_count)), st, -1e30)
            else:
                text_at = lax.broadcasted_iota(jnp.int32, (TEXT, ROWS), 0)
                st = jnp.concatenate([
                    jnp.where(text_at < text_count, st[:TEXT], -1e30),
                    st[TEXT:ROWS * i],
                    jnp.where(causal, st[ROWS * i:], -1e30),
                ], axis=0)
            e = jnp.exp(st - jnp.max(st, axis=0, keepdims=True))
            p = (e * (1.0 / jnp.sum(e, axis=0, keepdims=True))).astype(BF)
            pts[i][l] = p
            o = dot(n.v_s[l, pl.ds(0, width), :], p, 0, 0).T
            for j in range(MP_N):
                n.os_[i, pl.ds(PACK * j, PACK), :] = pack_rows(o[SHARE * j:SHARE * j + SHARE]).astype(BF)
            n.os_[i, pl.ds(PACK * MP_N, TAIL), :] = pad_lanes(o[SHARE * MP_N:]).astype(BF)
        back_send(n.os_, n.oA, l, PACK, TAIL, n.o_s, n.o_r)
        if not first:
            block_pass_on(hin[0], n.hf_s, n.hf_r, (1, 2))
        if first:
            loads[3].wait()
        for pos in BACK_ORDER[:4]:
            back_wait(n.os_, n.oA, l, pos, PACK, TAIL, n.o_s, n.o_r)
            j = m if pos == 0 else peers[pos - 1]
            got = [n.oA[l, h, chunk_rows(j, PACK), :] for h in range(SEQ_N)]
            rows = jnp.concatenate([side_by_side(got, True), side_by_side(got, False)], axis=0)
            n.att[l, share(j), :] = rows
            if pos > 0:
                send_part(pos - 1, dot(rows, n.wo[l]))
            else:
                back_wait(n.os_, n.oA, l, 4, PACK, TAIL, n.o_s, n.o_r)
                got = [n.oA[l, h, pl.ds(PACK * MP_N, TAIL), :] for h in range(SEQ_N)]
                rest = side_by_side(got, True)
                n.att[l, tail, :] = rest
                part = dot(jnp.concatenate([rows, rest], axis=0), n.wo[l])
                send_tail(0, part[SHARE:])
                keep_own(part)
        if not first:
            block_send(n.nrm0, n.nz_s, n.nz_r)
        branch = reduced(0) + n.bo[pl.ds(l, 1), :]
        settled = n.cur[...] + ln(branch, l, 1)
        n.stl[...] = settled
        own_rows = ln(settled, l, 2).astype(BF)
        copies = gather_rows(hin[l], own_rows)
        if first:
            block_send(hin[0], n.hz_s, n.hz_r, (1, 2))
        partner_copy(hin[l], 0, n.hp_s.at[l], n.hp_r.at[l]).start()
        partner_copy(hin[l], 4, n.hp_s.at[l], n.hp_r.at[l]).start()
        if first:
            loads[4].wait()
            loads[5].wait()
        for pos in range(4):
            if pos > 0:
                copies[pos - 1].wait_recv()
                partner_copy(hin[l], pos, n.hp_s.at[l], n.hp_r.at[l]).start()
            rows = order_rows(own_rows, pos, hin[l])
            value, slope = gelu_pair(dot(rows, n.wu[l]) + n.bu[pl.ds(l, 1), :])
            value = value.astype(BF)
            j = m if pos == 0 else peers[pos - 1]
            act[l][share(j), :] = value[:SHARE]
            n.gpr[l, share(j), :] = slope[:SHARE]
            part = dot(value, n.wd[l])
            if pos == 0:
                act[l][tail, :] = value[SHARE:]
                n.gpr[l, tail, :] = slope[SHARE:]
                send_tail(1, part[SHARE:])
                keep_own(part)
            else:
                send_part(pos - 1, part)
        for cp in copies:
            cp.wait_send()
        out_branch = reduced(1) + n.bd[pl.ds(l, 1), :]
        n.cur[...] = n.stl[...] + ln(out_branch, l, 3)

    result_copies = []

    def final_rows(which, stage):
        copies = []
        out = n.out_o.at[pl.ds(ROWS * which, ROWS)]
        for r in range(3):
            copies.append(rcopy(stage.at[pl.ds(0, SHARE)], out.at[share(m)], n.fr_s.at[which, r], n.fr_r.at[which, r], mp_dev(r)))
        copies.append(pltpu.make_async_copy(stage.at[pl.ds(0, SHARE)], out.at[share(m)], n.fl.at[which, 0]))
        copies.append(pltpu.make_async_copy(stage.at[pl.ds(SHARE, TAIL)], out.at[pl.ds(MP_N * SHARE, TAIL)], n.fl.at[which, 1]))
        for cp in copies:
            cp.start()
        return copies

    def backward(l):
        grad_rows = n.grd[...]
        d_ob = ln_back(l, 3, grad_rows).astype(BF)
        copies = gather_rows(dob[l], d_ob)
        if l == 1:
            partner_copy(dob[1], 0, n.dp_s, n.dp_r).start()
            partner_copy(dob[1], 4, n.dp_s, n.dp_r).start()
        else:
            block_send(dob[0], n.dz_s, n.dz_r)
        ln_params(l, 3, grad_rows)
        n.sg[l, pl.ds(9, 1), :] = jnp.sum(d_ob.astype(F32) * counted, axis=0, keepdims=True)
        hook(l, 0)
        for pos in range(4):
            if pos > 0:
                copies[pos - 1].wait_recv()
                if l == 1:
                    partner_copy(dob[1], pos, n.dp_s, n.dp_r).start()
            rows = order_rows(d_ob, pos, dob[l])
            j = m if pos == 0 else peers[pos - 1]
            slope = n.gpr[l, share(j), :]
            if pos == 0:
                slope = jnp.concatenate([slope, n.gpr[l, tail, :]], axis=0)
            d_l = (dot(rows, n.wd[l], 1, 1) * slope).astype(BF)
            n.dlf[share(j), :] = d_l[:SHARE]
            part = dot(d_l, n.wu[l], 1, 1)
            if pos == 0:
                n.dlf[tail, :] = d_l[SHARE:]
                send_tail(0, part[SHARE:])
                keep_own(part)
                if l == 1:
                    others_forward(1)
            else:
                send_part(pos - 1, part)
        for cp in copies:
            cp.wait_send()
        hook(l, 1)
        n.sg[l, pl.ds(10, 1), :] = jnp.sum(n.dlf[:ROWS, :].astype(F32), axis=0, keepdims=True)
        hook(l, 2)
        d_hidden = reduced(0)
        d_settled = grad_rows + ln_back(l, 2, d_hidden)
        d_br = ln_back(l, 1, d_settled).astype(BF)
        copies = gather_rows(n.dbr, d_br)
        n.stl[...] = d_settled
        ln_params(l, 2, d_hidden)
        ln_params(l, 1, d_settled)
        n.sg[l, pl.ds(8, 1), :] = jnp.sum(d_br.astype(F32) * counted, axis=0, keepdims=True)
        hook(l, 3)
        for pos in range(4):
            if pos > 0:
                copies[pos - 1].wait_recv()
            rows = order_rows(d_br, pos, n.dbr)
            j = m if pos == 0 else peers[pos - 1]
            d_at = dot(rows, n.wo[l], 1, 1)
            for h in range(SEQ_N):
                cut = slice(HD * h, HD * h + HD)
                n.ds_[h, chunk_rows(j, PACK), :] = pack_rows(d_at[:SHARE, cut]).astype(BF)
                if pos == 0:
                    n.ds_[h, pl.ds(MP_N * PACK, TAIL), :] = pad_lanes(d_at[SHARE:, cut]).astype(BF)
            chunk_send(n.ds_, n.dA, l, j, pos, PACK, n.do_ss, n.do_r)
            if pos == 0:
                tail_send(n.ds_, n.dA, l, MP_N * PACK, TAIL, n.do_ss, n.do_r)
                if l == 1:
                    others_backward(1)
                    grad_down(1)
                hook(l, 31)
        for cp in copies:
            cp.wait_send()
        hook(l, 4)
        if l == 1:
            grad_up(1)
            block_pass(n.nrm0, n.nz_s, n.nz_r, n.nf_s, n.nf_r)
        else:
            block_pass(dob[0], n.dz_s, n.dz_r, n.df_s, n.df_r)
        grad = dot(n.att[l], n.dbr[...], 0, 0).astype(BF)
        for k in range(8):
            n.gbo[l, k % 2, (k // 2) % 2, k // 4] = grad[:, 128 * k:128 * k + 128]
        f(0, l, "o")
        hook(l, 5)
        chunk_wait(n.ds_, n.dA, l, PACK, MP_N * PACK, TAIL, n.do_ss, n.do_r)
        for zb in range(SEQ_N):
            for j in range(MP_N):
                vals = n.dA[l, zb, pl.ds(PACK * j, PACK), :]
                at = ROWS * zb + SHARE * j
                n.do_s[pl.ds(at, PACK), :] = vals[:, :HD]
                n.do_s[pl.ds(at + PACK, PACK), :] = vals[:, HD:]
            n.do_s[pl.ds(ROWS * zb + SHARE * MP_N, TAIL), :] = n.dA[l, zb, pl.ds(PACK * MP_N, TAIL), :][:, :HD]
        hook(l, 6)
        for i in reversed(range(SEQ_N)):
            width = ROWS * (i + 1)
            here = pl.ds(ROWS * i, ROWS)
            p = pts[i][l]
            dpt = dot(n.v_s[l, pl.ds(0, width), :], n.do_s[here, :], 1, 1)
            pf = p.astype(F32)
            mean_term = jnp.sum(pf * dpt, axis=0, keepdims=True)
            dst = (pf * (dpt - mean_term)).astype(BF)
            dv = dot(p, n.do_s[here, :])
            dk = dot(dst, n.q_s[l, here, :])
            if i < SEQ_N - 1:
                dv = dv + n.dv_s[pl.ds(0, width), :]
                dk = dk + n.dk_s[pl.ds(0, width), :]
            if i > 0:
                n.dv_s[pl.ds(0, ROWS * i), :] = dv[:ROWS * i]
                n.dk_s[pl.ds(0, ROWS * i), :] = dk[:ROWS * i]
            dq = dot(n.k_s[l, pl.ds(0, width), :], dst, 0, 0).T * SCORE_SCALE
            dk = dk[ROWS * i:] * SCORE_SCALE
            dv = dv[ROWS * i:]
            if l == 0:
                place = (z0 if i % 2 == 0 else 1 - z0) + 2 * (z1 if i < 2 else 1 - z1)
                at = pl.ds(pl.multiple_of(place * ROWS, TAIL), ROWS)
                n.eq[at, pl.ds(0, 2 * HD)] = jnp.concatenate([dq, dk], axis=1).astype(BF)
                n.eq[at, pl.ds(2 * HD, HD)] = dv.astype(BF)
            for j in range(MP_N):
                cut = slice(SHARE * j, SHARE * j + SHARE)
                n.es[i, pl.ds(BLK * j, SHARE), :] = jnp.concatenate([dq[cut], dk[cut]], axis=1).astype(BF)
                n.es[i, pl.ds(BLK * j + SHARE, PACK), :] = pack_rows(dv[cut]).astype(BF)
            cut = slice(SHARE * MP_N, ROWS)
            n.es[i, pl.ds(BLK * MP_N, TAIL), :] = jnp.concatenate([dq[cut], dk[cut]], axis=1).astype(BF)
            n.es[i, pl.ds(BLK * MP_N + TAIL, TAIL), :] = pad_lanes(dv[cut]).astype(BF)
        back_send(n.es, n.eA, l, BLK, 2 * TAIL, n.e_s, n.e_r)
        hook(l, 7)
        if l == 1:
            others_forward(0)
            block_pass_on(n.nrm0, n.nf_s, n.nf_r)
        else:
            head_grad()
            block_pass_on(dob[0], n.df_s, n.df_r)

        def d_norm_part(rows):
            total = dot(rows[0], n.wq[l, 0], 1, 1)
            total = total + dot(rows[1], n.wq[l, 1], 1, 1)
            return total + dot(rows[2], n.wq[l, 2], 1, 1)

        for pos in BACK_ORDER[:4]:
            back_wait(n.es, n.eA, l, pos, BLK, 2 * TAIL, n.e_s, n.e_r)
            j = m if pos == 0 else peers[pos - 1]
            at = pl.multiple_of(j * BLK, BLK)
            both = [n.eA[l, h, pl.ds(at, SHARE), :] for h in range(SEQ_N)]
            vals = [n.eA[l, h, pl.ds(at + SHARE, PACK), :] for h in range(SEQ_N)]
            rows = [side_by_side(both, True), side_by_side(both, False)]
            rows.append(jnp.concatenate([side_by_side(vals, True), side_by_side(vals, False)], axis=0))
            for t in range(3):
                n.dpr[share(j), pl.ds(COLS * t, COLS)] = rows[t]
            if pos > 0:
                send_part(pos - 1, d_norm_part(rows))
            else:
                back_wait(n.es, n.eA, l, 4, BLK, 2 * TAIL, n.e_s, n.e_r)
                both = [n.eA[l, h, pl.ds(BLK * MP_N, TAIL), :] for h in range(SEQ_N)]
                vals = [n.eA[l, h, pl.ds(BLK * MP_N + TAIL, TAIL), :] for h in range(SEQ_N)]
                rest = [side_by_side(both, True), side_by_side(both, False), side_by_side(vals, True)]
                for t in range(3):
                    n.dpr[tail, pl.ds(COLS * t, COLS)] = rest[t]
                part = d_norm_part([jnp.concatenate([rows[t], rest[t]], axis=0) for t in range(3)])
                send_tail(1, part[SHARE:])
                keep_own(part)
        hook(l, 70)
        if l == 1:
            result_copies.extend(final_rows(0, n.resb))
        if l == 0:
            head_grad_send()
        if l == 1:
            grad = dot(nrm[l][...], n.dpr[...], 0, 0).astype(BF)
            for k in range(8):
                for t in range(6):
                    n.gbq[k % 2, (k // 2) % 2, k // 4, pl.ds(128 * t, 128), :] = grad[128 * k:128 * k + 128, 128 * t:128 * t + 128]
            f(0, l, "q")
        sums = jnp.sum(n.dpr[...].astype(F32), axis=0, keepdims=True)
        blank = jnp.zeros((1, 96), F32)
        for at, lane in ((11, 0), (12, 2 * COLS)):
            pieces = []
            for k in range(8):
                pieces += [sums[:, lane + 32 * k:lane + 32 * k + 32], blank]
            n.sg[l, pl.ds(at, 1), :] = jnp.concatenate(pieces, axis=1)
        n.sg[l, pl.ds(13, 3), :] = jnp.zeros((3, D), F32)
        hook(l, 8)
        d_norm = reduced(1)
        n.grd[...] = n.stl[...] + ln_back(l, 0, d_norm)
        ln_params(l, 0, d_norm)
        hook(l, 9)

    forward(0, True)
    forward(1, False)
    n.resb[...] = n.cur[...].astype(BF)
    loads[6].wait()
    loads[7].wait()
    backward(1)
    backward(0)
    n.gstb[...] = n.grd[...].astype(BF)
    grad_copies = final_rows(1, n.gstb)

    small = []
    for t, dev in enumerate(group):
        lanes = pl.ds(pl.multiple_of((dev[0] * 2 + dev[1]) * 128, 128), 128)
        cp = rcopy(n.sg.at[:, :, lanes], n.smR.at[t], n.sm_s.at[t], n.sm_r.at[t], dev)
        cp.start()
        small.append(cp)
    others_backward(0)
    grad_down(0)
    grad_up(0)
    hook(2, 0)
    head_grad_last()
    for cp in small:
        cp.wait()
    total = n.sg[:, :, pl.ds(pl.multiple_of((s * 2 + c) * 128, 128), 128)]
    for t in range(7):
        total = total + n.smR[t]
    n.smS[...] = total
    small = []
    for r in range(3):
        cp = rcopy(n.smS, n.smM.at[r], n.sn_s.at[r], n.sn_r.at[r], mp_dev(r))
        cp.start()
        small.append(cp)
    hook(2, 1)
    for cp in small:
        cp.wait()
    shared = lax.broadcasted_iota(jnp.int32, (2, SMALL, 128), 1) < 10
    total = total + jnp.where(shared, n.smM[0] + n.smM[1] + n.smM[2], 0.0)
    high = total.astype(BF)
    rest = (total - high.astype(F32)).astype(BF)
    n.sb[...] = jnp.zeros((16, D), BF)
    for l in range(2):
        n.sb[:, pl.ds(256 * l, 128)] = high[l]
        n.sb[:, pl.ds(256 * l + 128, 128)] = rest[l]
    last = [pltpu.make_async_copy(n.sb, n.out_o.at[pl.ds(OUT_SMALL, 16)], n.so.at[0])]
    last[0].start()
    hook(2, 2)
    for cp in g_out(0) + g_out(1):
        cp.start()
        last.append(cp)
    for cp in last + result_copies + grad_copies:
        cp.wait()


def finish_kernel(packed, res_o, gst_o, gain_o, shift_o, gq_o, qv_o, go_o, bo_o, gu_o, bu_o, gd_o, bd_o):
    res_o[...] = packed[:ROWS, :].astype(F32)
    gst_o[...] = packed[ROWS:2 * ROWS, :].astype(F32)
    for l in range(2):
        for b in range(24):
            lanes = slice(128 * (b // 3), 128 * (b // 3) + 128)
            start = OUT_GRADS + GPIECE * l + 128 * (b % 3)
            value = packed[start:start + 128, lanes].astype(F32)
            if b < 8:
                gd_o[l, 128 * b:128 * b + 128, :] = value
            elif b < 16:
                gu_o[l, :, 128 * (b - 8):128 * (b - 8) + 128] = value
            elif b < 18:
                go_o[l, 128 * (b - 16):128 * (b - 16) + 128, :] = value
            else:
                at = b - 18
                gq_o[l, at // 2, :, 128 * (at % 2):128 * (at % 2) + 128] = value
        small = packed[OUT_SMALL:OUT_SMALL + 16, 256 * l:256 * l + 128].astype(F32)
        small = small + packed[OUT_SMALL:OUT_SMALL + 16, 256 * l + 128:256 * l + 256].astype(F32)
        gain_o[l] = small[0:4]
        shift_o[l] = small[4:8]
        qv_o[l] = small[11:13, :32]
        bo_o[l:l + 1, :] = small[8:9]
        bd_o[l:l + 1, :] = small[9:10]
        bu_o[l:l + 1, :] = small[10:11]


def fused_shards(
    stream, text_len, norm_gain, norm_shift, w_qkv, bias_qv, w_out, bias_out, w_up, bias_up, w_down, bias_down, cotangent
):
    rows = (ROWS, D)
    any_space = pl.BlockSpec(memory_space=pl.ANY)
    vmem = pl.BlockSpec(memory_space=pltpu.VMEM)
    smem = pl.BlockSpec(memory_space=pltpu.SMEM)
    packed = pl.pallas_call(
        fused_kernel,
        out_shape=jax.ShapeDtypeStruct((OUT_ROWS, D), BF),
        in_specs=[smem, any_space, any_space, vmem, vmem, vmem, vmem, vmem, vmem] + [any_space] * 4,
        out_specs=any_space,
        scratch_shapes=[pltpu.VMEM(shape, dtype) for shape, dtype in VMEM_SCRATCH.values()]
        + [pltpu.SemaphoreType.DMA(shape) for shape in DMA_SEMS.values()],
        compiler_params=pltpu.CompilerParams(
            collective_id=0, has_side_effects=True, vmem_limit_bytes=63 * 2**20
        ),
    )(
        text_len,
        stream.reshape(rows),
        cotangent.reshape(rows),
        norm_gain,
        norm_shift,
        bias_qv,
        bias_out,
        bias_up,
        bias_down,
        w_qkv.transpose(0, 2, 1, 3),
        w_out,
        w_up,
        w_down,
    )
    shape = lambda *dims: jax.ShapeDtypeStruct(dims, F32)
    done = pl.pallas_call(
        finish_kernel,
        out_shape=(
            shape(*rows), shape(*rows), shape(2, 4, 128), shape(2, 4, 128), shape(2, 3, 128, COLS), shape(2, 2, 32),
            shape(2, COLS, 128), shape(2, 128), shape(2, 128, FFL), shape(2, 128), shape(2, FFL, 128), shape(2, 128),
        ),
        in_specs=[vmem],
        out_specs=[vmem] * 12,
        compiler_params=pltpu.CompilerParams(vmem_limit_bytes=32 * 2**20),
    )(packed)
    return (
        done[0].reshape(1, ROWS, D),
        done[1].reshape(1, ROWS, D),
        done[2],
        done[3],
        done[4].transpose(0, 2, 1, 3),
    ) + tuple(done[5:])


def solution(mesh):
    return jax.shard_map(
        fused_shards if fits(mesh) else shards,
        mesh=mesh,
        in_specs=(
            P("dp", "seq", None),
            P("dp"),
            P(),
            P(),
            P(None, None, None, "mp"),
            P(None, None, "mp"),
            P(None, "mp", None),
            P(),
            P(None, None, "mp"),
            P(None, "mp"),
            P(None, "mp", None),
            P(),
            P("dp", "seq", None),
        ),
        out_specs=(
            P("dp", "seq", None),
            P("dp", "seq", None),
            P(None, None, ("seq", "dp")),
            P(None, None, ("seq", "dp")),
            P(None, ("seq", "dp"), None, "mp"),
            P(None, None, ("mp", "seq", "dp")),
            P(None, "mp", ("seq", "dp")),
            P(None, ("seq", "dp")),
            P(None, ("seq", "dp"), "mp"),
            P(None, ("mp", "seq", "dp")),
            P(None, "mp", ("seq", "dp")),
            P(None, ("seq", "dp")),
        ),
        check_vma=False,
    )
```
